256 devices in a mesh: los: 8 (over z_hi, x), sky: 32 (over z_lo, y, core).
Axes of the slice: x: 4, y: 4, z: 8 (z_hi: 2, z_lo: 4; z = z_hi * 4 + z_lo), core: 2. Of those that a mesh axis runs over, the one named last changes fastest.
Arguments:
- density: bfloat16 [64, 2048, 2048], P('los', 'sky'), may hold values from 0.1 to 10
- refine: int32 [8, 256, 256], P('los', 'sky'), may hold values from 0 to 1, as said below
- weight_low: float32 [64], P('los'), may hold values from 0.1 to 0.5
- weight_high: float32 [64], P('los'), may hold values from 0.6 to 3
Outputs:
- deflection_x: float32 [2048, 2048], P('sky', 'los')
- deflection_y: float32 [2048, 2048], P('sky', 'los')
The draws below stay inside these ranges and needn't reach their ends.
Inputs may be any that keep to these rules, and one draw needn't show every extreme that they name: `refine`: the blocks of one slab and one sky column (one index of los and of sky) hold at most 512 refined blocks, and in every draw some slab and column holds exactly 512.
All inputs are finite; a program needn't handle non-finite values.
Results may differ from the reference program's by a relative error of at most 0.0003.
Values may be sent and summed in bfloat16 or wider, within the bound.
No kernel may reach another device: no remote copies, remote signals or barrier semaphores. Data moves between devices by JAX's collectives and lax.ppermute only.
A program may use at most 64 MiB of HBM per device.

```python
import math
import jax
import jax.numpy as jnp
from jax import lax

PLANE = 2048
DZ = 8
NZ = 64
CX = 64
REFINED = 512


def draw_refine(key, part):
    slab_count = NZ // DZ
    column_count = PLANE // CX
    per_device = DZ // 8 * (CX // 8) * (PLANE // 8)
    devices = slab_count * column_count
    keys = jax.random.split(jax.random.fold_in(key, 101), devices)
    ranks = jax.vmap(lambda single: jax.random.permutation(single, per_device))(keys)
    halvings = jax.random.randint(jax.random.fold_in(key, 102), (devices,), 0, 4)
    counts = jnp.right_shift(jnp.full((devices,), REFINED, jnp.int32), halvings)
    busiest = jax.random.randint(jax.random.fold_in(key, 103), (), 0, devices)
    counts = jnp.where(jnp.arange(devices) == busiest, REFINED, counts)
    flags = (ranks < counts[:, None]).astype(jnp.int32)
    flags = flags.reshape(slab_count, column_count, DZ // 8, CX // 8, PLANE // 8)
    return flags.transpose(0, 2, 1, 3, 4).reshape(NZ // 8, PLANE // 8, PLANE // 8)


def draw_density(key, part):
    rough_span = 1.4
    ramp_span = 0.7
    noise_span = 0.15
    step_low = 0.15
    step_high = 0.35
    rough = jax.random.uniform(jax.random.fold_in(key, 211), (PLANE, PLANE), jnp.float32, -rough_span, rough_span)
    increments = jax.random.uniform(jax.random.fold_in(key, 212), (NZ,), jnp.float32, step_low, step_high)
    offset = jax.random.uniform(jax.random.fold_in(key, 213), (), jnp.float32)
    phase = offset + jnp.cumsum(increments)
    ramp = ramp_span * (2.0 * (phase - jnp.floor(phase)) - 1.0)
    noise = jax.random.uniform(jax.random.fold_in(key, 214), (NZ, PLANE, PLANE), jnp.float32, -noise_span, noise_span)
    logs = rough[None, :, :] + ramp[:, None, None] + noise
    return jnp.exp(logs).astype(jnp.bfloat16)


def block_levels(key, dims, cuts, smallest, top_value):
    loudness, own = 1.0, jax.random.fold_in(key, 6)
    for dim, parts in cuts:
        draws = jnp.exp(jax.random.uniform(jax.random.fold_in(own, dim), (parts,), jnp.float32, smallest / len(cuts), top_value / len(cuts)))
        loudness = loudness * jnp.repeat(draws, dims[dim] // parts).reshape([-1 if axis == dim else 1 for axis in range(len(dims))])
    return loudness


def setup_inputs(seed: int = 0) -> dict:
    splits = jax.random.split(jax.random.key(seed), 5)
    density = draw_density(jax.random.fold_in(splits[4], 71), 0)
    refine = draw_refine(jax.random.fold_in(splits[4], 71), 0)
    weight_low = jnp.clip(jnp.exp(math.log(0.5) - 1.609438 * jax.random.uniform(splits[2], (NZ,), jnp.float32) ** block_levels(splits[2], (NZ,), ((0, 8),), -0.2, 0.2)), 0.1, 0.5)
    weight_high = jnp.clip(jnp.exp(math.log(3.0) - 1.60943787 * jax.random.uniform(splits[3], (NZ,), jnp.float32) ** block_levels(splits[3], (NZ,), ((0, 8),), -0.2, 0.2)), 0.6, 3.0)
    return dict(density=density, refine=refine, weight_low=weight_low, weight_high=weight_high)


def minmod(former, latter):
    return 0.5 * (jnp.sign(former) + jnp.sign(latter)) * jnp.minimum(jnp.abs(former), jnp.abs(latter))


def spread(field, dimension):
    return 0.75 * field + 0.125 * (jnp.roll(field, 1, dimension) + jnp.roll(field, -1, dimension))


def slanted(field, dimension):
    return (jnp.roll(field, 1, dimension) - jnp.roll(field, -1, dimension)) / 32.0


def reference(density, refine, weight_low, weight_high):
    layers = density.shape[0]
    plane = density.shape[1]

    def layer(totals, position):
        below = lax.dynamic_index_in_dim(density, jnp.maximum(position - 1, 0), 0, keepdims=False).astype(jnp.float32)
        centre = lax.dynamic_index_in_dim(density, position, 0, keepdims=False).astype(jnp.float32)
        above = lax.dynamic_index_in_dim(density, jnp.minimum(position + 1, layers - 1), 0, keepdims=False).astype(jnp.float32)
        grad_z = minmod(above - centre, centre - below)
        grad_x = minmod(jnp.roll(centre, -1, 0) - centre, centre - jnp.roll(centre, 1, 0))
        grad_y = minmod(jnp.roll(centre, -1, 1) - centre, centre - jnp.roll(centre, 1, 1))
        coarse = lax.dynamic_index_in_dim(refine, position // 8, 0, keepdims=False).astype(jnp.float32)
        marked = jnp.repeat(jnp.repeat(coarse, 8, 0), 8, 1)
        low = lax.dynamic_index_in_dim(weight_low, position, 0, keepdims=False)
        high = lax.dynamic_index_in_dim(weight_high, position, 0, keepdims=False)
        average = 0.5 * (low + high)
        weighted = average * centre
        base, refined_base, tilt_z, tilt_x, tilt_y = totals
        return (base + weighted,
                refined_base + marked * weighted,
                tilt_z + marked * (0.125 * (high - low)) * grad_z,
                tilt_x + marked * average * grad_x,
                tilt_y + marked * average * grad_y), None

    blank = jnp.zeros((plane, plane), jnp.float32)
    totals, leftover = lax.scan(layer, (blank, blank, blank, blank, blank), jnp.arange(layers, dtype=jnp.int32))
    base, refined_base, tilt_z, tilt_x, tilt_y = totals
    smoothed = spread(refined_base + tilt_z, 1) + slanted(tilt_y, 1)
    kappa = (base - refined_base + spread(smoothed, 0) + slanted(spread(tilt_x, 1), 0)) / jnp.float32(layers)
    spectrum = jnp.fft.fft2(kappa)
    wave = 2.0 * jnp.pi * jnp.fft.fftfreq(plane)
    wave_x = wave[:, None]
    wave_y = wave[None, :]
    squared = wave_x * wave_x + wave_y * wave_y
    at_anchor = squared == 0
    potential = jnp.where(at_anchor, 0.0, -2.0 / jnp.where(at_anchor, 1.0, squared)) * spectrum
    deflection_x = jnp.real(jnp.fft.ifft2(1j * wave_x * potential)).astype(jnp.float32)
    deflection_y = jnp.real(jnp.fft.ifft2(1j * wave_y * potential)).astype(jnp.float32)
    return (deflection_x, deflection_y)
```

```python
import functools

import jax
import jax.numpy as jnp
import ml_dtypes
import numpy as np
from jax import lax
from jax.experimental import pallas as pl
from jax.experimental.pallas import tpu as pltpu
from jax.sharding import Mesh, PartitionSpec as P

f32 = jnp.float32
bf16 = jnp.bfloat16
N = 2048
ROWS = 64
SKY = 32
LAYERS = 8
LOS = ("zhi", "x")
MB = 1024 * 1024


def halves(table):
    high = table.astype(np.float32).astype(ml_dtypes.bfloat16)
    low = (table - high.astype(np.float64)).astype(np.float32).astype(ml_dtypes.bfloat16)
    return high, low


def tile_modes(tile):
    n = np.arange(128)
    if tile:
        return tile + 16 * n
    return np.where(n < 64, 16 * n, 8 + 16 * (n - 64))


def tile_order(real, imag):
    pair = np.stack([real.reshape(SKY, 4, -1), imag.reshape(SKY, 4, -1)], axis=1)
    return pair.reshape(256, -1)


def forward_table():
    b = np.arange(128)
    tiles = []
    for tile in range(8):
        angle = (tile_modes(tile)[:, None] * b[None, :] % N) * (2 * np.pi / N)
        cosine, sine = np.cos(angle), np.sin(angle)
        if tile:
            real = np.concatenate([cosine, sine], 1)
            imag = np.concatenate([-sine, cosine], 1)
        else:
            zero = np.zeros((64, 128))
            real = np.block([[cosine[:64], zero], [zero, cosine[64:]]])
            imag = np.block([[-sine[:64], zero], [zero, -sine[64:]]])
            imag[0, :128] = (-1.0) ** b
        tiles.append(tile_order(real, imag).T)
    return np.stack(tiles)


def inverse_table():
    j = np.arange(256)
    tiles = []
    for tile in range(8):
        angle = (tile_modes(tile)[:, None] * j[None, :] % N) * (2 * np.pi / N)
        real, imag = 2 * np.cos(angle), -2 * np.sin(angle)
        if not tile:
            real[0] = 1.0
            imag[0] = (-1.0) ** j
        tiles.append(tile_order(real, imag))
    return np.stack(tiles).reshape(4, 512, 256)


def row_table():
    r = np.arange(64)
    angle = (r[:, None] * r[None, :] % 64) * (2 * np.pi / 64)
    both = np.eye(2)
    return np.concatenate([np.kron(both, np.cos(angle)), np.kron(both, np.sin(angle))], 1)


def twists():
    angle = (np.arange(32)[:, None] * (np.arange(128) % 64)[None, :]) * (2 * np.pi / N)
    sign = np.where(np.arange(8) < 4, 1.0, -1.0)
    cosine = np.broadcast_to(np.cos(angle)[:, None, :], (32, 8, 128))
    sine = np.sin(angle)[:, None, :] * sign[None, :, None]
    return cosine.astype(np.float32), sine.astype(np.float32)


def minmod(a, b):
    return jnp.maximum(jnp.minimum(a, b), 0.0) + jnp.minimum(jnp.maximum(a, b), 0.0)


def split(value):
    high = value.astype(bf16)
    return high, (value - high.astype(f32)).astype(bf16)


def dot3(value, high_table, low_table):
    high, low = split(value)
    dot = functools.partial(jnp.dot, preferred_element_type=f32)
    return dot(high, high_table) + (dot(low, high_table) + dot(high, low_table))


def limit(mib):
    return pltpu.CompilerParams(vmem_limit_bytes=mib * MB)


VM = pl.BlockSpec(memory_space=pltpu.VMEM)
SM = pl.BlockSpec(memory_space=pltpu.SMEM)


def rows_kernel(first_ref, last_ref, low_ref, high_ref):
    for z in range(LAYERS):
        low_ref[z : z + 1, :] = first_ref[z].astype(f32)[0:1]
        high_ref[z : z + 1, :] = last_ref[z].astype(f32)[15:16]


def edge_rows(density):
    shape = jax.ShapeDtypeStruct((LAYERS, N), f32)
    return pl.pallas_call(
        rows_kernel,
        grid=(1,),
        out_shape=(shape, shape),
        in_specs=[
            pl.BlockSpec((LAYERS, 16, N), lambda i: (0, 0, 0)),
            pl.BlockSpec((LAYERS, 16, N), lambda i: (0, 3, 0)),
        ],
        out_specs=(
            pl.BlockSpec((LAYERS, N), lambda i: (0, 0)),
            pl.BlockSpec((LAYERS, N), lambda i: (0, 0)),
        ),
        compiler_params=limit(24),
        name="edge_rows",
    )(density, density)


CHUNK = 512


def inner_kernel(
    low_ref, high_ref, d_ref, refine_ref, calm_ref, lifted_ref, tx_ref, ty_ref, mask_ref, near_ref
):
    block = lax.broadcasted_iota(jnp.int32, (256, N), 0)
    lane = lax.broadcasted_iota(jnp.int32, (256, N), 1)
    grow = jnp.where(lane // 8 == block, 1.0, 0.0).astype(bf16)
    coarse = refine_ref[0].astype(f32).astype(bf16)
    mask_ref[...] = jnp.dot(coarse, grow, preferred_element_type=f32)
    for z in range(LAYERS):
        first = d_ref[z, 0:16, :].astype(f32)
        last = d_ref[z, 48:64, :].astype(f32)
        near_ref[0, z : z + 1, :] = first[0:1]
        near_ref[1, z : z + 1, :] = first[1:2]
        near_ref[2, z : z + 1, :] = last[14:15]
        near_ref[3, z : z + 1, :] = last[15:16]

    wide = CHUNK + 256
    row = lax.broadcasted_iota(jnp.int32, (ROWS, CHUNK), 0)
    inside = jnp.logical_and(row > 0, row < ROWS - 1)

    def chunk(i, carry):
        start = pl.multiple_of(i * CHUNK, CHUNK)
        left = pl.multiple_of((start + N - 128) % N, 128)
        right = pl.multiple_of((start + CHUNK) % N, 128)
        base = jnp.zeros((ROWS, CHUNK), f32)
        tz, tx, ty = base, base, base
        centre, step = None, None
        for z in range(LAYERS):
            average = 0.5 * (low_ref[z] + high_ref[z])
            former = centre
            around = jnp.concatenate(
                [
                    d_ref[z, :, pl.ds(left, 128)],
                    d_ref[z, :, pl.ds(start, CHUNK)],
                    d_ref[z, :, pl.ds(right, 128)],
                ],
                axis=1,
            ).astype(f32)
            centre = around[:, 128 : 128 + CHUNK]
            base = base + average * centre
            dy = pltpu.roll(around, wide - 1, 1) - around
            gy = minmod(dy, pltpu.roll(dy, 1, 1))[:, 128 : 128 + CHUNK]
            ty = ty + average * gy
            dx = pltpu.roll(centre, ROWS - 1, 0) - centre
            tx = tx + average * minmod(dx, pltpu.roll(dx, 1, 0))
            if z > 0:
                latter = centre - former
                if step is not None:
                    slope = 0.125 * (high_ref[z - 1] - low_ref[z - 1])
                    tz = tz + slope * minmod(latter, step)
                step = latter
        marked = mask_ref[:, pl.ds(start, CHUNK)]
        marked = jnp.broadcast_to(marked[:, None, :], (8, 8, CHUNK)).reshape(ROWS, CHUNK)
        at = pl.ds(start, CHUNK)
        calm_ref[:, at] = base - marked * base
        lifted_ref[:, at] = marked * (base + tz)
        tx_ref[:, at] = jnp.where(inside, marked * tx, 0.0)
        ty_ref[:, at] = marked * ty
        return carry

    lax.fori_loop(0, N // CHUNK, chunk, 0)


def inner_sums(low, high, density, refine):
    field = jax.ShapeDtypeStruct((ROWS, N), f32)
    return pl.pallas_call(
        inner_kernel,
        out_shape=(
            field,
            field,
            field,
            field,
            jax.ShapeDtypeStruct((8, N), f32),
            jax.ShapeDtypeStruct((4, LAYERS, N), f32),
        ),
        in_specs=[SM, SM, VM, VM],
        out_specs=(VM,) * 6,
        compiler_params=limit(40),
        cost_estimate=pl.CostEstimate(flops=40_000_000, bytes_accessed=24 * MB, transcendentals=0),
        name="inner_sums",
    )(low, high, density, refine)


def outer_kernel(
    low_ref,
    high_ref,
    pos_ref,
    average_ref,
    bottom_ref,
    top_ref,
    below_ref,
    above_ref,
    before_ref,
    after_ref,
    calm_ref,
    lifted_ref,
    tx_ref,
    ty_ref,
    mask_ref,
    near_ref,
    high_table,
    low_table,
    out_ref,
):
    los = pos_ref[0] * 4 + pos_ref[1]
    v0, v1 = bottom_ref[0].astype(f32), bottom_ref[1].astype(f32)
    v6, v7 = top_ref[0].astype(f32), top_ref[1].astype(f32)
    below = jnp.where(los == 0, v0, below_ref[0].astype(f32))
    above = jnp.where(los == 7, v7, above_ref[0].astype(f32))
    slope0 = 0.125 * (high_ref[0] - low_ref[0])
    slope7 = 0.125 * (high_ref[7] - low_ref[7])
    tz = slope0 * minmod(v1 - v0, v0 - below) + slope7 * minmod(above - v7, v7 - v6)
    mask = mask_ref[...]
    marked = jnp.broadcast_to(mask[:, None, :], (8, 8, N)).reshape(ROWS, N)
    lifted = lifted_ref[...] + marked * tz
    average = average_ref[:, 0:1]
    r0, r1, r62, r63 = near_ref[0], near_ref[1], near_ref[2], near_ref[3]
    e0 = jnp.sum(average * minmod(r1 - r0, r0 - before_ref[...]), axis=0, keepdims=True)
    e63 = jnp.sum(average * minmod(after_ref[...] - r63, r63 - r62), axis=0, keepdims=True)
    row = lax.broadcasted_iota(jnp.int32, (ROWS, N), 0)
    tx = jnp.where(row == 0, mask[0:1] * e0, jnp.where(row == ROWS - 1, mask[7:8] * e63, tx_ref[...]))
    eighth, tilt = 0.125 * lifted, ty_ref[...] * (1.0 / 32.0)
    smooth = 0.75 * lifted + pltpu.roll(eighth + tilt, 1, 1) + pltpu.roll(eighth - tilt, N - 1, 1)
    sloped = 0.75 * tx + 0.125 * (pltpu.roll(tx, 1, 1) + pltpu.roll(tx, N - 1, 1))
    eighth, tilt = 0.125 * smooth, sloped * (1.0 / 32.0)
    none = jnp.zeros((8, N), f32)

    def longer(field):
        return jnp.concatenate([field, none], axis=0)

    kappa = (
        longer(calm_ref[...] + 0.75 * smooth)
        + pltpu.roll(longer(eighth + tilt), 1, 0)
        + pltpu.roll(longer(eighth - tilt), ROWS + 7, 0)
    )
    part = [kappa[:, 128 * a : 128 * a + 128] for a in range(16)]
    even = [part[a] + part[16 - a] for a in range(1, 8)]
    odd = [part[a] - part[16 - a] for a in range(1, 8)]

    def weigh(pairs):
        total = None
        for factor, value in pairs:
            if abs(factor) < 1e-9:
                continue
            term = value if abs(factor - 1) < 1e-9 else factor * value
            total = term if total is None else total + term
        return total

    def cosines(k):
        first = part[0] + part[8] if k % 2 == 0 else part[0] - part[8]
        return first + weigh((float(np.cos(np.pi * k * a / 8)), even[a - 1]) for a in range(1, 8))

    def sines(k):
        return weigh((float(-np.sin(np.pi * k * a / 8)), odd[a - 1]) for a in range(1, 8))

    for tile in range(8):
        second = sines(tile) if tile else cosines(8)
        value = jnp.concatenate([cosines(tile), second], axis=1)
        lanes = 256 * (tile % 2)
        out_ref[tile // 2, :, lanes : lanes + 256] = dot3(value, high_table[tile], low_table[tile])


def outer_sums(low, high, pos, average, density, below, above, before, after, inner, tables):
    whole = lambda *shape: pl.BlockSpec(shape, lambda i: (0,) * len(shape))
    return pl.pallas_call(
        outer_kernel,
        grid=(1,),
        out_shape=jax.ShapeDtypeStruct((4, 72, 512), f32),
        in_specs=[
            SM,
            SM,
            SM,
            whole(LAYERS, 128),
            pl.BlockSpec((2, ROWS, N), lambda i: (0, 0, 0)),
            pl.BlockSpec((2, ROWS, N), lambda i: (3, 0, 0)),
            whole(1, ROWS, N),
            whole(1, ROWS, N),
            whole(LAYERS, N),
            whole(LAYERS, N),
            whole(ROWS, N),
            whole(ROWS, N),
            whole(ROWS, N),
            whole(ROWS, N),
            whole(8, N),
            whole(4, LAYERS, N),
            whole(8, 256, 256),
            whole(8, 256, 256),
        ],
        out_specs=whole(4, 72, 512),
        compiler_params=limit(56),
        name="outer_sums",
    )(low, high, pos, average, density, density, below, above, before, after, *inner, *tables)


def turn_kernel(in_ref, out_ref):
    total = (in_ref[0] + in_ref[1]) + (in_ref[2] + in_ref[3])
    total = jnp.concatenate([total, jnp.zeros((56, 512), f32)], axis=0)
    out_ref[...] = total.T.reshape(64, 8, 128)


def turn(pieces):
    return pl.pallas_call(
        turn_kernel,
        out_shape=jax.ShapeDtypeStruct((64, 8, 128), f32),
        in_specs=[VM],
        out_specs=VM,
        compiler_params=limit(24),
        name="turn",
    )(pieces)


def dft_32(values):
    even = [values[s] + values[32 - s] for s in range(1, 16)]
    odd = [values[s] - values[32 - s] for s in range(1, 16)]
    ends = [values[0] + values[16], values[0] - values[16]]
    cosine, sine = [None] * 17, [None] * 17
    for k in range(9):
        plain = ends[k % 2]
        turned = None
        for s in range(1, 16):
            term = float(np.cos(np.pi * k * s / 16)) * even[s - 1]
            if s % 2 == 0:
                plain = plain + term
            else:
                turned = term if turned is None else turned + term
        cosine[k] = plain + turned
        cosine[16 - k] = plain - turned
    for k in range(1, 9):
        plain, turned = None, None
        for s in range(1, 16):
            term = float(np.sin(np.pi * k * s / 16)) * odd[s - 1]
            if s % 2 == 0:
                plain = term if plain is None else plain + term
            else:
                turned = term if turned is None else turned + term
        sine[k] = turned + plain
        sine[16 - k] = turned - plain
    return cosine, sine


def solve_kernel(pos_ref, in_ref, cos_ref, sin_ref, high_table, low_table, out_ref):
    zhi, column, sky = pos_ref[0], pos_ref[1], pos_ref[2]
    tile = 2 * column + zhi
    lane = lax.broadcasted_iota(jnp.int32, (8, 128), 1)
    sub = lax.broadcasted_iota(jnp.int32, (8, 128), 0)
    lower = lane < 64
    sign = jnp.where(sub < 4, 1.0, -1.0)
    first = jnp.logical_and(tile == 0, sky == 0)
    packed = jnp.logical_and(sub % 4 == 0, first)

    def swap(v):
        return pltpu.roll(v, 4, v.ndim - 2)

    def bent(v):
        return swap(v) * sign

    total = [in_ref[s] + in_ref[SKY + s] for s in range(SKY)]
    values = []
    for s in range(SKY):
        up = pltpu.roll(total[(s - 1) % SKY], 64, 1)
        down = pltpu.roll(total[(s + 1) % SKY], 120, 1)
        v = total[s] + jnp.where(lane == 0, up, jnp.where(lane == 63, down, 0.0))
        v = jnp.where(lower, v, pltpu.roll(v, 64, 1))
        apart = jnp.where(sub == 4, 0.0, jnp.where(lower, v, swap(v)))
        values.append(jnp.where(packed, apart, v))
    cosine, sine = dft_32(values)
    spectrum = [None] * 32
    spectrum[0], spectrum[16] = cosine[0], cosine[16]
    for k in range(1, 16):
        turned = bent(sine[k])
        spectrum[k], spectrum[32 - k] = cosine[k] + turned, cosine[k] - turned
    twisted = [spectrum[k] * cos_ref[k] + swap(spectrum[k]) * sin_ref[k] for k in range(32)]
    rows = jnp.concatenate(twisted, axis=0)
    pair = dot3(rows, high_table[...], low_table[...])
    pair_c = pair[:, :128].reshape(32, 8, 128)
    pair_s = pair[:, 128:].reshape(32, 8, 128)

    k1 = lax.broadcasted_iota(jnp.int32, (32, 8, 128), 0)
    k2 = lax.broadcasted_iota(jnp.int32, (32, 8, 128), 2) % 64
    nx = k1 + 32 * k2
    nx = jnp.where(nx < N // 2, nx, nx - N)
    n = 4 * sky + sub % 4
    ny = jnp.where(tile > 0, tile + 16 * n, jnp.where(n < 64, 16 * n, 8 + 16 * (n - 64)))
    ny = jnp.where(ny < N // 2, ny, ny - N)
    ny = jnp.where(jnp.logical_and(packed, jnp.logical_not(lower)), -(N // 2), ny)
    along_x = jnp.logical_or(packed, lower)[None]
    squared = nx * nx + (ny * ny)[None]
    wave = jnp.where(along_x, jnp.where(nx == -(N // 2), 0, nx), ny[None])
    unit = 2.0 * np.pi / N
    scale = float(-2.0 / unit / 64.0 / N / N)
    factor = scale * wave.astype(f32) / jnp.maximum(squared, 1).astype(f32)
    kappa_hat = pair_c + swap(pair_s) * sign[None]
    field = factor * (swap(kappa_hat) * (-sign)[None])
    pair = dot3(field.reshape(256, 128), high_table[...], low_table[...])
    values = []
    for k in range(32):
        v = pair[8 * k : 8 * k + 8, :128] - bent(pair[8 * k : 8 * k + 8, 128:])
        values.append(v * cos_ref[k] - swap(v) * sin_ref[k])
    cosine, sine = dft_32(values)
    for s in range(17):
        turned = bent(sine[s]) if 0 < s < 16 else None
        for at in (s,) if turned is None else (s, 32 - s):
            v = cosine[s]
            if turned is not None:
                v = v - turned if at == s else v + turned
            other = swap(pltpu.roll(v, 64, 1))
            joined = jnp.where(lower, jnp.where(sub == 4, other, v), 0.0)
            v = jnp.where(packed, joined, v)
            out_ref[at] = v
            out_ref[SKY + at] = v


def solve(pos, pieces, tables):
    return pl.pallas_call(
        solve_kernel,
        out_shape=jax.ShapeDtypeStruct((64, 8, 128), f32),
        in_specs=[SM] + [VM] * 5,
        out_specs=VM,
        compiler_params=limit(24),
        name="solve",
    )(pos, pieces, *tables)


def back_kernel(pos_ref, phase_ref, in_ref, high_table, low_table, out_ref):
    value = in_ref[...]
    sub = lax.broadcasted_iota(jnp.int32, (64, 8, 128), 1)
    bent = pltpu.roll(value, 4, 1) * jnp.where(sub < 4, -1.0, 1.0)
    plain = value.reshape(512, 128).T
    bent = bent.reshape(512, 128).T
    for target in range(4):
        parts = []
        for half in range(2):
            lanes = slice(256 * half, 256 * half + 256)
            at = 4 * target + 2 * half
            parts.append(phase_ref[at] * plain[:, lanes] + phase_ref[at + 1] * bent[:, lanes])
        out_ref[target] = dot3(jnp.concatenate(parts, axis=1), high_table[0], low_table[0])


def back(pos, phase, pieces, tables):
    table = pl.BlockSpec((1, 512, 256), lambda i, pos, phase: (pos[1], 0, 0))
    return pl.pallas_call(
        back_kernel,
        grid_spec=pltpu.PrefetchScalarGridSpec(
            num_scalar_prefetch=2,
            grid=(1,),
            in_specs=[pl.BlockSpec((64, 8, 128), lambda i, pos, phase: (0, 0, 0)), table, table],
            out_specs=pl.BlockSpec((4, 128, 256), lambda i, pos, phase: (0, 0, 0)),
        ),
        out_shape=jax.ShapeDtypeStruct((4, 128, 256), f32),
        compiler_params=limit(24),
        name="back",
    )(pos, phase, pieces, *tables)


def final_kernel(in_ref, x_ref, y_ref):
    total = (in_ref[0] + in_ref[1]) + (in_ref[2] + in_ref[3])
    x_ref[...] = total[:ROWS]
    y_ref[...] = total[ROWS:]


def final(pieces):
    shape = jax.ShapeDtypeStruct((ROWS, 256), f32)
    return pl.pallas_call(
        final_kernel,
        out_shape=(shape, shape),
        in_specs=[VM],
        out_specs=(VM, VM),
        compiler_params=limit(24),
        name="final",
    )(pieces)


def body(density, refine, weight_low, weight_high):
    zhi, column, sky = lax.axis_index("zhi"), lax.axis_index("x"), lax.axis_index("sky")
    pos = jnp.stack([zhi, column, sky]).astype(jnp.int32)
    above = lax.ppermute(density[:1], LOS, [(i + 1, i) for i in range(7)])
    below = lax.ppermute(density[-1:], LOS, [(i, i + 1) for i in range(7)])
    row_first, row_last = edge_rows(density)
    before = lax.ppermute(row_last, "sky", [(i, (i + 1) % SKY) for i in range(SKY)])
    after = lax.ppermute(row_first, "sky", [((i + 1) % SKY, i) for i in range(SKY)])
    inner = inner_sums(weight_low, weight_high, density, refine)
    average = jnp.broadcast_to((0.5 * (weight_low + weight_high))[:, None], (LAYERS, 128))
    summed = outer_sums(
        weight_low,
        weight_high,
        pos,
        average,
        density,
        below,
        above,
        before,
        after,
        inner,
        halves(forward_table()),
    )
    summed = lax.all_to_all(summed, "x", 0, 0, tiled=True)
    pieces = lax.all_to_all(turn(summed), ("zhi", "sky"), 0, 0, tiled=True)
    cosine, sine = twists()
    high, low = halves(row_table())
    pieces = solve(pos, pieces, (cosine, sine, high, low))
    pieces = lax.all_to_all(pieces, ("zhi", "sky"), 0, 0, tiled=True)
    eighths = (2 * column + jnp.arange(2))[None, :] * (4 * zhi + jnp.arange(4))[:, None] % 8
    angle = eighths.astype(f32) * (2 * np.pi / 8)
    phase = jnp.stack([jnp.cos(angle), jnp.sin(angle)], axis=-1).reshape(16)
    fields = back(pos, phase, pieces, halves(inverse_table()))
    fields = lax.all_to_all(fields, "x", 0, 0, tiled=True)
    return final(fields)


def solution(mesh):
    devices = mesh.devices.reshape(2, 4, SKY)
    inner = Mesh(devices, ("zhi", "x", "sky"))
    placed = (P(LOS, "sky", None), P(LOS, "sky", None), P(LOS), P(LOS))
    return jax.shard_map(
        body,
        mesh=inner,
        in_specs=placed,
        out_specs=(P("sky", LOS), P("sky", LOS)),
        check_vma=False,
    )
```

```python
import functools

import jax
import jax.numpy as jnp
import ml_dtypes
import numpy as np
from jax import lax
from jax.experimental import pallas as pl
from jax.experimental.pallas import tpu as pltpu
from jax.sharding import Mesh, PartitionSpec as P

f32 = jnp.float32
bf16 = jnp.bfloat16
N = 2048
ROWS = 64
SKY = 32
LAYERS = 8
LOS = ("zhi", "x")
MB = 1024 * 1024


def halves(table):
    high = table.astype(np.float32).astype(ml_dtypes.bfloat16)
    low = (table - high.astype(np.float64)).astype(np.float32).astype(ml_dtypes.bfloat16)
    return high, low


def tile_modes(tile):
    n = np.arange(128)
    if tile:
        return tile + 16 * n
    return np.where(n < 64, 16 * n, 8 + 16 * (n - 64))


def tile_order(real, imag):
    pair = np.stack([real.reshape(SKY, 4, -1), imag.reshape(SKY, 4, -1)], axis=1)
    return pair.reshape(256, -1)


def forward_table():
    b = np.arange(128)
    tiles = []
    for tile in range(8):
        angle = (tile_modes(tile)[:, None] * b[None, :] % N) * (2 * np.pi / N)
        cosine, sine = np.cos(angle), np.sin(angle)
        if tile:
            real = np.concatenate([cosine, sine], 1)
            imag = np.concatenate([-sine, cosine], 1)
        else:
            zero = np.zeros((64, 128))
            real = np.block([[cosine[:64], zero], [zero, cosine[64:]]])
            imag = np.block([[-sine[:64], zero], [zero, -sine[64:]]])
            imag[0, :128] = (-1.0) ** b
        tiles.append(tile_order(real, imag).T)
    return np.stack(tiles)


def inverse_table():
    j = np.arange(256)
    tiles = []
    for tile in range(8):
        angle = (tile_modes(tile)[:, None] * j[None, :] % N) * (2 * np.pi / N)
        real, imag = 2 * np.cos(angle), -2 * np.sin(angle)
        if not tile:
            real[0] = 1.0
            imag[0] = (-1.0) ** j
        tiles.append(tile_order(real, imag))
    return np.stack(tiles).reshape(4, 512, 256)


def row_table():
    r = np.arange(64)
    angle = (r[:, None] * r[None, :] % 64) * (2 * np.pi / 64)
    both = np.eye(2)
    return np.concatenate([np.kron(both, np.cos(angle)), np.kron(both, np.sin(angle))], 1)


def twists():
    angle = (np.arange(32)[:, None] * (np.arange(128) % 64)[None, :]) * (2 * np.pi / N)
    sign = np.where(np.arange(8) < 4, 1.0, -1.0)
    cosine = np.broadcast_to(np.cos(angle)[:, None, :], (32, 8, 128))
    sine = np.sin(angle)[:, None, :] * sign[None, :, None]
    return cosine.astype(np.float32), sine.astype(np.float32)


def minmod(a, b):
    return jnp.maximum(jnp.minimum(a, b), 0.0) + jnp.minimum(jnp.maximum(a, b), 0.0)


def split(value):
    high = value.astype(bf16)
    return high, (value - high.astype(f32)).astype(bf16)


def dot3(value, high_table, low_table):
    high, low = split(value)
    dot = functools.partial(jnp.dot, preferred_element_type=f32)
    return dot(high, high_table) + (dot(low, high_table) + dot(high, low_table))


def limit(mib):
    return pltpu.CompilerParams(vmem_limit_bytes=mib * MB)


VM = pl.BlockSpec(memory_space=pltpu.VMEM)
SM = pl.BlockSpec(memory_space=pltpu.SMEM)


def rows_kernel(d_ref, low_ref, high_ref):
    for z in range(LAYERS):
        low_ref[z : z + 1, :] = d_ref[z, 0:16, :].astype(f32)[0:1]
        high_ref[z : z + 1, :] = d_ref[z, 48:64, :].astype(f32)[15:16]


def edge_rows(density):
    shape = jax.ShapeDtypeStruct((LAYERS, N), f32)
    return pl.pallas_call(
        rows_kernel,
        out_shape=(shape, shape),
        in_specs=[VM],
        out_specs=(VM, VM),
        compiler_params=limit(8),
        name="edge_rows",
    )(density)


CHUNK = 512


def inner_kernel(
    low_ref, high_ref, d_ref, refine_ref, calm_ref, lifted_ref, tx_ref, ty_ref, mask_ref, near_ref
):
    block = lax.broadcasted_iota(jnp.int32, (256, N), 0)
    lane = lax.broadcasted_iota(jnp.int32, (256, N), 1)
    grow = jnp.where(lane // 8 == block, 1.0, 0.0).astype(bf16)
    coarse = refine_ref[0].astype(f32).astype(bf16)
    mask_ref[...] = jnp.dot(coarse, grow, preferred_element_type=f32)
    for z in range(LAYERS):
        first = d_ref[z, 0:16, :].astype(f32)
        last = d_ref[z, 48:64, :].astype(f32)
        near_ref[0, z : z + 1, :] = first[0:1]
        near_ref[1, z : z + 1, :] = first[1:2]
        near_ref[2, z : z + 1, :] = last[14:15]
        near_ref[3, z : z + 1, :] = last[15:16]

    wide = CHUNK + 256
    row = lax.broadcasted_iota(jnp.int32, (ROWS, CHUNK), 0)
    inside = jnp.logical_and(row > 0, row < ROWS - 1)

    def chunk(i, carry):
        start = pl.multiple_of(i * CHUNK, CHUNK)
        left = pl.multiple_of((start + N - 128) % N, 128)
        right = pl.multiple_of((start + CHUNK) % N, 128)
        base = jnp.zeros((ROWS, CHUNK), f32)
        tz, tx, ty = base, base, base
        centre, step = None, None
        for z in range(LAYERS):
            average = 0.5 * (low_ref[z] + high_ref[z])
            former = centre
            around = jnp.concatenate(
                [
                    d_ref[z, :, pl.ds(left, 128)],
                    d_ref[z, :, pl.ds(start, CHUNK)],
                    d_ref[z, :, pl.ds(right, 128)],
                ],
                axis=1,
            ).astype(f32)
            centre = around[:, 128 : 128 + CHUNK]
            base = base + average * centre
            dy = pltpu.roll(around, wide - 1, 1) - around
            gy = minmod(dy, pltpu.roll(dy, 1, 1))[:, 128 : 128 + CHUNK]
            ty = ty + average * gy
            dx = pltpu.roll(centre, ROWS - 1, 0) - centre
            tx = tx + average * minmod(dx, pltpu.roll(dx, 1, 0))
            if z > 0:
                latter = centre - former
                if step is not None:
                    slope = 0.125 * (high_ref[z - 1] - low_ref[z - 1])
                    tz = tz + slope * minmod(latter, step)
                step = latter
        marked = mask_ref[:, pl.ds(start, CHUNK)]
        marked = jnp.broadcast_to(marked[:, None, :], (8, 8, CHUNK)).reshape(ROWS, CHUNK)
        at = pl.ds(start, CHUNK)
        calm_ref[:, at] = base - marked * base
        lifted_ref[:, at] = marked * (base + tz)
        tx_ref[:, at] = jnp.where(inside, marked * tx, 0.0)
        ty_ref[:, at] = marked * ty
        return carry

    lax.fori_loop(0, N // CHUNK, chunk, 0)


def inner_sums(low, high, density, refine):
    field = jax.ShapeDtypeStruct((ROWS, N), f32)
    return pl.pallas_call(
        inner_kernel,
        out_shape=(
            field,
            field,
            field,
            field,
            jax.ShapeDtypeStruct((8, N), f32),
            jax.ShapeDtypeStruct((4, LAYERS, N), f32),
        ),
        in_specs=[SM, SM, VM, VM],
        out_specs=(VM,) * 6,
        compiler_params=limit(40),
        cost_estimate=pl.CostEstimate(flops=40_000_000, bytes_accessed=24 * MB, transcendentals=0),
        name="inner_sums",
    )(low, high, density, refine)


def outer_kernel(
    low_ref,
    high_ref,
    d_ref,
    below_ref,
    above_ref,
    before_ref,
    after_ref,
    calm_ref,
    lifted_ref,
    tx_ref,
    ty_ref,
    mask_ref,
    near_ref,
    high_table,
    low_table,
    out_ref,
):
    los = lax.axis_index("zhi") * 4 + lax.axis_index("x")
    v0, v1 = d_ref[0].astype(f32), d_ref[1].astype(f32)
    v6, v7 = d_ref[6].astype(f32), d_ref[7].astype(f32)
    below = jnp.where(los == 0, v0, below_ref[0].astype(f32))
    above = jnp.where(los == 7, v7, above_ref[0].astype(f32))
    slope0 = 0.125 * (high_ref[0] - low_ref[0])
    slope7 = 0.125 * (high_ref[7] - low_ref[7])
    tz = slope0 * minmod(v1 - v0, v0 - below) + slope7 * minmod(above - v7, v7 - v6)
    mask = mask_ref[...]
    marked = jnp.broadcast_to(mask[:, None, :], (8, 8, N)).reshape(ROWS, N)
    lifted = lifted_ref[...] + marked * tz
    layer = lax.broadcasted_iota(jnp.int32, (LAYERS, 1), 0)
    average = jnp.zeros((LAYERS, 1), f32)
    for z in range(LAYERS):
        average = jnp.where(layer == z, 0.5 * (low_ref[z] + high_ref[z]), average)
    r0, r1, r62, r63 = near_ref[0], near_ref[1], near_ref[2], near_ref[3]
    e0 = jnp.sum(average * minmod(r1 - r0, r0 - before_ref[...]), axis=0, keepdims=True)
    e63 = jnp.sum(average * minmod(after_ref[...] - r63, r63 - r62), axis=0, keepdims=True)
    row = lax.broadcasted_iota(jnp.int32, (ROWS, N), 0)
    tx = jnp.where(row == 0, mask[0:1] * e0, jnp.where(row == ROWS - 1, mask[7:8] * e63, tx_ref[...]))
    eighth, tilt = 0.125 * lifted, ty_ref[...] * (1.0 / 32.0)
    smooth = 0.75 * lifted + pltpu.roll(eighth + tilt, 1, 1) + pltpu.roll(eighth - tilt, N - 1, 1)
    sloped = 0.75 * tx + 0.125 * (pltpu.roll(tx, 1, 1) + pltpu.roll(tx, N - 1, 1))
    eighth, tilt = 0.125 * smooth, sloped * (1.0 / 32.0)
    none = jnp.zeros((8, N), f32)

    def longer(field):
        return jnp.concatenate([field, none], axis=0)

    kappa = (
        longer(calm_ref[...] + 0.75 * smooth)
        + pltpu.roll(longer(eighth + tilt), 1, 0)
        + pltpu.roll(longer(eighth - tilt), ROWS + 7, 0)
    )
    part = [kappa[:, 128 * a : 128 * a + 128] for a in range(16)]
    even = [part[a] + part[16 - a] for a in range(1, 8)]
    odd = [part[a] - part[16 - a] for a in range(1, 8)]

    def weigh(pairs):
        total = None
        for factor, value in pairs:
            if abs(factor) < 1e-9:
                continue
            term = value if abs(factor - 1) < 1e-9 else factor * value
            total = term if total is None else total + term
        return total

    def cosines(k):
        first = part[0] + part[8] if k % 2 == 0 else part[0] - part[8]
        return first + weigh((float(np.cos(np.pi * k * a / 8)), even[a - 1]) for a in range(1, 8))

    def sines(k):
        return weigh((float(-np.sin(np.pi * k * a / 8)), odd[a - 1]) for a in range(1, 8))

    for tile in range(8):
        second = sines(tile) if tile else cosines(8)
        value = jnp.concatenate([cosines(tile), second], axis=1)
        lanes = 256 * (tile % 2)
        out_ref[tile // 2, :, lanes : lanes + 256] = dot3(value, high_table[tile], low_table[tile])


def outer_sums(low, high, density, below, above, before, after, inner, tables):
    return pl.pallas_call(
        outer_kernel,
        out_shape=jax.ShapeDtypeStruct((4, 72, 512), f32),
        in_specs=[SM, SM] + [VM] * 13,
        out_specs=VM,
        compiler_params=limit(32),
        name="outer_sums",
    )(low, high, density, below, above, before, after, *inner, *tables)


def turn_kernel(in_ref, out_ref):
    total = (in_ref[0] + in_ref[1]) + (in_ref[2] + in_ref[3])
    total = jnp.concatenate([total, jnp.zeros((56, 512), f32)], axis=0)
    out_ref[...] = total.T.reshape(64, 8, 128)


def turn(pieces):
    return pl.pallas_call(
        turn_kernel,
        out_shape=jax.ShapeDtypeStruct((64, 8, 128), f32),
        in_specs=[VM],
        out_specs=VM,
        compiler_params=limit(24),
        name="turn",
    )(pieces)


def dft_32(values):
    even = [values[s] + values[32 - s] for s in range(1, 16)]
    odd = [values[s] - values[32 - s] for s in range(1, 16)]
    ends = [values[0] + values[16], values[0] - values[16]]
    cosine, sine = [None] * 17, [None] * 17
    for k in range(9):
        plain = ends[k % 2]
        turned = None
        for s in range(1, 16):
            term = float(np.cos(np.pi * k * s / 16)) * even[s - 1]
            if s % 2 == 0:
                plain = plain + term
            else:
                turned = term if turned is None else turned + term
        cosine[k] = plain + turned
        cosine[16 - k] = plain - turned
    for k in range(1, 9):
        plain, turned = None, None
        for s in range(1, 16):
            term = float(np.sin(np.pi * k * s / 16)) * odd[s - 1]
            if s % 2 == 0:
                plain = term if plain is None else plain + term
            else:
                turned = term if turned is None else turned + term
        sine[k] = turned + plain
        sine[16 - k] = turned - plain
    return cosine, sine


def solve_kernel(in_ref, cos_ref, sin_ref, high_table, low_table, out_ref):
    sky = lax.axis_index("sky")
    tile = 2 * lax.axis_index("x") + lax.axis_index("zhi")
    lane = lax.broadcasted_iota(jnp.int32, (8, 128), 1)
    sub = lax.broadcasted_iota(jnp.int32, (8, 128), 0)
    lower = lane < 64
    sign = jnp.where(sub < 4, 1.0, -1.0)
    first = jnp.logical_and(tile == 0, sky == 0)
    packed = jnp.logical_and(sub % 4 == 0, first)

    def swap(v):
        return pltpu.roll(v, 4, v.ndim - 2)

    def bent(v):
        return swap(v) * sign

    total = [in_ref[s] + in_ref[SKY + s] for s in range(SKY)]
    values = []
    for s in range(SKY):
        up = pltpu.roll(total[(s - 1) % SKY], 64, 1)
        down = pltpu.roll(total[(s + 1) % SKY], 120, 1)
        v = total[s] + jnp.where(lane == 0, up, jnp.where(lane == 63, down, 0.0))
        v = jnp.where(lower, v, pltpu.roll(v, 64, 1))
        apart = jnp.where(sub == 4, 0.0, jnp.where(lower, v, swap(v)))
        values.append(jnp.where(packed, apart, v))
    cosine, sine = dft_32(values)
    spectrum = [None] * 32
    spectrum[0], spectrum[16] = cosine[0], cosine[16]
    for k in range(1, 16):
        turned = bent(sine[k])
        spectrum[k], spectrum[32 - k] = cosine[k] + turned, cosine[k] - turned
    twisted = [spectrum[k] * cos_ref[k] + swap(spectrum[k]) * sin_ref[k] for k in range(32)]
    rows = jnp.concatenate(twisted, axis=0)
    pair = dot3(rows, high_table[...], low_table[...])
    pair_c = pair[:, :128].reshape(32, 8, 128)
    pair_s = pair[:, 128:].reshape(32, 8, 128)

    k1 = lax.broadcasted_iota(jnp.int32, (32, 8, 128), 0)
    k2 = lax.broadcasted_iota(jnp.int32, (32, 8, 128), 2) % 64
    nx = k1 + 32 * k2
    nx = jnp.where(nx < N // 2, nx, nx - N)
    n = 4 * sky + sub % 4
    ny = jnp.where(tile > 0, tile + 16 * n, jnp.where(n < 64, 16 * n, 8 + 16 * (n - 64)))
    ny = jnp.where(ny < N // 2, ny, ny - N)
    ny = jnp.where(jnp.logical_and(packed, jnp.logical_not(lower)), -(N // 2), ny)
    along_x = jnp.logical_or(packed, lower)[None]
    squared = nx * nx + (ny * ny)[None]
    wave = jnp.where(along_x, jnp.where(nx == -(N // 2), 0, nx), ny[None])
    unit = 2.0 * np.pi / N
    scale = float(-2.0 / unit / 64.0 / N / N)
    factor = scale * wave.astype(f32) / jnp.maximum(squared, 1).astype(f32)
    kappa_hat = pair_c + swap(pair_s) * sign[None]
    field = factor * (swap(kappa_hat) * (-sign)[None])
    pair = dot3(field.reshape(256, 128), high_table[...], low_table[...])
    values = []
    for k in range(32):
        v = pair[8 * k : 8 * k + 8, :128] - bent(pair[8 * k : 8 * k + 8, 128:])
        values.append(v * cos_ref[k] - swap(v) * sin_ref[k])
    cosine, sine = dft_32(values)
    for s in range(17):
        turned = bent(sine[s]) if 0 < s < 16 else None
        for at in (s,) if turned is None else (s, 32 - s):
            v = cosine[s]
            if turned is not None:
                v = v - turned if at == s else v + turned
            other = swap(pltpu.roll(v, 64, 1))
            joined = jnp.where(lower, jnp.where(sub == 4, other, v), 0.0)
            v = jnp.where(packed, joined, v)
            out_ref[at] = v
            out_ref[SKY + at] = v


def solve(pieces, tables):
    return pl.pallas_call(
        solve_kernel,
        out_shape=jax.ShapeDtypeStruct((64, 8, 128), f32),
        in_specs=[VM] * 5,
        out_specs=VM,
        compiler_params=limit(24),
        name="solve",
    )(pieces, *tables)


def back_kernel(eighth_ref, in_ref, high_table, low_table, out_ref):
    zhi, column = lax.axis_index("zhi"), lax.axis_index("x")
    value = in_ref[...]
    sub = lax.broadcasted_iota(jnp.int32, (64, 8, 128), 1)
    bent = pltpu.roll(value, 4, 1) * jnp.where(sub < 4, -1.0, 1.0)
    plain = value.reshape(512, 128).T
    bent = bent.reshape(512, 128).T
    for target in range(4):
        parts = []
        for half in range(2):
            lanes = slice(256 * half, 256 * half + 256)
            turns = (2 * column + half) * (4 * zhi + target) % 8
            cosine, sine = eighth_ref[turns], eighth_ref[8 + turns]
            parts.append(cosine * plain[:, lanes] + sine * bent[:, lanes])
        value = jnp.concatenate(parts, axis=1)
        out_ref[target] = dot3(value, high_table[column], low_table[column])


def back(pieces, tables):
    turns = np.arange(8) * (2 * np.pi / 8)
    eighth = np.concatenate([np.cos(turns), np.sin(turns)]).astype(np.float32)
    return pl.pallas_call(
        back_kernel,
        out_shape=jax.ShapeDtypeStruct((4, 128, 256), f32),
        in_specs=[SM, VM, VM, VM],
        out_specs=VM,
        compiler_params=limit(24),
        name="back",
    )(eighth, pieces, *tables)


def final_kernel(in_ref, x_ref, y_ref):
    total = (in_ref[0] + in_ref[1]) + (in_ref[2] + in_ref[3])
    x_ref[...] = total[:ROWS]
    y_ref[...] = total[ROWS:]


def final(pieces):
    shape = jax.ShapeDtypeStruct((ROWS, 256), f32)
    return pl.pallas_call(
        final_kernel,
        out_shape=(shape, shape),
        in_specs=[VM],
        out_specs=(VM, VM),
        compiler_params=limit(24),
        name="final",
    )(pieces)


def body(density, refine, weight_low, weight_high):
    above = lax.ppermute(density[:1], LOS, [(i + 1, i) for i in range(7)])
    below = lax.ppermute(density[-1:], LOS, [(i, i + 1) for i in range(7)])
    row_first, row_last = edge_rows(density)
    before = lax.ppermute(row_last, "sky", [(i, (i + 1) % SKY) for i in range(SKY)])
    after = lax.ppermute(row_first, "sky", [((i + 1) % SKY, i) for i in range(SKY)])
    inner = inner_sums(weight_low, weight_high, density, refine)
    tables = halves(forward_table())
    summed = outer_sums(
        weight_low, weight_high, density, below, above, before, after, inner, tables
    )
    summed = lax.all_to_all(summed, "x", 0, 0, tiled=True)
    pieces = lax.all_to_all(turn(summed), ("zhi", "sky"), 0, 0, tiled=True)
    pieces = solve(pieces, twists() + halves(row_table()))
    pieces = lax.all_to_all(pieces, ("zhi", "sky"), 0, 0, tiled=True)
    fields = back(pieces, halves(inverse_table()))
    fields = lax.all_to_all(fields, "x", 0, 0, tiled=True)
    return final(fields)


def solution(mesh):
    devices = mesh.devices.reshape(2, 4, SKY)
    inner = Mesh(devices, ("zhi", "x", "sky"))
    placed = (P(LOS, "sky", None), P(LOS, "sky", None), P(LOS), P(LOS))
    return jax.shard_map(
        body,
        mesh=inner,
        in_specs=placed,
        out_specs=(P("sky", LOS), P("sky", LOS)),
        check_vma=False,
    )
```

```python
import functools

import jax
import jax.numpy as jnp
import ml_dtypes
import numpy as np
from jax import lax
from jax.experimental import pallas as pl
from jax.experimental.pallas import tpu as pltpu
from jax.sharding import Mesh, PartitionSpec as P

f32 = jnp.float32
bf16 = jnp.bfloat16
N = 2048
ROWS = 64
SKY = 32
LAYERS = 8
LOS = ("zhi", "x")
MB = 1024 * 1024


def halves(table):
    high = table.astype(np.float32).astype(ml_dtypes.bfloat16)
    low = (table - high.astype(np.float64)).astype(np.float32).astype(ml_dtypes.bfloat16)
    return high, low


def tile_modes(tile):
    n = np.arange(128)
    if tile:
        return tile + 16 * n
    return np.where(n < 64, 16 * n, 8 + 16 * (n - 64))


def tile_order(real, imag):
    pair = np.stack([real.reshape(SKY, 4, -1), imag.reshape(SKY, 4, -1)], axis=1)
    return pair.reshape(256, -1)


def forward_table():
    b = np.arange(128)
    tiles = []
    for tile in range(8):
        angle = (tile_modes(tile)[:, None] * b[None, :] % N) * (2 * np.pi / N)
        cosine, sine = np.cos(angle), np.sin(angle)
        if tile:
            real = np.concatenate([cosine, sine], 1)
            imag = np.concatenate([-sine, cosine], 1)
        else:
            zero = np.zeros((64, 128))
            real = np.block([[cosine[:64], zero], [zero, cosine[64:]]])
            imag = np.block([[-sine[:64], zero], [zero, -sine[64:]]])
            imag[0, :128] = (-1.0) ** b
        tiles.append(tile_order(real, imag).T)
    return np.stack(tiles)


def inverse_table():
    j = np.arange(256)
    tiles = []
    for tile in range(8):
        angle = (tile_modes(tile)[:, None] * j[None, :] % N) * (2 * np.pi / N)
        real, imag = 2 * np.cos(angle), -2 * np.sin(angle)
        if not tile:
            real[0] = 1.0
            imag[0] = (-1.0) ** j
        tiles.append(tile_order(real, imag))
    return np.stack(tiles).reshape(4, 512, 256)


def row_table():
    r = np.arange(64)
    angle = (r[:, None] * r[None, :] % 64) * (2 * np.pi / 64)
    both = np.eye(2)
    return np.concatenate([np.kron(both, np.cos(angle)), np.kron(both, np.sin(angle))], 1)


def twists():
    angle = (np.arange(32)[:, None] * (np.arange(128) % 64)[None, :]) * (2 * np.pi / N)
    sign = np.where(np.arange(8) < 4, 1.0, -1.0)
    cosine = np.broadcast_to(np.cos(angle)[:, None, :], (32, 8, 128))
    sine = np.sin(angle)[:, None, :] * sign[None, :, None]
    return cosine.astype(np.float32), sine.astype(np.float32)


def minmod(a, b):
    return jnp.maximum(jnp.minimum(a, b), 0.0) + jnp.minimum(jnp.maximum(a, b), 0.0)


def split(value):
    high = value.astype(bf16)
    return high, (value - high.astype(f32)).astype(bf16)


def dot3(value, high_table, low_table):
    high, low = split(value)
    dot = functools.partial(jnp.dot, preferred_element_type=f32)
    return dot(high, high_table) + (dot(low, high_table) + dot(high, low_table))


def limit(mib):
    return pltpu.CompilerParams(vmem_limit_bytes=mib * MB)


VM = pl.BlockSpec(memory_space=pltpu.VMEM)
SM = pl.BlockSpec(memory_space=pltpu.SMEM)


def rows_kernel(d_ref, near_ref, far_ref, layer_ref):
    layer_ref[0] = jnp.where(lax.axis_index("x") % 2 == 1, d_ref[0], d_ref[LAYERS - 1])
    even = lax.axis_index("sky") % 2 == 0
    for z in range(LAYERS):
        first = d_ref[z, 0:16, :].astype(f32)[0:1]
        last = d_ref[z, 48:64, :].astype(f32)[15:16]
        near_ref[z : z + 1, :] = jnp.where(even, last, first)
        far_ref[z : z + 1, :] = jnp.where(even, first, last)


def edge_rows(density):
    shape = jax.ShapeDtypeStruct((LAYERS, N), f32)
    return pl.pallas_call(
        rows_kernel,
        out_shape=(shape, shape, jax.ShapeDtypeStruct((1, ROWS, N), bf16)),
        in_specs=[VM],
        out_specs=(VM, VM, VM),
        compiler_params=limit(8),
        name="edge_rows",
    )(density)


CHUNK = 512


def inner_kernel(
    low_ref, high_ref, d_ref, refine_ref, calm_ref, lifted_ref, tx_ref, ty_ref, mask_ref, near_ref
):
    block = lax.broadcasted_iota(jnp.int32, (256, N), 0)
    lane = lax.broadcasted_iota(jnp.int32, (256, N), 1)
    grow = jnp.where(lane // 8 == block, 1.0, 0.0).astype(bf16)
    coarse = refine_ref[0].astype(f32).astype(bf16)
    mask_ref[...] = jnp.dot(coarse, grow, preferred_element_type=f32)
    for z in range(LAYERS):
        first = d_ref[z, 0:16, :].astype(f32)
        last = d_ref[z, 48:64, :].astype(f32)
        near_ref[0, z : z + 1, :] = first[0:1]
        near_ref[1, z : z + 1, :] = first[1:2]
        near_ref[2, z : z + 1, :] = last[14:15]
        near_ref[3, z : z + 1, :] = last[15:16]

    wide = CHUNK + 256
    row = lax.broadcasted_iota(jnp.int32, (ROWS, CHUNK), 0)
    inside = jnp.logical_and(row > 0, row < ROWS - 1)

    def chunk(i, carry):
        start = pl.multiple_of(i * CHUNK, CHUNK)
        left = pl.multiple_of((start + N - 128) % N, 128)
        right = pl.multiple_of((start + CHUNK) % N, 128)
        base = jnp.zeros((ROWS, CHUNK), f32)
        tz, tx, ty = base, base, base
        centre, step = None, None
        for z in range(LAYERS):
            average = 0.5 * (low_ref[z] + high_ref[z])
            former = centre
            around = jnp.concatenate(
                [
                    d_ref[z, :, pl.ds(left, 128)],
                    d_ref[z, :, pl.ds(start, CHUNK)],
                    d_ref[z, :, pl.ds(right, 128)],
                ],
                axis=1,
            ).astype(f32)
            centre = around[:, 128 : 128 + CHUNK]
            base = base + average * centre
            dy = pltpu.roll(around, wide - 1, 1) - around
            gy = minmod(dy, pltpu.roll(dy, 1, 1))[:, 128 : 128 + CHUNK]
            ty = ty + average * gy
            dx = pltpu.roll(centre, ROWS - 1, 0) - centre
            tx = tx + average * minmod(dx, pltpu.roll(dx, 1, 0))
            if z > 0:
                latter = centre - former
                if step is not None:
                    slope = 0.125 * (high_ref[z - 1] - low_ref[z - 1])
                    tz = tz + slope * minmod(latter, step)
                step = latter
        marked = mask_ref[:, pl.ds(start, CHUNK)]
        marked = jnp.broadcast_to(marked[:, None, :], (8, 8, CHUNK)).reshape(ROWS, CHUNK)
        at = pl.ds(start, CHUNK)
        calm_ref[:, at] = base - marked * base
        lifted_ref[:, at] = marked * (base + tz)
        tx_ref[:, at] = jnp.where(inside, marked * tx, 0.0)
        ty_ref[:, at] = marked * ty
        return carry

    lax.fori_loop(0, N // CHUNK, chunk, 0)


def inner_sums(low, high, density, refine):
    field = jax.ShapeDtypeStruct((ROWS, N), f32)
    return pl.pallas_call(
        inner_kernel,
        out_shape=(
            field,
            field,
            field,
            field,
            jax.ShapeDtypeStruct((8, N), f32),
            jax.ShapeDtypeStruct((4, LAYERS, N), f32),
        ),
        in_specs=[SM, SM, VM, VM],
        out_specs=(VM,) * 6,
        compiler_params=limit(40),
        cost_estimate=pl.CostEstimate(flops=40_000_000, bytes_accessed=24 * MB, transcendentals=0),
        name="inner_sums",
    )(low, high, density, refine)


def outer_kernel(
    low_ref,
    high_ref,
    d_ref,
    layer_ref,
    other_layer_ref,
    row_ref,
    other_row_ref,
    calm_ref,
    lifted_ref,
    tx_ref,
    ty_ref,
    mask_ref,
    near_ref,
    high_table,
    low_table,
    out_ref,
):
    los = lax.axis_index("zhi") * 4 + lax.axis_index("x")
    v0, v1 = d_ref[0].astype(f32), d_ref[1].astype(f32)
    v6, v7 = d_ref[6].astype(f32), d_ref[7].astype(f32)
    odd = los % 2 == 1
    one, other = layer_ref[0].astype(f32), other_layer_ref[0].astype(f32)
    below = jnp.where(los == 0, v0, jnp.where(odd, other, one))
    above = jnp.where(los == 7, v7, jnp.where(odd, one, other))
    slope0 = 0.125 * (high_ref[0] - low_ref[0])
    slope7 = 0.125 * (high_ref[7] - low_ref[7])
    tz = slope0 * minmod(v1 - v0, v0 - below) + slope7 * minmod(above - v7, v7 - v6)
    mask = mask_ref[...]
    marked = jnp.broadcast_to(mask[:, None, :], (8, 8, N)).reshape(ROWS, N)
    lifted = lifted_ref[...] + marked * tz
    layer = lax.broadcasted_iota(jnp.int32, (LAYERS, 1), 0)
    average = jnp.zeros((LAYERS, 1), f32)
    for z in range(LAYERS):
        average = jnp.where(layer == z, 0.5 * (low_ref[z] + high_ref[z]), average)
    r0, r1, r62, r63 = near_ref[0], near_ref[1], near_ref[2], near_ref[3]
    even = lax.axis_index("sky") % 2 == 0
    before = jnp.where(even, other_row_ref[...], row_ref[...])
    after = jnp.where(even, row_ref[...], other_row_ref[...])
    e0 = jnp.sum(average * minmod(r1 - r0, r0 - before), axis=0, keepdims=True)
    e63 = jnp.sum(average * minmod(after - r63, r63 - r62), axis=0, keepdims=True)
    row = lax.broadcasted_iota(jnp.int32, (ROWS, N), 0)
    tx = jnp.where(row == 0, mask[0:1] * e0, jnp.where(row == ROWS - 1, mask[7:8] * e63, tx_ref[...]))
    eighth, tilt = 0.125 * lifted, ty_ref[...] * (1.0 / 32.0)
    smooth = 0.75 * lifted + pltpu.roll(eighth + tilt, 1, 1) + pltpu.roll(eighth - tilt, N - 1, 1)
    sloped = 0.75 * tx + 0.125 * (pltpu.roll(tx, 1, 1) + pltpu.roll(tx, N - 1, 1))
    eighth, tilt = 0.125 * smooth, sloped * (1.0 / 32.0)
    none = jnp.zeros((8, N), f32)

    def longer(field):
        return jnp.concatenate([field, none], axis=0)

    kappa = (
        longer(calm_ref[...] + 0.75 * smooth)
        + pltpu.roll(longer(eighth + tilt), 1, 0)
        + pltpu.roll(longer(eighth - tilt), ROWS + 7, 0)
    )
    part = [kappa[:, 128 * a : 128 * a + 128] for a in range(16)]
    even = [part[a] + part[16 - a] for a in range(1, 8)]
    odd = [part[a] - part[16 - a] for a in range(1, 8)]

    def weigh(pairs):
        total = None
        for factor, value in pairs:
            if abs(factor) < 1e-9:
                continue
            term = value if abs(factor - 1) < 1e-9 else factor * value
            total = term if total is None else total + term
        return total

    def cosines(k):
        first = part[0] + part[8] if k % 2 == 0 else part[0] - part[8]
        return first + weigh((float(np.cos(np.pi * k * a / 8)), even[a - 1]) for a in range(1, 8))

    def sines(k):
        return weigh((float(-np.sin(np.pi * k * a / 8)), odd[a - 1]) for a in range(1, 8))

    for tile in range(8):
        second = sines(tile) if tile else cosines(8)
        value = jnp.concatenate([cosines(tile), second], axis=1)
        lanes = 256 * (tile % 2)
        out_ref[tile // 2, :, lanes : lanes + 256] = dot3(value, high_table[tile], low_table[tile])


def outer_sums(low, high, density, layers, rows, inner, tables):
    return pl.pallas_call(
        outer_kernel,
        out_shape=jax.ShapeDtypeStruct((4, 72, 512), f32),
        in_specs=[SM, SM] + [VM] * 13,
        out_specs=VM,
        compiler_params=limit(32),
        name="outer_sums",
    )(low, high, density, *layers, *rows, *inner, *tables)


def turn_kernel(in_ref, out_ref):
    total = (in_ref[0] + in_ref[1]) + (in_ref[2] + in_ref[3])
    total = jnp.concatenate([total, jnp.zeros((56, 512), f32)], axis=0)
    out_ref[...] = total.T.reshape(64, 8, 128)


def turn(pieces):
    return pl.pallas_call(
        turn_kernel,
        out_shape=jax.ShapeDtypeStruct((64, 8, 128), f32),
        in_specs=[VM],
        out_specs=VM,
        compiler_params=limit(24),
        name="turn",
    )(pieces)


def dft_32(values):
    even = [values[s] + values[32 - s] for s in range(1, 16)]
    odd = [values[s] - values[32 - s] for s in range(1, 16)]
    ends = [values[0] + values[16], values[0] - values[16]]
    cosine, sine = [None] * 17, [None] * 17
    for k in range(9):
        plain = ends[k % 2]
        turned = None
        for s in range(1, 16):
            term = float(np.cos(np.pi * k * s / 16)) * even[s - 1]
            if s % 2 == 0:
                plain = plain + term
            else:
                turned = term if turned is None else turned + term
        cosine[k] = plain + turned
        cosine[16 - k] = plain - turned
    for k in range(1, 9):
        plain, turned = None, None
        for s in range(1, 16):
            term = float(np.sin(np.pi * k * s / 16)) * odd[s - 1]
            if s % 2 == 0:
                plain = term if plain is None else plain + term
            else:
                turned = term if turned is None else turned + term
        sine[k] = turned + plain
        sine[16 - k] = turned - plain
    return cosine, sine


def solve_kernel(in_ref, cos_ref, sin_ref, high_table, low_table, out_ref):
    sky = lax.axis_index("sky")
    tile = 2 * lax.axis_index("x") + lax.axis_index("zhi")
    lane = lax.broadcasted_iota(jnp.int32, (8, 128), 1)
    sub = lax.broadcasted_iota(jnp.int32, (8, 128), 0)
    lower = lane < 64
    sign = jnp.where(sub < 4, 1.0, -1.0)
    first = jnp.logical_and(tile == 0, sky == 0)
    packed = jnp.logical_and(sub % 4 == 0, first)

    def swap(v):
        return pltpu.roll(v, 4, v.ndim - 2)

    def bent(v):
        return swap(v) * sign

    total = [in_ref[s] + in_ref[SKY + s] for s in range(SKY)]
    values = []
    for s in range(SKY):
        up = pltpu.roll(total[(s - 1) % SKY], 64, 1)
        down = pltpu.roll(total[(s + 1) % SKY], 120, 1)
        v = total[s] + jnp.where(lane == 0, up, jnp.where(lane == 63, down, 0.0))
        v = jnp.where(lower, v, pltpu.roll(v, 64, 1))
        apart = jnp.where(sub == 4, 0.0, jnp.where(lower, v, swap(v)))
        values.append(jnp.where(packed, apart, v))
    cosine, sine = dft_32(values)
    spectrum = [None] * 32
    spectrum[0], spectrum[16] = cosine[0], cosine[16]
    for k in range(1, 16):
        turned = bent(sine[k])
        spectrum[k], spectrum[32 - k] = cosine[k] + turned, cosine[k] - turned
    twisted = [spectrum[k] * cos_ref[k] + swap(spectrum[k]) * sin_ref[k] for k in range(32)]
    rows = jnp.concatenate(twisted, axis=0)
    pair = dot3(rows, high_table[...], low_table[...])
    pair_c = pair[:, :128].reshape(32, 8, 128)
    pair_s = pair[:, 128:].reshape(32, 8, 128)

    k1 = lax.broadcasted_iota(jnp.int32, (32, 8, 128), 0)
    k2 = lax.broadcasted_iota(jnp.int32, (32, 8, 128), 2) % 64
    nx = k1 + 32 * k2
    nx = jnp.where(nx < N // 2, nx, nx - N)
    n = 4 * sky + sub % 4
    ny = jnp.where(tile > 0, tile + 16 * n, jnp.where(n < 64, 16 * n, 8 + 16 * (n - 64)))
    ny = jnp.where(ny < N // 2, ny, ny - N)
    ny = jnp.where(jnp.logical_and(packed, jnp.logical_not(lower)), -(N // 2), ny)
    along_x = jnp.logical_or(packed, lower)[None]
    squared = nx * nx + (ny * ny)[None]
    wave = jnp.where(along_x, jnp.where(nx == -(N // 2), 0, nx), ny[None])
    unit = 2.0 * np.pi / N
    scale = float(-2.0 / unit / 64.0 / N / N)
    factor = scale * wave.astype(f32) / jnp.maximum(squared, 1).astype(f32)
    kappa_hat = pair_c + swap(pair_s) * sign[None]
    field = factor * (swap(kappa_hat) * (-sign)[None])
    pair = dot3(field.reshape(256, 128), high_table[...], low_table[...])
    values = []
    for k in range(32):
        v = pair[8 * k : 8 * k + 8, :128] - bent(pair[8 * k : 8 * k + 8, 128:])
        values.append(v * cos_ref[k] - swap(v) * sin_ref[k])
    cosine, sine = dft_32(values)
    for s in range(17):
        turned = bent(sine[s]) if 0 < s < 16 else None
        for at in (s,) if turned is None else (s, 32 - s):
            v = cosine[s]
            if turned is not None:
                v = v - turned if at == s else v + turned
            other = swap(pltpu.roll(v, 64, 1))
            joined = jnp.where(lower, jnp.where(sub == 4, other, v), 0.0)
            v = jnp.where(packed, joined, v)
            out_ref[at] = v
            out_ref[SKY + at] = v


def solve(pieces, tables):
    return pl.pallas_call(
        solve_kernel,
        out_shape=jax.ShapeDtypeStruct((64, 8, 128), f32),
        in_specs=[VM] * 5,
        out_specs=VM,
        compiler_params=limit(24),
        name="solve",
    )(pieces, *tables)


def back_kernel(eighth_ref, in_ref, high_table, low_table, out_ref):
    zhi, column = lax.axis_index("zhi"), lax.axis_index("x")
    value = in_ref[...]
    sub = lax.broadcasted_iota(jnp.int32, (64, 8, 128), 1)
    bent = pltpu.roll(value, 4, 1) * jnp.where(sub < 4, -1.0, 1.0)
    plain = value.reshape(512, 128).T
    bent = bent.reshape(512, 128).T
    for target in range(4):
        parts = []
        for half in range(2):
            lanes = slice(256 * half, 256 * half + 256)
            turns = (2 * column + half) * (4 * zhi + target) % 8
            cosine, sine = eighth_ref[turns], eighth_ref[8 + turns]
            parts.append(cosine * plain[:, lanes] + sine * bent[:, lanes])
        value = jnp.concatenate(parts, axis=1)
        out_ref[target] = dot3(value, high_table[column], low_table[column])


def back(pieces, tables):
    turns = np.arange(8) * (2 * np.pi / 8)
    eighth = np.concatenate([np.cos(turns), np.sin(turns)]).astype(np.float32)
    return pl.pallas_call(
        back_kernel,
        out_shape=jax.ShapeDtypeStruct((4, 128, 256), f32),
        in_specs=[SM, VM, VM, VM],
        out_specs=VM,
        compiler_params=limit(24),
        name="back",
    )(eighth, pieces, *tables)


def final_kernel(in_ref, x_ref, y_ref):
    total = (in_ref[0] + in_ref[1]) + (in_ref[2] + in_ref[3])
    x_ref[...] = total[:ROWS]
    y_ref[...] = total[ROWS:]


def final(pieces):
    shape = jax.ShapeDtypeStruct((ROWS, 256), f32)
    return pl.pallas_call(
        final_kernel,
        out_shape=(shape, shape),
        in_specs=[VM],
        out_specs=(VM, VM),
        compiler_params=limit(24),
        name="final",
    )(pieces)


def body(density, refine, weight_low, weight_high):
    odd = lax.axis_index("x") % 2 == 1

    def swap(array, axes, pairs):
        return lax.ppermute(array, axes, pairs + [(b, a) for a, b in pairs])

    layer = lax.dynamic_slice_in_dim(density, jnp.where(odd, LAYERS - 1, 0), 1, 0)
    layer = swap(layer, LOS, [(1, 2), (3, 4), (5, 6)])
    row, other_row, other_layer = edge_rows(density)
    other_layer = swap(other_layer, LOS, [(0, 1), (2, 3), (4, 5), (6, 7)])
    row = swap(row, "sky", [(i, i + 1) for i in range(0, SKY, 2)])
    other_row = swap(other_row, "sky", [(i, (i + 1) % SKY) for i in range(1, SKY, 2)])
    inner = inner_sums(weight_low, weight_high, density, refine)
    tables = halves(forward_table())
    summed = outer_sums(
        weight_low, weight_high, density, (layer, other_layer), (row, other_row), inner, tables
    )
    summed = lax.all_to_all(summed, "x", 0, 0, tiled=True)
    pieces = lax.all_to_all(turn(summed), ("zhi", "sky"), 0, 0, tiled=True)
    pieces = solve(pieces, twists() + halves(row_table()))
    pieces = lax.all_to_all(pieces, ("zhi", "sky"), 0, 0, tiled=True)
    fields = back(pieces, halves(inverse_table()))
    fields = lax.all_to_all(fields, "x", 0, 0, tiled=True)
    return final(fields)


def solution(mesh):
    devices = mesh.devices.reshape(2, 4, SKY)
    inner = Mesh(devices, ("zhi", "x", "sky"))
    placed = (P(LOS, "sky", None), P(LOS, "sky", None), P(LOS), P(LOS))
    return jax.shard_map(
        body,
        mesh=inner,
        in_specs=placed,
        out_specs=(P("sky", LOS), P("sky", LOS)),
        check_vma=False,
    )
```

```python
import functools

import jax
import jax.numpy as jnp
import ml_dtypes
import numpy as np
from jax import lax
from jax.experimental import pallas as pl
from jax.experimental.pallas import tpu as pltpu
from jax.sharding import Mesh, PartitionSpec as P

f32 = jnp.float32
bf16 = jnp.bfloat16
N = 2048
ROWS = 64
SKY = 32
LAYERS = 8
LOS = ("zhi", "x")
MB = 1024 * 1024


def halves(table):
    high = table.astype(np.float32).astype(ml_dtypes.bfloat16)
    low = (table - high.astype(np.float64)).astype(np.float32).astype(ml_dtypes.bfloat16)
    return high, low


def tile_modes(tile):
    n = np.arange(128)
    if tile:
        return tile + 16 * n
    return np.where(n < 64, 16 * n, 8 + 16 * (n - 64))


def tile_order(real, imag):
    pair = np.stack([real.reshape(SKY, 4, -1), imag.reshape(SKY, 4, -1)], axis=1)
    return pair.reshape(256, -1)


def forward_table():
    b = np.arange(128)
    tiles = []
    for tile in range(8):
        angle = (tile_modes(tile)[:, None] * b[None, :] % N) * (2 * np.pi / N)
        cosine, sine = np.cos(angle), np.sin(angle)
        if tile:
            real = np.concatenate([cosine, sine], 1)
            imag = np.concatenate([-sine, cosine], 1)
        else:
            zero = np.zeros((64, 128))
            real = np.block([[cosine[:64], zero], [zero, cosine[64:]]])
            imag = np.block([[-sine[:64], zero], [zero, -sine[64:]]])
            imag[0, :128] = (-1.0) ** b
        tiles.append(tile_order(real, imag).T)
    return np.stack(tiles)


def inverse_table():
    j = np.arange(256)
    tiles = []
    for tile in range(8):
        angle = (tile_modes(tile)[:, None] * j[None, :] % N) * (2 * np.pi / N)
        real, imag = 2 * np.cos(angle), -2 * np.sin(angle)
        if not tile:
            real[0] = 1.0
            imag[0] = (-1.0) ** j
        tiles.append(tile_order(real, imag))
    return np.stack(tiles).reshape(4, 512, 256)


def row_table():
    r = np.arange(64)
    angle = (r[:, None] * r[None, :] % 64) * (2 * np.pi / 64)
    both = np.eye(2)
    return np.concatenate([np.kron(both, np.cos(angle)), np.kron(both, np.sin(angle))], 1)


def twists():
    angle = (np.arange(32)[:, None] * (np.arange(128) % 64)[None, :]) * (2 * np.pi / N)
    sign = np.where(np.arange(8) < 4, 1.0, -1.0)
    cosine = np.broadcast_to(np.cos(angle)[:, None, :], (32, 8, 128))
    sine = np.sin(angle)[:, None, :] * sign[None, :, None]
    return cosine.astype(np.float32), sine.astype(np.float32)


def minmod(a, b):
    return jnp.maximum(jnp.minimum(a, b), 0.0) + jnp.minimum(jnp.maximum(a, b), 0.0)


def split(value):
    high = value.astype(bf16)
    return high, (value - high.astype(f32)).astype(bf16)


def dot3(value, high_table, low_table):
    high, low = split(value)
    dot = functools.partial(jnp.dot, preferred_element_type=f32)
    return dot(high, high_table) + (dot(low, high_table) + dot(high, low_table))


def limit(mib):
    return pltpu.CompilerParams(vmem_limit_bytes=mib * MB)


VM = pl.BlockSpec(memory_space=pltpu.VMEM)
SM = pl.BlockSpec(memory_space=pltpu.SMEM)


def rows_kernel(d_ref, near_ref, far_ref, layer_ref):
    layer_ref[0] = jnp.where(lax.axis_index("x") % 2 == 1, d_ref[0], d_ref[LAYERS - 1])
    even = lax.axis_index("sky") % 2 == 0
    for z in range(LAYERS):
        first = d_ref[z, 0:16, :].astype(f32)[0:1]
        last = d_ref[z, 48:64, :].astype(f32)[15:16]
        near_ref[z : z + 1, :] = jnp.where(even, last, first)
        far_ref[z : z + 1, :] = jnp.where(even, first, last)


def edge_rows(density):
    shape = jax.ShapeDtypeStruct((LAYERS, N), f32)
    return pl.pallas_call(
        rows_kernel,
        out_shape=(shape, shape, jax.ShapeDtypeStruct((1, ROWS, N), bf16)),
        in_specs=[VM],
        out_specs=(VM, VM, VM),
        compiler_params=limit(8),
        name="edge_rows",
    )(density)


CHUNK = 512


def inner_kernel(
    low_ref, high_ref, d_ref, refine_ref, calm_ref, lifted_ref, tx_ref, ty_ref, mask_ref, near_ref
):
    block = lax.broadcasted_iota(jnp.int32, (256, N), 0)
    lane = lax.broadcasted_iota(jnp.int32, (256, N), 1)
    grow = jnp.where(lane // 8 == block, 1.0, 0.0).astype(bf16)
    coarse = refine_ref[0].astype(f32).astype(bf16)
    mask_ref[...] = jnp.dot(coarse, grow, preferred_element_type=f32)
    for z in range(LAYERS):
        first = d_ref[z, 0:16, :].astype(f32)
        last = d_ref[z, 48:64, :].astype(f32)
        near_ref[0, z : z + 1, :] = first[0:1]
        near_ref[1, z : z + 1, :] = first[1:2]
        near_ref[2, z : z + 1, :] = last[14:15]
        near_ref[3, z : z + 1, :] = last[15:16]

    wide = CHUNK + 256
    row = lax.broadcasted_iota(jnp.int32, (ROWS, CHUNK), 0)
    inside = jnp.logical_and(row > 0, row < ROWS - 1)

    def chunk(i, carry):
        start = pl.multiple_of(i * CHUNK, CHUNK)
        left = pl.multiple_of((start + N - 128) % N, 128)
        right = pl.multiple_of((start + CHUNK) % N, 128)
        base = jnp.zeros((ROWS, CHUNK), f32)
        tz, tx, ty = base, base, base
        centre, step = None, None
        for z in range(LAYERS):
            average = 0.5 * (low_ref[z] + high_ref[z])
            former = centre
            around = jnp.concatenate(
                [
                    d_ref[z, :, pl.ds(left, 128)],
                    d_ref[z, :, pl.ds(start, CHUNK)],
                    d_ref[z, :, pl.ds(right, 128)],
                ],
                axis=1,
            ).astype(f32)
            centre = around[:, 128 : 128 + CHUNK]
            base = base + average * centre
            dy = pltpu.roll(around, wide - 1, 1) - around
            gy = minmod(dy, pltpu.roll(dy, 1, 1))[:, 128 : 128 + CHUNK]
            ty = ty + average * gy
            dx = pltpu.roll(centre, ROWS - 1, 0) - centre
            tx = tx + average * minmod(dx, pltpu.roll(dx, 1, 0))
            if z > 0:
                latter = centre - former
                if step is not None:
                    slope = 0.125 * (high_ref[z - 1] - low_ref[z - 1])
                    tz = tz + slope * minmod(latter, step)
                step = latter
        marked = mask_ref[:, pl.ds(start, CHUNK)]
        marked = jnp.broadcast_to(marked[:, None, :], (8, 8, CHUNK)).reshape(ROWS, CHUNK)
        at = pl.ds(start, CHUNK)
        calm_ref[:, at] = base - marked * base
        lifted_ref[:, at] = marked * (base + tz)
        tx_ref[:, at] = jnp.where(inside, marked * tx, 0.0)
        ty_ref[:, at] = marked * ty
        return carry

    lax.fori_loop(0, N // CHUNK, chunk, 0)


def inner_sums(low, high, density, refine):
    field = jax.ShapeDtypeStruct((ROWS, N), f32)
    return pl.pallas_call(
        inner_kernel,
        out_shape=(
            field,
            field,
            field,
            field,
            jax.ShapeDtypeStruct((8, N), f32),
            jax.ShapeDtypeStruct((4, LAYERS, N), f32),
        ),
        in_specs=[SM, SM, VM, VM],
        out_specs=(VM,) * 6,
        compiler_params=limit(40),
        cost_estimate=pl.CostEstimate(flops=40_000_000, bytes_accessed=24 * MB, transcendentals=0),
        name="inner_sums",
    )(low, high, density, refine)


def outer_kernel(
    low_ref,
    high_ref,
    d_ref,
    layer_ref,
    other_layer_ref,
    row_ref,
    other_row_ref,
    calm_ref,
    lifted_ref,
    tx_ref,
    ty_ref,
    mask_ref,
    near_ref,
    high_table,
    low_table,
    *rest,
):
    outs, (high_part, low_part) = rest[:4], rest[4:]
    los = lax.axis_index("zhi") * 4 + lax.axis_index("x")
    v0, v1 = d_ref[0].astype(f32), d_ref[1].astype(f32)
    v6, v7 = d_ref[6].astype(f32), d_ref[7].astype(f32)
    odd = los % 2 == 1
    one, other = layer_ref[0].astype(f32), other_layer_ref[0].astype(f32)
    below = jnp.where(los == 0, v0, jnp.where(odd, other, one))
    above = jnp.where(los == 7, v7, jnp.where(odd, one, other))
    slope0 = 0.125 * (high_ref[0] - low_ref[0])
    slope7 = 0.125 * (high_ref[7] - low_ref[7])
    tz = slope0 * minmod(v1 - v0, v0 - below) + slope7 * minmod(above - v7, v7 - v6)
    mask = mask_ref[...]
    marked = jnp.broadcast_to(mask[:, None, :], (8, 8, N)).reshape(ROWS, N)
    lifted = lifted_ref[...] + marked * tz
    layer = lax.broadcasted_iota(jnp.int32, (LAYERS, 1), 0)
    average = jnp.zeros((LAYERS, 1), f32)
    for z in range(LAYERS):
        average = jnp.where(layer == z, 0.5 * (low_ref[z] + high_ref[z]), average)
    r0, r1, r62, r63 = near_ref[0], near_ref[1], near_ref[2], near_ref[3]
    even = lax.axis_index("sky") % 2 == 0
    before = jnp.where(even, other_row_ref[...], row_ref[...])
    after = jnp.where(even, row_ref[...], other_row_ref[...])
    e0 = jnp.sum(average * minmod(r1 - r0, r0 - before), axis=0, keepdims=True)
    e63 = jnp.sum(average * minmod(after - r63, r63 - r62), axis=0, keepdims=True)
    row = lax.broadcasted_iota(jnp.int32, (ROWS, N), 0)
    tx = jnp.where(row == 0, mask[0:1] * e0, jnp.where(row == ROWS - 1, mask[7:8] * e63, tx_ref[...]))
    eighth, tilt = 0.125 * lifted, ty_ref[...] * (1.0 / 32.0)
    smooth = 0.75 * lifted + pltpu.roll(eighth + tilt, 1, 1) + pltpu.roll(eighth - tilt, N - 1, 1)
    sloped = 0.75 * tx + 0.125 * (pltpu.roll(tx, 1, 1) + pltpu.roll(tx, N - 1, 1))
    eighth, tilt = 0.125 * smooth, sloped * (1.0 / 32.0)
    none = jnp.zeros((8, N), f32)

    def longer(field):
        return jnp.concatenate([field, none], axis=0)

    kappa = (
        longer(calm_ref[...] + 0.75 * smooth)
        + pltpu.roll(longer(eighth + tilt), 1, 0)
        + pltpu.roll(longer(eighth - tilt), ROWS + 7, 0)
    )
    part = [kappa[:, 128 * a : 128 * a + 128] for a in range(16)]
    even = [part[a] + part[16 - a] for a in range(1, 8)]
    odd = [part[a] - part[16 - a] for a in range(1, 8)]

    def weigh(pairs):
        total = None
        for factor, value in pairs:
            if abs(factor) < 1e-9:
                continue
            term = value if abs(factor - 1) < 1e-9 else factor * value
            total = term if total is None else total + term
        return total

    def cosines(k):
        first = part[0] + part[8] if k % 2 == 0 else part[0] - part[8]
        return first + weigh((float(np.cos(np.pi * k * a / 8)), even[a - 1]) for a in range(1, 8))

    def sines(k):
        return weigh((float(-np.sin(np.pi * k * a / 8)), odd[a - 1]) for a in range(1, 8))

    for tile in range(8):
        second = sines(tile) if tile else cosines(8)
        high_part[tile], low_part[tile] = split(jnp.concatenate([cosines(tile), second], axis=1))
    dot = functools.partial(jnp.dot, preferred_element_type=f32)
    for ahead in range(4):
        target = (lax.axis_index("x") + ahead) % 4
        for half in range(2):
            tile = 2 * target + half
            high, low, table = high_part[tile], low_part[tile], high_table[tile]
            value = dot(high, table) + (dot(low, table) + dot(high, low_table[tile]))
            outs[ahead][:, 256 * half : 256 * half + 256] = value


def outer_sums(low, high, density, layers, rows, inner, tables):
    return pl.pallas_call(
        outer_kernel,
        out_shape=(jax.ShapeDtypeStruct((72, 512), f32),) * 4,
        in_specs=[SM, SM] + [VM] * 13,
        out_specs=(VM,) * 4,
        scratch_shapes=[pltpu.VMEM((8, 72, 256), bf16)] * 2,
        compiler_params=limit(32),
        name="outer_sums",
    )(low, high, density, *layers, *rows, *inner, *tables)


def turn_kernel(a_ref, b_ref, c_ref, d_ref, out_ref):
    total = (a_ref[...] + b_ref[...]) + (c_ref[...] + d_ref[...])
    total = jnp.concatenate([total, jnp.zeros((56, 512), f32)], axis=0)
    out_ref[...] = total.T.reshape(64, 8, 128)


def turn(pieces):
    return pl.pallas_call(
        turn_kernel,
        out_shape=jax.ShapeDtypeStruct((64, 8, 128), f32),
        in_specs=[VM] * 4,
        out_specs=VM,
        compiler_params=limit(24),
        name="turn",
    )(*pieces)


def dft_32(values):
    even = [values[s] + values[32 - s] for s in range(1, 16)]
    odd = [values[s] - values[32 - s] for s in range(1, 16)]
    ends = [values[0] + values[16], values[0] - values[16]]
    cosine, sine = [None] * 17, [None] * 17
    for k in range(9):
        plain = ends[k % 2]
        turned = None
        for s in range(1, 16):
            term = float(np.cos(np.pi * k * s / 16)) * even[s - 1]
            if s % 2 == 0:
                plain = plain + term
            else:
                turned = term if turned is None else turned + term
        cosine[k] = plain + turned
        cosine[16 - k] = plain - turned
    for k in range(1, 9):
        plain, turned = None, None
        for s in range(1, 16):
            term = float(np.sin(np.pi * k * s / 16)) * odd[s - 1]
            if s % 2 == 0:
                plain = term if plain is None else plain + term
            else:
                turned = term if turned is None else turned + term
        sine[k] = turned + plain
        sine[16 - k] = turned - plain
    return cosine, sine


def solve_kernel(in_ref, cos_ref, sin_ref, high_table, low_table, out_ref):
    sky = lax.axis_index("sky")
    tile = 2 * lax.axis_index("x") + lax.axis_index("zhi")
    lane = lax.broadcasted_iota(jnp.int32, (8, 128), 1)
    sub = lax.broadcasted_iota(jnp.int32, (8, 128), 0)
    lower = lane < 64
    sign = jnp.where(sub < 4, 1.0, -1.0)
    first = jnp.logical_and(tile == 0, sky == 0)
    packed = jnp.logical_and(sub % 4 == 0, first)

    def swap(v):
        return pltpu.roll(v, 4, v.ndim - 2)

    def bent(v):
        return swap(v) * sign

    total = [in_ref[s] + in_ref[SKY + s] for s in range(SKY)]
    values = []
    for s in range(SKY):
        up = pltpu.roll(total[(s - 1) % SKY], 64, 1)
        down = pltpu.roll(total[(s + 1) % SKY], 120, 1)
        v = total[s] + jnp.where(lane == 0, up, jnp.where(lane == 63, down, 0.0))
        v = jnp.where(lower, v, pltpu.roll(v, 64, 1))
        apart = jnp.where(sub == 4, 0.0, jnp.where(lower, v, swap(v)))
        values.append(jnp.where(packed, apart, v))
    cosine, sine = dft_32(values)
    spectrum = [None] * 32
    spectrum[0], spectrum[16] = cosine[0], cosine[16]
    for k in range(1, 16):
        turned = bent(sine[k])
        spectrum[k], spectrum[32 - k] = cosine[k] + turned, cosine[k] - turned
    twisted = [spectrum[k] * cos_ref[k] + swap(spectrum[k]) * sin_ref[k] for k in range(32)]
    rows = jnp.concatenate(twisted, axis=0)
    pair = dot3(rows, high_table[...], low_table[...])
    pair_c = pair[:, :128].reshape(32, 8, 128)
    pair_s = pair[:, 128:].reshape(32, 8, 128)

    k1 = lax.broadcasted_iota(jnp.int32, (32, 8, 128), 0)
    k2 = lax.broadcasted_iota(jnp.int32, (32, 8, 128), 2) % 64
    nx = k1 + 32 * k2
    nx = jnp.where(nx < N // 2, nx, nx - N)
    n = 4 * sky + sub % 4
    ny = jnp.where(tile > 0, tile + 16 * n, jnp.where(n < 64, 16 * n, 8 + 16 * (n - 64)))
    ny = jnp.where(ny < N // 2, ny, ny - N)
    ny = jnp.where(jnp.logical_and(packed, jnp.logical_not(lower)), -(N // 2), ny)
    along_x = jnp.logical_or(packed, lower)[None]
    squared = nx * nx + (ny * ny)[None]
    wave = jnp.where(along_x, jnp.where(nx == -(N // 2), 0, nx), ny[None])
    unit = 2.0 * np.pi / N
    scale = float(-2.0 / unit / 64.0 / N / N)
    factor = scale * wave.astype(f32) / jnp.maximum(squared, 1).astype(f32)
    kappa_hat = pair_c + swap(pair_s) * sign[None]
    field = factor * (swap(kappa_hat) * (-sign)[None])
    pair = dot3(field.reshape(256, 128), high_table[...], low_table[...])
    values = []
    for k in range(32):
        v = pair[8 * k : 8 * k + 8, :128] - bent(pair[8 * k : 8 * k + 8, 128:])
        values.append(v * cos_ref[k] - swap(v) * sin_ref[k])
    cosine, sine = dft_32(values)
    for s in range(17):
        turned = bent(sine[s]) if 0 < s < 16 else None
        for at in (s,) if turned is None else (s, 32 - s):
            v = cosine[s]
            if turned is not None:
                v = v - turned if at == s else v + turned
            other = swap(pltpu.roll(v, 64, 1))
            joined = jnp.where(lower, jnp.where(sub == 4, other, v), 0.0)
            v = jnp.where(packed, joined, v)
            out_ref[at] = v
            out_ref[SKY + at] = v


def solve(pieces, tables):
    return pl.pallas_call(
        solve_kernel,
        out_shape=jax.ShapeDtypeStruct((64, 8, 128), f32),
        in_specs=[VM] * 5,
        out_specs=VM,
        compiler_params=limit(24),
        name="solve",
    )(pieces, *tables)


def back_kernel(eighth_ref, in_ref, high_table, low_table, *outs):
    zhi, column = lax.axis_index("zhi"), lax.axis_index("x")
    value = in_ref[...]
    sub = lax.broadcasted_iota(jnp.int32, (64, 8, 128), 1)
    bent = pltpu.roll(value, 4, 1) * jnp.where(sub < 4, -1.0, 1.0)
    plain = value.reshape(512, 128).T
    bent = bent.reshape(512, 128).T
    for ahead in range(4):
        target = (column + ahead) % 4
        parts = []
        for half in range(2):
            lanes = slice(256 * half, 256 * half + 256)
            turns = (2 * column + half) * (4 * zhi + target) % 8
            cosine, sine = eighth_ref[turns], eighth_ref[8 + turns]
            parts.append(cosine * plain[:, lanes] + sine * bent[:, lanes])
        value = jnp.concatenate(parts, axis=1)
        outs[ahead][...] = dot3(value, high_table[column], low_table[column])


def back(pieces, tables):
    turns = np.arange(8) * (2 * np.pi / 8)
    eighth = np.concatenate([np.cos(turns), np.sin(turns)]).astype(np.float32)
    return pl.pallas_call(
        back_kernel,
        out_shape=(jax.ShapeDtypeStruct((128, 256), f32),) * 4,
        in_specs=[SM, VM, VM, VM],
        out_specs=(VM,) * 4,
        compiler_params=limit(24),
        name="back",
    )(eighth, pieces, *tables)


def final_kernel(a_ref, b_ref, c_ref, d_ref, x_ref, y_ref):
    total = (a_ref[...] + b_ref[...]) + (c_ref[...] + d_ref[...])
    x_ref[...] = total[:ROWS]
    y_ref[...] = total[ROWS:]


def final(pieces):
    shape = jax.ShapeDtypeStruct((ROWS, 256), f32)
    return pl.pallas_call(
        final_kernel,
        out_shape=(shape, shape),
        in_specs=[VM] * 4,
        out_specs=(VM, VM),
        compiler_params=limit(24),
        name="final",
    )(*pieces)


def deliver(pieces):
    return [pieces[0]] + [
        lax.ppermute(pieces[a], "x", [(i, (i + a) % 4) for i in range(4)]) for a in (1, 2, 3)
    ]


def body(density, refine, weight_low, weight_high):
    odd = lax.axis_index("x") % 2 == 1

    def swap(array, axes, pairs):
        return lax.ppermute(array, axes, pairs + [(b, a) for a, b in pairs])

    layer = lax.dynamic_slice_in_dim(density, jnp.where(odd, LAYERS - 1, 0), 1, 0)
    layer = swap(layer, LOS, [(1, 2), (3, 4), (5, 6)])
    row, other_row, other_layer = edge_rows(density)
    other_layer = swap(other_layer, LOS, [(0, 1), (2, 3), (4, 5), (6, 7)])
    row = swap(row, "sky", [(i, i + 1) for i in range(0, SKY, 2)])
    other_row = swap(other_row, "sky", [(i, (i + 1) % SKY) for i in range(1, SKY, 2)])
    inner = inner_sums(weight_low, weight_high, density, refine)
    tables = halves(forward_table())
    summed = outer_sums(
        weight_low, weight_high, density, (layer, other_layer), (row, other_row), inner, tables
    )
    summed = deliver(summed)
    pieces = lax.all_to_all(turn(summed), ("zhi", "sky"), 0, 0, tiled=True)
    pieces = solve(pieces, twists() + halves(row_table()))
    pieces = lax.all_to_all(pieces, ("zhi", "sky"), 0, 0, tiled=True)
    fields = back(pieces, halves(inverse_table()))
    return final(deliver(fields))


def solution(mesh):
    devices = mesh.devices.reshape(2, 4, SKY)
    inner = Mesh(devices, ("zhi", "x", "sky"))
    placed = (P(LOS, "sky", None), P(LOS, "sky", None), P(LOS), P(LOS))
    return jax.shard_map(
        body,
        mesh=inner,
        in_specs=placed,
        out_specs=(P("sky", LOS), P("sky", LOS)),
        check_vma=False,
    )
```

```python
import functools

import jax
import jax.numpy as jnp
import ml_dtypes
import numpy as np
from jax import lax
from jax.experimental import pallas as pl
from jax.experimental.pallas import tpu as pltpu
from jax.sharding import Mesh, PartitionSpec as P

f32 = jnp.float32
bf16 = jnp.bfloat16
N = 2048
ROWS = 64
SKY = 32
LAYERS = 8
LOS = ("zhi", "x")
MB = 1024 * 1024


def halves(table):
    high = table.astype(np.float32).astype(ml_dtypes.bfloat16)
    low = (table - high.astype(np.float64)).astype(np.float32).astype(ml_dtypes.bfloat16)
    return high, low


def tile_modes(tile):
    n = np.arange(128)
    if tile:
        return tile + 16 * n
    return np.where(n < 64, 16 * n, 8 + 16 * (n - 64))


def tile_order(real, imag):
    pair = np.stack([real.reshape(SKY, 4, -1), imag.reshape(SKY, 4, -1)], axis=1)
    return pair.reshape(256, -1)


def forward_table():
    b = np.arange(128)
    tiles = []
    for tile in range(8):
        angle = (tile_modes(tile)[:, None] * b[None, :] % N) * (2 * np.pi / N)
        cosine, sine = np.cos(angle), np.sin(angle)
        if tile:
            real = np.concatenate([cosine, sine], 1)
            imag = np.concatenate([-sine, cosine], 1)
        else:
            zero = np.zeros((64, 128))
            real = np.block([[cosine[:64], zero], [zero, cosine[64:]]])
            imag = np.block([[-sine[:64], zero], [zero, -sine[64:]]])
            imag[0, :128] = (-1.0) ** b
        tiles.append(tile_order(real, imag).T)
    return np.stack(tiles)


def inverse_table():
    j = np.arange(256)
    tiles = []
    for tile in range(8):
        angle = (tile_modes(tile)[:, None] * j[None, :] % N) * (2 * np.pi / N)
        real, imag = 2 * np.cos(angle), -2 * np.sin(angle)
        if not tile:
            real[0] = 1.0
            imag[0] = (-1.0) ** j
        tiles.append(tile_order(real, imag))
    return np.stack(tiles).reshape(4, 512, 256)


def row_table():
    r = np.arange(64)
    angle = (r[:, None] * r[None, :] % 64) * (2 * np.pi / 64)
    both = np.eye(2)
    return np.concatenate([np.kron(both, np.cos(angle)), np.kron(both, np.sin(angle))], 1)


def twists():
    angle = (np.arange(32)[:, None] * (np.arange(128) % 64)[None, :]) * (2 * np.pi / N)
    sign = np.where(np.arange(8) < 4, 1.0, -1.0)
    cosine = np.broadcast_to(np.cos(angle)[:, None, :], (32, 8, 128))
    sine = np.sin(angle)[:, None, :] * sign[None, :, None]
    return cosine.astype(np.float32), sine.astype(np.float32)


def minmod(a, b):
    return jnp.maximum(jnp.minimum(a, b), 0.0) + jnp.minimum(jnp.maximum(a, b), 0.0)


def split(value):
    high = value.astype(bf16)
    return high, (value - high.astype(f32)).astype(bf16)


def dot3(value, high_table, low_table):
    high, low = split(value)
    dot = functools.partial(jnp.dot, preferred_element_type=f32)
    return dot(high, high_table) + (dot(low, high_table) + dot(high, low_table))


def limit(mib):
    return pltpu.CompilerParams(vmem_limit_bytes=mib * MB)


VM = pl.BlockSpec(memory_space=pltpu.VMEM)
SM = pl.BlockSpec(memory_space=pltpu.SMEM)


def rows_kernel(d_ref, near_ref, far_ref, layer_ref):
    layer_ref[0] = jnp.where(lax.axis_index("x") % 2 == 1, d_ref[0], d_ref[LAYERS - 1])
    even = lax.axis_index("sky") % 2 == 0
    for z in range(LAYERS):
        first = d_ref[z, 0:16, :].astype(f32)[0:1]
        last = d_ref[z, 48:64, :].astype(f32)[15:16]
        near_ref[z : z + 1, :] = jnp.where(even, last, first)
        far_ref[z : z + 1, :] = jnp.where(even, first, last)


def edge_rows(density):
    shape = jax.ShapeDtypeStruct((LAYERS, N), f32)
    return pl.pallas_call(
        rows_kernel,
        out_shape=(shape, shape, jax.ShapeDtypeStruct((1, ROWS, N), bf16)),
        in_specs=[VM],
        out_specs=(VM, VM, VM),
        compiler_params=limit(8),
        name="edge_rows",
    )(density)


def longer(field):
    return jnp.concatenate([field, jnp.zeros((8, N), f32)], axis=0)


def smooth_y(field):
    return 0.75 * field + 0.125 * (pltpu.roll(field, 1, 1) + pltpu.roll(field, N - 1, 1))


CHUNK = 512


def inner_kernel(
    low_ref,
    high_ref,
    d_ref,
    refine_ref,
    kappa_ref,
    mask_ref,
    near_ref,
    calm_ref,
    lifted_ref,
    tx_ref,
    ty_ref,
):
    block = lax.broadcasted_iota(jnp.int32, (256, N), 0)
    lane = lax.broadcasted_iota(jnp.int32, (256, N), 1)
    grow = jnp.where(lane // 8 == block, 1.0, 0.0).astype(bf16)
    coarse = refine_ref[0].astype(f32).astype(bf16)
    mask_ref[...] = jnp.dot(coarse, grow, preferred_element_type=f32)
    for z in range(LAYERS):
        first = d_ref[z, 0:16, :].astype(f32)
        last = d_ref[z, 48:64, :].astype(f32)
        near_ref[0, z : z + 1, :] = first[0:1]
        near_ref[1, z : z + 1, :] = first[1:2]
        near_ref[2, z : z + 1, :] = last[14:15]
        near_ref[3, z : z + 1, :] = last[15:16]

    wide = CHUNK + 256
    row = lax.broadcasted_iota(jnp.int32, (ROWS, CHUNK), 0)
    inside = jnp.logical_and(row > 0, row < ROWS - 1)

    def chunk(i, carry):
        start = pl.multiple_of(i * CHUNK, CHUNK)
        left = pl.multiple_of((start + N - 128) % N, 128)
        right = pl.multiple_of((start + CHUNK) % N, 128)
        base = jnp.zeros((ROWS, CHUNK), f32)
        tz, tx, ty = base, base, base
        centre, step = None, None
        for z in range(LAYERS):
            average = 0.5 * (low_ref[z] + high_ref[z])
            former = centre
            around = jnp.concatenate(
                [
                    d_ref[z, :, pl.ds(left, 128)],
                    d_ref[z, :, pl.ds(start, CHUNK)],
                    d_ref[z, :, pl.ds(right, 128)],
                ],
                axis=1,
            ).astype(f32)
            centre = around[:, 128 : 128 + CHUNK]
            base = base + average * centre
            dy = pltpu.roll(around, wide - 1, 1) - around
            gy = minmod(dy, pltpu.roll(dy, 1, 1))[:, 128 : 128 + CHUNK]
            ty = ty + average * gy
            dx = pltpu.roll(centre, ROWS - 1, 0) - centre
            tx = tx + average * minmod(dx, pltpu.roll(dx, 1, 0))
            if z > 0:
                latter = centre - former
                if step is not None:
                    slope = 0.125 * (high_ref[z - 1] - low_ref[z - 1])
                    tz = tz + slope * minmod(latter, step)
                step = latter
        marked = mask_ref[:, pl.ds(start, CHUNK)]
        marked = jnp.broadcast_to(marked[:, None, :], (8, 8, CHUNK)).reshape(ROWS, CHUNK)
        at = pl.ds(start, CHUNK)
        calm_ref[:, at] = base - marked * base
        lifted_ref[:, at] = marked * (base + tz)
        tx_ref[:, at] = jnp.where(inside, marked * tx, 0.0)
        ty_ref[:, at] = marked * ty
        return carry

    lax.fori_loop(0, N // CHUNK, chunk, 0)
    lifted, tx = lifted_ref[...], tx_ref[...]
    eighth, tilt = 0.125 * lifted, ty_ref[...] * (1.0 / 32.0)
    smooth = 0.75 * lifted + pltpu.roll(eighth + tilt, 1, 1) + pltpu.roll(eighth - tilt, N - 1, 1)
    eighth, tilt = 0.125 * smooth, smooth_y(tx) * (1.0 / 32.0)
    kappa_ref[...] = (
        longer(calm_ref[...] + 0.75 * smooth)
        + pltpu.roll(longer(eighth + tilt), 1, 0)
        + pltpu.roll(longer(eighth - tilt), ROWS + 7, 0)
    )


def inner_sums(low, high, density, refine):
    return pl.pallas_call(
        inner_kernel,
        out_shape=(
            jax.ShapeDtypeStruct((ROWS + 8, N), f32),
            jax.ShapeDtypeStruct((8, N), f32),
            jax.ShapeDtypeStruct((4, LAYERS, N), f32),
        ),
        in_specs=[SM, SM, VM, VM],
        out_specs=(VM,) * 3,
        scratch_shapes=[pltpu.VMEM((ROWS, N), f32)] * 4,
        compiler_params=limit(40),
        cost_estimate=pl.CostEstimate(flops=40_000_000, bytes_accessed=24 * MB, transcendentals=0),
        name="inner_sums",
    )(low, high, density, refine)


def outer_kernel(
    low_ref,
    high_ref,
    d_ref,
    layer_ref,
    other_layer_ref,
    row_ref,
    other_row_ref,
    kappa_ref,
    mask_ref,
    near_ref,
    high_table,
    low_table,
    *rest,
):
    outs, (high_part, low_part) = rest[:4], rest[4:]
    los = lax.axis_index("zhi") * 4 + lax.axis_index("x")
    v0, v1 = d_ref[0].astype(f32), d_ref[1].astype(f32)
    v6, v7 = d_ref[6].astype(f32), d_ref[7].astype(f32)
    odd = los % 2 == 1
    one, other = layer_ref[0].astype(f32), other_layer_ref[0].astype(f32)
    below = jnp.where(los == 0, v0, jnp.where(odd, other, one))
    above = jnp.where(los == 7, v7, jnp.where(odd, one, other))
    slope0 = 0.125 * (high_ref[0] - low_ref[0])
    slope7 = 0.125 * (high_ref[7] - low_ref[7])
    tz = slope0 * minmod(v1 - v0, v0 - below) + slope7 * minmod(above - v7, v7 - v6)
    mask = mask_ref[...]
    marked = jnp.broadcast_to(mask[:, None, :], (8, 8, N)).reshape(ROWS, N)
    smooth = smooth_y(marked * tz)
    layer = lax.broadcasted_iota(jnp.int32, (LAYERS, 1), 0)
    average = jnp.zeros((LAYERS, 1), f32)
    for z in range(LAYERS):
        average = jnp.where(layer == z, 0.5 * (low_ref[z] + high_ref[z]), average)
    r0, r1, r62, r63 = near_ref[0], near_ref[1], near_ref[2], near_ref[3]
    even = lax.axis_index("sky") % 2 == 0
    before = jnp.where(even, other_row_ref[...], row_ref[...])
    after = jnp.where(even, row_ref[...], other_row_ref[...])
    e0 = jnp.sum(average * minmod(r1 - r0, r0 - before), axis=0, keepdims=True)
    e63 = jnp.sum(average * minmod(after - r63, r63 - r62), axis=0, keepdims=True)
    row = lax.broadcasted_iota(jnp.int32, (8, N), 0)
    e0 = smooth_y(jnp.where(row == 0, mask[0:1] * e0, 0.0)) * (1.0 / 32.0)
    e63 = smooth_y(jnp.where(row == 7, mask[7:8] * e63, 0.0)) * (1.0 / 32.0)
    first = pltpu.roll(e0, 1, 0)
    last = pltpu.roll(e63, 7, 0)
    spill = jnp.where(row == 0, pltpu.roll(e63, 1, 0), -pltpu.roll(e0, 7, 0))
    sides = jnp.concatenate([first, jnp.zeros((ROWS - 16, N), f32), -last, spill], axis=0)
    eighth = longer(0.125 * smooth)
    kappa = (
        (kappa_ref[...] + sides)
        + longer(0.75 * smooth)
        + (pltpu.roll(eighth, 1, 0) + pltpu.roll(eighth, ROWS + 7, 0))
    )
    part = [kappa[:, 128 * a : 128 * a + 128] for a in range(16)]
    even = [part[a] + part[16 - a] for a in range(1, 8)]
    odd = [part[a] - part[16 - a] for a in range(1, 8)]

    def weigh(pairs):
        total = None
        for factor, value in pairs:
            if abs(factor) < 1e-9:
                continue
            term = value if abs(factor - 1) < 1e-9 else factor * value
            total = term if total is None else total + term
        return total

    def cosines(k):
        first = part[0] + part[8] if k % 2 == 0 else part[0] - part[8]
        return first + weigh((float(np.cos(np.pi * k * a / 8)), even[a - 1]) for a in range(1, 8))

    def sines(k):
        return weigh((float(-np.sin(np.pi * k * a / 8)), odd[a - 1]) for a in range(1, 8))

    for tile in range(8):
        second = sines(tile) if tile else cosines(8)
        high_part[tile], low_part[tile] = split(jnp.concatenate([cosines(tile), second], axis=1))
    dot = functools.partial(jnp.dot, preferred_element_type=f32)
    for ahead in range(4):
        target = (lax.axis_index("x") + ahead) % 4
        for half in range(2):
            tile = 2 * target + half
            high, low, table = high_part[tile], low_part[tile], high_table[tile]
            value = dot(high, table) + (dot(low, table) + dot(high, low_table[tile]))
            outs[ahead][:, 256 * half : 256 * half + 256] = value


def outer_sums(low, high, density, layers, rows, inner, tables):
    return pl.pallas_call(
        outer_kernel,
        out_shape=(jax.ShapeDtypeStruct((72, 512), f32),) * 4,
        in_specs=[SM, SM] + [VM] * 10,
        out_specs=(VM,) * 4,
        scratch_shapes=[pltpu.VMEM((8, 72, 256), bf16)] * 2,
        compiler_params=limit(32),
        name="outer_sums",
    )(low, high, density, *layers, *rows, *inner, *tables)


def turn_kernel(a_ref, b_ref, c_ref, d_ref, out_ref):
    total = (a_ref[...] + b_ref[...]) + (c_ref[...] + d_ref[...])
    total = jnp.concatenate([total, jnp.zeros((56, 512), f32)], axis=0)
    out_ref[...] = total.T.reshape(64, 8, 128)


def turn(pieces):
    return pl.pallas_call(
        turn_kernel,
        out_shape=jax.ShapeDtypeStruct((64, 8, 128), f32),
        in_specs=[VM] * 4,
        out_specs=VM,
        compiler_params=limit(24),
        name="turn",
    )(*pieces)


def dft_32(values):
    even = [values[s] + values[32 - s] for s in range(1, 16)]
    odd = [values[s] - values[32 - s] for s in range(1, 16)]
    ends = [values[0] + values[16], values[0] - values[16]]
    cosine, sine = [None] * 17, [None] * 17
    for k in range(9):
        plain = ends[k % 2]
        turned = None
        for s in range(1, 16):
            term = float(np.cos(np.pi * k * s / 16)) * even[s - 1]
            if s % 2 == 0:
                plain = plain + term
            else:
                turned = term if turned is None else turned + term
        cosine[k] = plain + turned
        cosine[16 - k] = plain - turned
    for k in range(1, 9):
        plain, turned = None, None
        for s in range(1, 16):
            term = float(np.sin(np.pi * k * s / 16)) * odd[s - 1]
            if s % 2 == 0:
                plain = term if plain is None else plain + term
            else:
                turned = term if turned is None else turned + term
        sine[k] = turned + plain
        sine[16 - k] = turned - plain
    return cosine, sine


def solve_kernel(in_ref, cos_ref, sin_ref, high_table, low_table, out_ref):
    sky = lax.axis_index("sky")
    tile = 2 * lax.axis_index("x") + lax.axis_index("zhi")
    lane = lax.broadcasted_iota(jnp.int32, (8, 128), 1)
    sub = lax.broadcasted_iota(jnp.int32, (8, 128), 0)
    lower = lane < 64
    sign = jnp.where(sub < 4, 1.0, -1.0)
    first = jnp.logical_and(tile == 0, sky == 0)
    packed = jnp.logical_and(sub % 4 == 0, first)

    def swap(v):
        return pltpu.roll(v, 4, v.ndim - 2)

    def bent(v):
        return swap(v) * sign

    total = [in_ref[s] + in_ref[SKY + s] for s in range(SKY)]
    values = []
    for s in range(SKY):
        up = pltpu.roll(total[(s - 1) % SKY], 64, 1)
        down = pltpu.roll(total[(s + 1) % SKY], 120, 1)
        v = total[s] + jnp.where(lane == 0, up, jnp.where(lane == 63, down, 0.0))
        v = jnp.where(lower, v, pltpu.roll(v, 64, 1))
        apart = jnp.where(sub == 4, 0.0, jnp.where(lower, v, swap(v)))
        values.append(jnp.where(packed, apart, v))
    cosine, sine = dft_32(values)
    spectrum = [None] * 32
    spectrum[0], spectrum[16] = cosine[0], cosine[16]
    for k in range(1, 16):
        turned = bent(sine[k])
        spectrum[k], spectrum[32 - k] = cosine[k] + turned, cosine[k] - turned
    twisted = [spectrum[k] * cos_ref[k] + swap(spectrum[k]) * sin_ref[k] for k in range(32)]
    rows = jnp.concatenate(twisted, axis=0)
    pair = dot3(rows, high_table[...], low_table[...])
    pair_c = pair[:, :128].reshape(32, 8, 128)
    pair_s = pair[:, 128:].reshape(32, 8, 128)

    k1 = lax.broadcasted_iota(jnp.int32, (32, 8, 128), 0)
    k2 = lax.broadcasted_iota(jnp.int32, (32, 8, 128), 2) % 64
    nx = k1 + 32 * k2
    nx = jnp.where(nx < N // 2, nx, nx - N)
    n = 4 * sky + sub % 4
    ny = jnp.where(tile > 0, tile + 16 * n, jnp.where(n < 64, 16 * n, 8 + 16 * (n - 64)))
    ny = jnp.where(ny < N // 2, ny, ny - N)
    ny = jnp.where(jnp.logical_and(packed, jnp.logical_not(lower)), -(N // 2), ny)
    along_x = jnp.logical_or(packed, lower)[None]
    squared = nx * nx + (ny * ny)[None]
    wave = jnp.where(along_x, jnp.where(nx == -(N // 2), 0, nx), ny[None])
    unit = 2.0 * np.pi / N
    scale = float(-2.0 / unit / 64.0 / N / N)
    factor = scale * wave.astype(f32) / jnp.maximum(squared, 1).astype(f32)
    kappa_hat = pair_c + swap(pair_s) * sign[None]
    field = factor * (swap(kappa_hat) * (-sign)[None])
    pair = dot3(field.reshape(256, 128), high_table[...], low_table[...])
    values = []
    for k in range(32):
        v = pair[8 * k : 8 * k + 8, :128] - bent(pair[8 * k : 8 * k + 8, 128:])
        values.append(v * cos_ref[k] - swap(v) * sin_ref[k])
    cosine, sine = dft_32(values)
    for s in range(17):
        turned = bent(sine[s]) if 0 < s < 16 else None
        for at in (s,) if turned is None else (s, 32 - s):
            v = cosine[s]
            if turned is not None:
                v = v - turned if at == s else v + turned
            other = swap(pltpu.roll(v, 64, 1))
            joined = jnp.where(lower, jnp.where(sub == 4, other, v), 0.0)
            v = jnp.where(packed, joined, v)
            out_ref[at] = v
            out_ref[SKY + at] = v


def solve(pieces, tables):
    return pl.pallas_call(
        solve_kernel,
        out_shape=jax.ShapeDtypeStruct((64, 8, 128), f32),
        in_specs=[VM] * 5,
        out_specs=VM,
        compiler_params=limit(24),
        name="solve",
    )(pieces, *tables)


def back_kernel(eighth_ref, in_ref, high_table, low_table, *outs):
    zhi, column = lax.axis_index("zhi"), lax.axis_index("x")
    value = in_ref[...]
    sub = lax.broadcasted_iota(jnp.int32, (64, 8, 128), 1)
    bent = pltpu.roll(value, 4, 1) * jnp.where(sub < 4, -1.0, 1.0)
    plain = value.reshape(512, 128).T
    bent = bent.reshape(512, 128).T
    for ahead in range(4):
        target = (column + ahead) % 4
        parts = []
        for half in range(2):
            lanes = slice(256 * half, 256 * half + 256)
            turns = (2 * column + half) * (4 * zhi + target) % 8
            cosine, sine = eighth_ref[turns], eighth_ref[8 + turns]
            parts.append(cosine * plain[:, lanes] + sine * bent[:, lanes])
        value = jnp.concatenate(parts, axis=1)
        outs[ahead][...] = dot3(value, high_table[column], low_table[column])


def back(pieces, tables):
    turns = np.arange(8) * (2 * np.pi / 8)
    eighth = np.concatenate([np.cos(turns), np.sin(turns)]).astype(np.float32)
    return pl.pallas_call(
        back_kernel,
        out_shape=(jax.ShapeDtypeStruct((128, 256), f32),) * 4,
        in_specs=[SM, VM, VM, VM],
        out_specs=(VM,) * 4,
        compiler_params=limit(24),
        name="back",
    )(eighth, pieces, *tables)


def final_kernel(a_ref, b_ref, c_ref, d_ref, x_ref, y_ref):
    total = (a_ref[...] + b_ref[...]) + (c_ref[...] + d_ref[...])
    x_ref[...] = total[:ROWS]
    y_ref[...] = total[ROWS:]


def final(pieces):
    shape = jax.ShapeDtypeStruct((ROWS, 256), f32)
    return pl.pallas_call(
        final_kernel,
        out_shape=(shape, shape),
        in_specs=[VM] * 4,
        out_specs=(VM, VM),
        compiler_params=limit(24),
        name="final",
    )(*pieces)


def deliver(pieces):
    return [pieces[0]] + [
        lax.ppermute(pieces[a], "x", [(i, (i + a) % 4) for i in range(4)]) for a in (1, 2, 3)
    ]


def body(density, refine, weight_low, weight_high):
    def swap(array, axes, pairs):
        return lax.ppermute(array, axes, pairs + [(b, a) for a, b in pairs])

    odd = lax.axis_index("x") % 2 == 1
    layer = lax.dynamic_slice_in_dim(density, jnp.where(odd, LAYERS - 1, 0), 1, 0)
    layer = swap(layer, LOS, [(1, 2), (3, 4), (5, 6)])
    row, other_row, other_layer = edge_rows(density)
    other_layer = swap(other_layer, LOS, [(0, 1), (2, 3), (4, 5), (6, 7)])
    row = swap(row, "sky", [(i, i + 1) for i in range(0, SKY, 2)])
    other_row = swap(other_row, "sky", [(i, (i + 1) % SKY) for i in range(1, SKY, 2)])
    inner = inner_sums(weight_low, weight_high, density, refine)
    tables = halves(forward_table())
    summed = outer_sums(
        weight_low, weight_high, density, (layer, other_layer), (row, other_row), inner, tables
    )
    summed = deliver(summed)
    pieces = lax.all_to_all(turn(summed), ("zhi", "sky"), 0, 0, tiled=True)
    pieces = solve(pieces, twists() + halves(row_table()))
    pieces = lax.all_to_all(pieces, ("zhi", "sky"), 0, 0, tiled=True)
    fields = back(pieces, halves(inverse_table()))
    return final(deliver(fields))


def solution(mesh):
    devices = mesh.devices.reshape(2, 4, SKY)
    inner = Mesh(devices, ("zhi", "x", "sky"))
    placed = (P(LOS, "sky", None), P(LOS, "sky", None), P(LOS), P(LOS))
    return jax.shard_map(
        body,
        mesh=inner,
        in_specs=placed,
        out_specs=(P("sky", LOS), P("sky", LOS)),
        check_vma=False,
    )
```

```python
import functools

import jax
import jax.numpy as jnp
import ml_dtypes
import numpy as np
from jax import lax
from jax.experimental import pallas as pl
from jax.experimental.pallas import tpu as pltpu
from jax.sharding import Mesh, PartitionSpec as P

f32 = jnp.float32
bf16 = jnp.bfloat16
N = 2048
ROWS = 64
SKY = 32
LAYERS = 8
LOS = ("zhi", "x")
MB = 1024 * 1024


def halves(table):
    high = table.astype(np.float32).astype(ml_dtypes.bfloat16)
    low = (table - high.astype(np.float64)).astype(np.float32).astype(ml_dtypes.bfloat16)
    return high, low


def tile_modes(tile):
    n = np.arange(128)
    if tile:
        return tile + 16 * n
    return np.where(n < 64, 16 * n, 8 + 16 * (n - 64))


def tile_order(real, imag):
    pair = np.stack([real.reshape(SKY, 4, -1), imag.reshape(SKY, 4, -1)], axis=1)
    return pair.reshape(256, -1)


def forward_table():
    b = np.arange(128)
    tiles = []
    for tile in range(8):
        angle = (tile_modes(tile)[:, None] * b[None, :] % N) * (2 * np.pi / N)
        cosine, sine = np.cos(angle), np.sin(angle)
        if tile:
            real = np.concatenate([cosine, sine], 1)
            imag = np.concatenate([-sine, cosine], 1)
        else:
            zero = np.zeros((64, 128))
            real = np.block([[cosine[:64], zero], [zero, cosine[64:]]])
            imag = np.block([[-sine[:64], zero], [zero, -sine[64:]]])
            imag[0, :128] = (-1.0) ** b
        tiles.append(tile_order(real, imag).T)
    return np.stack(tiles)


def inverse_table():
    j = np.arange(256)
    tiles = []
    for tile in range(8):
        angle = (tile_modes(tile)[:, None] * j[None, :] % N) * (2 * np.pi / N)
        real, imag = 2 * np.cos(angle), -2 * np.sin(angle)
        if not tile:
            real[0] = 1.0
            imag[0] = (-1.0) ** j
        tiles.append(tile_order(real, imag))
    return np.stack(tiles).reshape(4, 512, 256)


def row_table():
    r = np.arange(64)
    angle = (r[:, None] * r[None, :] % 64) * (2 * np.pi / 64)
    both = np.eye(2)
    return np.concatenate([np.kron(both, np.cos(angle)), np.kron(both, np.sin(angle))], 1)


def twists():
    angle = (np.arange(32)[:, None] * (np.arange(128) % 64)[None, :]) * (2 * np.pi / N)
    sign = np.where(np.arange(8) < 4, 1.0, -1.0)
    cosine = np.broadcast_to(np.cos(angle)[:, None, :], (32, 8, 128))
    sine = np.sin(angle)[:, None, :] * sign[None, :, None]
    return cosine.astype(np.float32), sine.astype(np.float32)


def minmod(a, b):
    return jnp.maximum(jnp.minimum(a, b), 0.0) + jnp.minimum(jnp.maximum(a, b), 0.0)


def split(value):
    high = value.astype(bf16)
    return high, (value - high.astype(f32)).astype(bf16)


def dot3(value, high_table, low_table):
    high, low = split(value)
    dot = functools.partial(jnp.dot, preferred_element_type=f32)
    return dot(high, high_table) + (dot(low, high_table) + dot(high, low_table))


def stacked(value):
    return jnp.concatenate(split(value), axis=0)


def dot3_stacked(parts, high_table, low_table):
    rows = parts.shape[0] // 2
    dot = functools.partial(jnp.dot, preferred_element_type=f32)
    both = dot(parts, high_table)
    return both[:rows] + (both[rows:] + dot(parts[:rows], low_table))


def limit(mib):
    return pltpu.CompilerParams(vmem_limit_bytes=mib * MB)


VM = pl.BlockSpec(memory_space=pltpu.VMEM)
SM = pl.BlockSpec(memory_space=pltpu.SMEM)


def rows_kernel(d_ref, near_ref, far_ref, layer_ref):
    layer_ref[0] = jnp.where(lax.axis_index("x") % 2 == 1, d_ref[0], d_ref[LAYERS - 1])
    even = lax.axis_index("sky") % 2 == 0
    for z in range(LAYERS):
        first = d_ref[z, 0:16, :].astype(f32)[0:1]
        last = d_ref[z, 48:64, :].astype(f32)[15:16]
        near_ref[z : z + 1, :] = jnp.where(even, last, first)
        far_ref[z : z + 1, :] = jnp.where(even, first, last)


def edge_rows(density):
    shape = jax.ShapeDtypeStruct((LAYERS, N), f32)
    return pl.pallas_call(
        rows_kernel,
        out_shape=(shape, shape, jax.ShapeDtypeStruct((1, ROWS, N), bf16)),
        in_specs=[VM],
        out_specs=(VM, VM, VM),
        compiler_params=limit(8),
        name="edge_rows",
    )(density)


def longer(field):
    return jnp.concatenate([field, jnp.zeros((8, N), f32)], axis=0)


def smooth_y(field):
    return 0.75 * field + 0.125 * (pltpu.roll(field, 1, 1) + pltpu.roll(field, N - 1, 1))


CHUNK = 512


def inner_kernel(
    low_ref,
    high_ref,
    d_ref,
    refine_ref,
    kappa_ref,
    mask_ref,
    near_ref,
    calm_ref,
    lifted_ref,
    tx_ref,
    ty_ref,
):
    block = lax.broadcasted_iota(jnp.int32, (256, N), 0)
    lane = lax.broadcasted_iota(jnp.int32, (256, N), 1)
    grow = jnp.where(lane // 8 == block, 1.0, 0.0).astype(bf16)
    coarse = refine_ref[0].astype(f32).astype(bf16)
    mask_ref[...] = jnp.dot(coarse, grow, preferred_element_type=f32)
    for z in range(LAYERS):
        first = d_ref[z, 0:16, :].astype(f32)
        last = d_ref[z, 48:64, :].astype(f32)
        near_ref[0, z : z + 1, :] = first[0:1]
        near_ref[1, z : z + 1, :] = first[1:2]
        near_ref[2, z : z + 1, :] = last[14:15]
        near_ref[3, z : z + 1, :] = last[15:16]

    wide = CHUNK + 256
    row = lax.broadcasted_iota(jnp.int32, (ROWS, CHUNK), 0)
    inside = jnp.logical_and(row > 0, row < ROWS - 1)

    def chunk(i, carry):
        start = pl.multiple_of(i * CHUNK, CHUNK)
        left = pl.multiple_of((start + N - 128) % N, 128)
        right = pl.multiple_of((start + CHUNK) % N, 128)
        base = jnp.zeros((ROWS, CHUNK), f32)
        tz, tx, ty = base, base, base
        centre, step = None, None
        for z in range(LAYERS):
            average = 0.5 * (low_ref[z] + high_ref[z])
            former = centre
            around = jnp.concatenate(
                [
                    d_ref[z, :, pl.ds(left, 128)],
                    d_ref[z, :, pl.ds(start, CHUNK)],
                    d_ref[z, :, pl.ds(right, 128)],
                ],
                axis=1,
            ).astype(f32)
            centre = around[:, 128 : 128 + CHUNK]
            base = base + average * centre
            dy = pltpu.roll(around, wide - 1, 1) - around
            gy = minmod(dy, pltpu.roll(dy, 1, 1))[:, 128 : 128 + CHUNK]
            ty = ty + average * gy
            dx = pltpu.roll(centre, ROWS - 1, 0) - centre
            tx = tx + average * minmod(dx, pltpu.roll(dx, 1, 0))
            if z > 0:
                latter = centre - former
                if step is not None:
                    slope = 0.125 * (high_ref[z - 1] - low_ref[z - 1])
                    tz = tz + slope * minmod(latter, step)
                step = latter
        marked = mask_ref[:, pl.ds(start, CHUNK)]
        marked = jnp.broadcast_to(marked[:, None, :], (8, 8, CHUNK)).reshape(ROWS, CHUNK)
        at = pl.ds(start, CHUNK)
        calm_ref[:, at] = base - marked * base
        lifted_ref[:, at] = marked * (base + tz)
        tx_ref[:, at] = jnp.where(inside, marked * tx, 0.0)
        ty_ref[:, at] = marked * ty
        return carry

    lax.fori_loop(0, N // CHUNK, chunk, 0)
    lifted, tx = lifted_ref[...], tx_ref[...]
    eighth, tilt = 0.125 * lifted, ty_ref[...] * (1.0 / 32.0)
    smooth = 0.75 * lifted + pltpu.roll(eighth + tilt, 1, 1) + pltpu.roll(eighth - tilt, N - 1, 1)
    eighth, tilt = 0.125 * smooth, smooth_y(tx) * (1.0 / 32.0)
    kappa_ref[...] = (
        longer(calm_ref[...] + 0.75 * smooth)
        + pltpu.roll(longer(eighth + tilt), 1, 0)
        + pltpu.roll(longer(eighth - tilt), ROWS + 7, 0)
    )


def inner_sums(low, high, density, refine):
    return pl.pallas_call(
        inner_kernel,
        out_shape=(
            jax.ShapeDtypeStruct((ROWS + 8, N), f32),
            jax.ShapeDtypeStruct((8, N), f32),
            jax.ShapeDtypeStruct((4, LAYERS, N), f32),
        ),
        in_specs=[SM, SM, VM, VM],
        out_specs=(VM,) * 3,
        scratch_shapes=[pltpu.VMEM((ROWS, N), f32)] * 4,
        compiler_params=limit(40),
        cost_estimate=pl.CostEstimate(flops=40_000_000, bytes_accessed=24 * MB, transcendentals=0),
        name="inner_sums",
    )(low, high, density, refine)


def outer_kernel(
    low_ref,
    high_ref,
    d_ref,
    layer_ref,
    other_layer_ref,
    row_ref,
    other_row_ref,
    kappa_ref,
    mask_ref,
    near_ref,
    high_table,
    low_table,
    far_ref,
    next_ref,
    last_ref,
    part_ref,
):
    los = lax.axis_index("zhi") * 4 + lax.axis_index("x")
    v0, v1 = d_ref[0].astype(f32), d_ref[1].astype(f32)
    v6, v7 = d_ref[6].astype(f32), d_ref[7].astype(f32)
    odd = los % 2 == 1
    one, other = layer_ref[0].astype(f32), other_layer_ref[0].astype(f32)
    below = jnp.where(los == 0, v0, jnp.where(odd, other, one))
    above = jnp.where(los == 7, v7, jnp.where(odd, one, other))
    slope0 = 0.125 * (high_ref[0] - low_ref[0])
    slope7 = 0.125 * (high_ref[7] - low_ref[7])
    tz = slope0 * minmod(v1 - v0, v0 - below) + slope7 * minmod(above - v7, v7 - v6)
    mask = mask_ref[...]
    marked = jnp.broadcast_to(mask[:, None, :], (8, 8, N)).reshape(ROWS, N)
    smooth = smooth_y(marked * tz)
    layer = lax.broadcasted_iota(jnp.int32, (LAYERS, 1), 0)
    average = jnp.zeros((LAYERS, 1), f32)
    for z in range(LAYERS):
        average = jnp.where(layer == z, 0.5 * (low_ref[z] + high_ref[z]), average)
    r0, r1, r62, r63 = near_ref[0], near_ref[1], near_ref[2], near_ref[3]
    even = lax.axis_index("sky") % 2 == 0
    before = jnp.where(even, other_row_ref[...], row_ref[...])
    after = jnp.where(even, row_ref[...], other_row_ref[...])
    e0 = jnp.sum(average * minmod(r1 - r0, r0 - before), axis=0, keepdims=True)
    e63 = jnp.sum(average * minmod(after - r63, r63 - r62), axis=0, keepdims=True)
    row = lax.broadcasted_iota(jnp.int32, (8, N), 0)
    e0 = smooth_y(jnp.where(row == 0, mask[0:1] * e0, 0.0)) * (1.0 / 32.0)
    e63 = smooth_y(jnp.where(row == 7, mask[7:8] * e63, 0.0)) * (1.0 / 32.0)
    first = pltpu.roll(e0, 1, 0)
    last = pltpu.roll(e63, 7, 0)
    spill = jnp.where(row == 0, pltpu.roll(e63, 1, 0), -pltpu.roll(e0, 7, 0))
    sides = jnp.concatenate([first, jnp.zeros((ROWS - 16, N), f32), -last, spill], axis=0)
    eighth = longer(0.125 * smooth)
    kappa = (
        (kappa_ref[...] + sides)
        + longer(0.75 * smooth)
        + (pltpu.roll(eighth, 1, 0) + pltpu.roll(eighth, ROWS + 7, 0))
    )
    part = [kappa[:, 128 * a : 128 * a + 128] for a in range(16)]
    even = [part[a] + part[16 - a] for a in range(1, 8)]
    odd = [part[a] - part[16 - a] for a in range(1, 8)]

    def weigh(pairs):
        total = None
        for factor, value in pairs:
            if abs(factor) < 1e-9:
                continue
            term = value if abs(factor - 1) < 1e-9 else factor * value
            total = term if total is None else total + term
        return total

    def cosines(k):
        first = part[0] + part[8] if k % 2 == 0 else part[0] - part[8]
        return first + weigh((float(np.cos(np.pi * k * a / 8)), even[a - 1]) for a in range(1, 8))

    def sines(k):
        return weigh((float(-np.sin(np.pi * k * a / 8)), odd[a - 1]) for a in range(1, 8))

    for tile in range(8):
        second = sines(tile) if tile else cosines(8)
        value = jnp.concatenate([cosines(tile), second], axis=1)
        value = jnp.concatenate([value, jnp.zeros((8, 256), f32)], axis=0)
        part_ref[tile] = stacked(value)
    transform_for(2, part_ref, high_table, low_table, far_ref)
    transform_for(1, part_ref, high_table, low_table, next_ref)
    transform_for(3, part_ref, high_table, low_table, last_ref)


def transform_for(ahead, part_ref, high_table, low_table, out_ref):
    target = (lax.axis_index("x") + ahead) % 4
    for half in range(2):
        tile = 2 * target + half
        value = dot3_stacked(part_ref[tile], high_table[tile], low_table[tile])
        out_ref[:, 256 * half : 256 * half + 256] = value[:72]


def rest_kernel(part_ref, high_table, low_table, own_ref):
    transform_for(0, part_ref, high_table, low_table, own_ref)


def outer_sums(low, high, density, layers, rows, inner, tables):
    piece = jax.ShapeDtypeStruct((72, 512), f32)
    two, one, three, parts = pl.pallas_call(
        outer_kernel,
        out_shape=(piece, piece, piece, jax.ShapeDtypeStruct((8, 160, 256), bf16)),
        in_specs=[SM, SM] + [VM] * 10,
        out_specs=(VM,) * 4,
        compiler_params=limit(32),
        name="outer_sums",
    )(low, high, density, *layers, *rows, *inner, *tables)
    own = pl.pallas_call(
        rest_kernel,
        out_shape=piece,
        in_specs=[VM] * 3,
        out_specs=VM,
        compiler_params=limit(24),
        name="other_sums",
    )(parts, *tables)
    return own, one, two, three


def turn_kernel(a_ref, b_ref, c_ref, d_ref, out_ref):
    total = (a_ref[...] + b_ref[...]) + (c_ref[...] + d_ref[...])
    total = jnp.concatenate([total, jnp.zeros((56, 512), f32)], axis=0)
    out_ref[...] = total.T.reshape(64, 8, 128)


def turn(pieces):
    return pl.pallas_call(
        turn_kernel,
        out_shape=jax.ShapeDtypeStruct((64, 8, 128), f32),
        in_specs=[VM] * 4,
        out_specs=VM,
        compiler_params=limit(24),
        name="turn",
    )(*pieces)


def dft_32(values):
    even = [values[s] + values[32 - s] for s in range(1, 16)]
    odd = [values[s] - values[32 - s] for s in range(1, 16)]
    ends = [values[0] + values[16], values[0] - values[16]]
    cosine, sine = [None] * 17, [None] * 17
    for k in range(9):
        plain = ends[k % 2]
        turned = None
        for s in range(1, 16):
            term = float(np.cos(np.pi * k * s / 16)) * even[s - 1]
            if s % 2 == 0:
                plain = plain + term
            else:
                turned = term if turned is None else turned + term
        cosine[k] = plain + turned
        cosine[16 - k] = plain - turned
    for k in range(1, 9):
        plain, turned = None, None
        for s in range(1, 16):
            term = float(np.sin(np.pi * k * s / 16)) * odd[s - 1]
            if s % 2 == 0:
                plain = term if plain is None else plain + term
            else:
                turned = term if turned is None else turned + term
        sine[k] = turned + plain
        sine[16 - k] = turned - plain
    return cosine, sine


def solve_kernel(in_ref, cos_ref, sin_ref, high_table, low_table, out_ref):
    sky = lax.axis_index("sky")
    tile = 2 * lax.axis_index("x") + lax.axis_index("zhi")
    lane = lax.broadcasted_iota(jnp.int32, (8, 128), 1)
    sub = lax.broadcasted_iota(jnp.int32, (8, 128), 0)
    lower = lane < 64
    sign = jnp.where(sub < 4, 1.0, -1.0)
    first = jnp.logical_and(tile == 0, sky == 0)
    packed = jnp.logical_and(sub % 4 == 0, first)

    def swap(v):
        return pltpu.roll(v, 4, v.ndim - 2)

    def bent(v):
        return swap(v) * sign

    total = [in_ref[s] + in_ref[SKY + s] for s in range(SKY)]
    values = []
    for s in range(SKY):
        up = pltpu.roll(total[(s - 1) % SKY], 64, 1)
        down = pltpu.roll(total[(s + 1) % SKY], 120, 1)
        v = total[s] + jnp.where(lane == 0, up, jnp.where(lane == 63, down, 0.0))
        v = jnp.where(lower, v, pltpu.roll(v, 64, 1))
        apart = jnp.where(sub == 4, 0.0, jnp.where(lower, v, swap(v)))
        values.append(jnp.where(packed, apart, v))
    cosine, sine = dft_32(values)
    spectrum = [None] * 32
    spectrum[0], spectrum[16] = cosine[0], cosine[16]
    for k in range(1, 16):
        turned = bent(sine[k])
        spectrum[k], spectrum[32 - k] = cosine[k] + turned, cosine[k] - turned
    twisted = [spectrum[k] * cos_ref[k] + swap(spectrum[k]) * sin_ref[k] for k in range(32)]
    rows = jnp.concatenate(twisted, axis=0)
    pair = dot3(rows, high_table[...], low_table[...])
    pair_c = pair[:, :128].reshape(32, 8, 128)
    pair_s = pair[:, 128:].reshape(32, 8, 128)

    k1 = lax.broadcasted_iota(jnp.int32, (32, 8, 128), 0)
    k2 = lax.broadcasted_iota(jnp.int32, (32, 8, 128), 2) % 64
    nx = k1 + 32 * k2
    nx = jnp.where(nx < N // 2, nx, nx - N)
    n = 4 * sky + sub % 4
    ny = jnp.where(tile > 0, tile + 16 * n, jnp.where(n < 64, 16 * n, 8 + 16 * (n - 64)))
    ny = jnp.where(ny < N // 2, ny, ny - N)
    ny = jnp.where(jnp.logical_and(packed, jnp.logical_not(lower)), -(N // 2), ny)
    along_x = jnp.logical_or(packed, lower)[None]
    squared = nx * nx + (ny * ny)[None]
    wave = jnp.where(along_x, jnp.where(nx == -(N // 2), 0, nx), ny[None])
    unit = 2.0 * np.pi / N
    scale = float(-2.0 / unit / 64.0 / N / N)
    factor = scale * wave.astype(f32) / jnp.maximum(squared, 1).astype(f32)
    kappa_hat = pair_c + swap(pair_s) * sign[None]
    field = factor * (swap(kappa_hat) * (-sign)[None])
    pair = dot3(field.reshape(256, 128), high_table[...], low_table[...])
    values = []
    for k in range(32):
        v = pair[8 * k : 8 * k + 8, :128] - bent(pair[8 * k : 8 * k + 8, 128:])
        values.append(v * cos_ref[k] - swap(v) * sin_ref[k])
    cosine, sine = dft_32(values)
    for s in range(17):
        turned = bent(sine[s]) if 0 < s < 16 else None
        for at in (s,) if turned is None else (s, 32 - s):
            v = cosine[s]
            if turned is not None:
                v = v - turned if at == s else v + turned
            other = swap(pltpu.roll(v, 64, 1))
            joined = jnp.where(lower, jnp.where(sub == 4, other, v), 0.0)
            v = jnp.where(packed, joined, v)
            out_ref[at] = v
            out_ref[SKY + at] = v


def solve(pieces, tables):
    return pl.pallas_call(
        solve_kernel,
        out_shape=jax.ShapeDtypeStruct((64, 8, 128), f32),
        in_specs=[VM] * 5,
        out_specs=VM,
        compiler_params=limit(24),
        name="solve",
    )(pieces, *tables)


def back_for(ahead, eighth_ref, plain, bent, high_table, low_table, out_ref):
    zhi, column = lax.axis_index("zhi"), lax.axis_index("x")
    target = (column + ahead) % 4
    parts = []
    for half in range(2):
        lanes = slice(256 * half, 256 * half + 256)
        turns = (2 * column + half) * (4 * zhi + target) % 8
        cosine, sine = eighth_ref[turns], eighth_ref[8 + turns]
        parts.append(cosine * plain[:, lanes] + sine * bent[:, lanes])
    value = stacked(jnp.concatenate(parts, axis=1))
    out_ref[...] = dot3_stacked(value, high_table[column], low_table[column])


def back_kernel(
    eighth_ref, in_ref, high_table, low_table, far_ref, next_ref, last_ref, plain_ref, bent_ref
):
    value = in_ref[...]
    sub = lax.broadcasted_iota(jnp.int32, (64, 8, 128), 1)
    bent = pltpu.roll(value, 4, 1) * jnp.where(sub < 4, -1.0, 1.0)
    plain, bent = value.reshape(512, 128).T, bent.reshape(512, 128).T
    plain_ref[...] = plain
    bent_ref[...] = bent
    back_for(2, eighth_ref, plain, bent, high_table, low_table, far_ref)
    back_for(1, eighth_ref, plain, bent, high_table, low_table, next_ref)
    back_for(3, eighth_ref, plain, bent, high_table, low_table, last_ref)


def back_rest_kernel(eighth_ref, plain_ref, bent_ref, high_table, low_table, own_ref):
    back_for(0, eighth_ref, plain_ref[...], bent_ref[...], high_table, low_table, own_ref)


def back(pieces, tables):
    turns = np.arange(8) * (2 * np.pi / 8)
    eighth = np.concatenate([np.cos(turns), np.sin(turns)]).astype(np.float32)
    piece = jax.ShapeDtypeStruct((128, 256), f32)
    held = jax.ShapeDtypeStruct((128, 512), f32)
    two, one, three, plain, bent = pl.pallas_call(
        back_kernel,
        out_shape=(piece, piece, piece, held, held),
        in_specs=[SM, VM, VM, VM],
        out_specs=(VM,) * 5,
        compiler_params=limit(24),
        name="back",
    )(eighth, pieces, *tables)
    own = pl.pallas_call(
        back_rest_kernel,
        out_shape=piece,
        in_specs=[SM] + [VM] * 4,
        out_specs=VM,
        compiler_params=limit(24),
        name="back_rest",
    )(eighth, plain, bent, *tables)
    return own, one, two, three


def final_kernel(a_ref, b_ref, c_ref, d_ref, x_ref, y_ref):
    total = (a_ref[...] + b_ref[...]) + (c_ref[...] + d_ref[...])
    x_ref[...] = total[:ROWS]
    y_ref[...] = total[ROWS:]


def final(pieces):
    shape = jax.ShapeDtypeStruct((ROWS, 256), f32)
    return pl.pallas_call(
        final_kernel,
        out_shape=(shape, shape),
        in_specs=[VM] * 4,
        out_specs=(VM, VM),
        compiler_params=limit(24),
        name="final",
    )(*pieces)


def deliver(pieces):
    return [pieces[0]] + [
        lax.ppermute(pieces[a], "x", [(i, (i + a) % 4) for i in range(4)]) for a in (2, 1, 3)
    ]


def body(density, refine, weight_low, weight_high):
    def swap(array, axes, pairs):
        return lax.ppermute(array, axes, pairs + [(b, a) for a, b in pairs])

    odd = lax.axis_index("x") % 2 == 1
    layer = lax.dynamic_slice_in_dim(density, jnp.where(odd, LAYERS - 1, 0), 1, 0)
    layer = swap(layer, LOS, [(1, 2), (3, 4), (5, 6)])
    row, other_row, other_layer = edge_rows(density)
    other_layer = swap(other_layer, LOS, [(0, 1), (2, 3), (4, 5), (6, 7)])
    row = swap(row, "sky", [(i, i + 1) for i in range(0, SKY, 2)])
    other_row = swap(other_row, "sky", [(i, (i + 1) % SKY) for i in range(1, SKY, 2)])
    inner = inner_sums(weight_low, weight_high, density, refine)
    tables = halves(forward_table())
    summed = outer_sums(
        weight_low, weight_high, density, (layer, other_layer), (row, other_row), inner, tables
    )
    summed = deliver(summed)
    pieces = lax.all_to_all(turn(summed), ("zhi", "sky"), 0, 0, tiled=True)
    pieces = solve(pieces, twists() + halves(row_table()))
    pieces = lax.all_to_all(pieces, ("zhi", "sky"), 0, 0, tiled=True)
    fields = back(pieces, halves(inverse_table()))
    return final(deliver(fields))


def solution(mesh):
    devices = mesh.devices.reshape(2, 4, SKY)
    inner = Mesh(devices, ("zhi", "x", "sky"))
    placed = (P(LOS, "sky", None), P(LOS, "sky", None), P(LOS), P(LOS))
    return jax.shard_map(
        body,
        mesh=inner,
        in_specs=placed,
        out_specs=(P("sky", LOS), P("sky", LOS)),
        check_vma=False,
    )
```

```python
import functools

import jax
import jax.numpy as jnp
import ml_dtypes
import numpy as np
from jax import lax
from jax.experimental import pallas as pl
from jax.experimental.pallas import tpu as pltpu
from jax.sharding import Mesh, PartitionSpec as P

f32 = jnp.float32
bf16 = jnp.bfloat16
N = 2048
ROWS = 64
SKY = 32
LAYERS = 8
LOS = ("zhi", "x")
MB = 1024 * 1024


def halves(table):
    high = table.astype(np.float32).astype(ml_dtypes.bfloat16)
    low = (table - high.astype(np.float64)).astype(np.float32).astype(ml_dtypes.bfloat16)
    return high, low


def tile_modes(tile):
    n = np.arange(128)
    if tile:
        return tile + 16 * n
    return np.where(n < 64, 16 * n, 8 + 16 * (n - 64))


def tile_order(real, imag):
    pair = np.stack([real.reshape(SKY, 4, -1), imag.reshape(SKY, 4, -1)], axis=1)
    return pair.reshape(256, -1)


def tile_groups(real, imag):
    pair = np.stack([real.reshape(SKY, 4, -1), imag.reshape(SKY, 4, -1)], axis=1)
    return pair.transpose(2, 1, 0, 3).reshape(256, -1)


def forward_table():
    b = np.arange(128)
    tiles = []
    for tile in range(8):
        angle = (tile_modes(tile)[:, None] * b[None, :] % N) * (2 * np.pi / N)
        cosine, sine = np.cos(angle), np.sin(angle)
        if tile:
            real = np.concatenate([cosine, sine], 1)
            imag = np.concatenate([-sine, cosine], 1)
        else:
            zero = np.zeros((64, 128))
            real = np.block([[cosine[:64], zero], [zero, cosine[64:]]])
            imag = np.block([[-sine[:64], zero], [zero, -sine[64:]]])
            imag[0, :128] = (-1.0) ** b
        tiles.append(tile_groups(real, imag).T)
    return np.stack(tiles)


def inverse_table():
    j = np.arange(256)
    tiles = []
    for tile in range(8):
        angle = (tile_modes(tile)[:, None] * j[None, :] % N) * (2 * np.pi / N)
        real, imag = 2 * np.cos(angle), -2 * np.sin(angle)
        if not tile:
            real[0] = 1.0
            imag[0] = (-1.0) ** j
        tiles.append(tile_order(real, imag))
    return np.stack(tiles).reshape(4, 512, 256)


def row_table():
    r = np.arange(64)
    angle = (r[:, None] * r[None, :] % 64) * (2 * np.pi / 64)
    both = np.eye(2)
    return np.concatenate([np.kron(both, np.cos(angle)), np.kron(both, np.sin(angle))], 1)


def twists():
    angle = (np.arange(32)[:, None] * (np.arange(128) % 64)[None, :]) * (2 * np.pi / N)
    sign = np.where(np.arange(8) < 4, 1.0, -1.0)
    cosine = np.broadcast_to(np.cos(angle)[:, None, :], (32, 8, 128))
    sine = np.sin(angle)[:, None, :] * sign[None, :, None]
    return cosine.astype(np.float32), sine.astype(np.float32)


def minmod(a, b):
    return jnp.maximum(jnp.minimum(a, b), 0.0) + jnp.minimum(jnp.maximum(a, b), 0.0)


def split(value):
    high = value.astype(bf16)
    return high, (value - high.astype(f32)).astype(bf16)


def dot3(value, high_table, low_table):
    high, low = split(value)
    dot = functools.partial(jnp.dot, preferred_element_type=f32)
    return dot(high, high_table) + (dot(low, high_table) + dot(high, low_table))


def stacked(value):
    return jnp.concatenate(split(value), axis=0)


def dot3_stacked(parts, high_table, low_table):
    rows = parts.shape[0] // 2
    dot = functools.partial(jnp.dot, preferred_element_type=f32)
    both = dot(parts, high_table)
    return both[:rows] + (both[rows:] + dot(parts[:rows], low_table))


def limit(mib):
    return pltpu.CompilerParams(vmem_limit_bytes=mib * MB)


VM = pl.BlockSpec(memory_space=pltpu.VMEM)
SM = pl.BlockSpec(memory_space=pltpu.SMEM)


def rows_kernel(d_ref, near_ref, far_ref, layer_ref):
    layer_ref[0] = jnp.where(lax.axis_index("x") % 2 == 1, d_ref[0], d_ref[LAYERS - 1])
    even = lax.axis_index("sky") % 2 == 0
    for z in range(LAYERS):
        first = d_ref[z, 0:16, :].astype(f32)[0:1]
        last = d_ref[z, 48:64, :].astype(f32)[15:16]
        near_ref[z : z + 1, :] = jnp.where(even, last, first)
        far_ref[z : z + 1, :] = jnp.where(even, first, last)


def edge_rows(density):
    shape = jax.ShapeDtypeStruct((LAYERS, N), f32)
    return pl.pallas_call(
        rows_kernel,
        out_shape=(shape, shape, jax.ShapeDtypeStruct((1, ROWS, N), bf16)),
        in_specs=[VM],
        out_specs=(VM, VM, VM),
        compiler_params=limit(8),
        name="edge_rows",
    )(density)


def longer(field):
    return jnp.concatenate([field, jnp.zeros((8, N), f32)], axis=0)


def smooth_y(field):
    return 0.75 * field + 0.125 * (pltpu.roll(field, 1, 1) + pltpu.roll(field, N - 1, 1))


CHUNK = 512


def inner_kernel(
    low_ref,
    high_ref,
    d_ref,
    refine_ref,
    kappa_ref,
    mask_ref,
    near_ref,
    calm_ref,
    lifted_ref,
    tx_ref,
    ty_ref,
):
    block = lax.broadcasted_iota(jnp.int32, (256, N), 0)
    lane = lax.broadcasted_iota(jnp.int32, (256, N), 1)
    grow = jnp.where(lane // 8 == block, 1.0, 0.0).astype(bf16)
    coarse = refine_ref[0].astype(f32).astype(bf16)
    mask_ref[...] = jnp.dot(coarse, grow, preferred_element_type=f32)
    for z in range(LAYERS):
        first = d_ref[z, 0:16, :].astype(f32)
        last = d_ref[z, 48:64, :].astype(f32)
        near_ref[0, z : z + 1, :] = first[0:1]
        near_ref[1, z : z + 1, :] = first[1:2]
        near_ref[2, z : z + 1, :] = last[14:15]
        near_ref[3, z : z + 1, :] = last[15:16]

    wide = CHUNK + 256
    row = lax.broadcasted_iota(jnp.int32, (ROWS, CHUNK), 0)
    inside = jnp.logical_and(row > 0, row < ROWS - 1)

    def chunk(i, carry):
        start = pl.multiple_of(i * CHUNK, CHUNK)
        left = pl.multiple_of((start + N - 128) % N, 128)
        right = pl.multiple_of((start + CHUNK) % N, 128)
        base = jnp.zeros((ROWS, CHUNK), f32)
        tz, tx, ty = base, base, base
        centre, step = None, None
        for z in range(LAYERS):
            average = 0.5 * (low_ref[z] + high_ref[z])
            former = centre
            around = jnp.concatenate(
                [
                    d_ref[z, :, pl.ds(left, 128)],
                    d_ref[z, :, pl.ds(start, CHUNK)],
                    d_ref[z, :, pl.ds(right, 128)],
                ],
                axis=1,
            ).astype(f32)
            centre = around[:, 128 : 128 + CHUNK]
            base = base + average * centre
            dy = pltpu.roll(around, wide - 1, 1) - around
            gy = minmod(dy, pltpu.roll(dy, 1, 1))[:, 128 : 128 + CHUNK]
            ty = ty + average * gy
            dx = pltpu.roll(centre, ROWS - 1, 0) - centre
            tx = tx + average * minmod(dx, pltpu.roll(dx, 1, 0))
            if z > 0:
                latter = centre - former
                if step is not None:
                    slope = 0.125 * (high_ref[z - 1] - low_ref[z - 1])
                    tz = tz + slope * minmod(latter, step)
                step = latter
        marked = mask_ref[:, pl.ds(start, CHUNK)]
        marked = jnp.broadcast_to(marked[:, None, :], (8, 8, CHUNK)).reshape(ROWS, CHUNK)
        at = pl.ds(start, CHUNK)
        calm_ref[:, at] = base - marked * base
        lifted_ref[:, at] = marked * (base + tz)
        tx_ref[:, at] = jnp.where(inside, marked * tx, 0.0)
        ty_ref[:, at] = marked * ty
        return carry

    lax.fori_loop(0, N // CHUNK, chunk, 0)
    lifted, tx = lifted_ref[...], tx_ref[...]
    eighth, tilt = 0.125 * lifted, ty_ref[...] * (1.0 / 32.0)
    smooth = 0.75 * lifted + pltpu.roll(eighth + tilt, 1, 1) + pltpu.roll(eighth - tilt, N - 1, 1)
    eighth, tilt = 0.125 * smooth, smooth_y(tx) * (1.0 / 32.0)
    kappa_ref[...] = (
        longer(calm_ref[...] + 0.75 * smooth)
        + pltpu.roll(longer(eighth + tilt), 1, 0)
        + pltpu.roll(longer(eighth - tilt), ROWS + 7, 0)
    )


def inner_sums(low, high, density, refine):
    return pl.pallas_call(
        inner_kernel,
        out_shape=(
            jax.ShapeDtypeStruct((ROWS + 8, N), f32),
            jax.ShapeDtypeStruct((8, N), f32),
            jax.ShapeDtypeStruct((4, LAYERS, N), f32),
        ),
        in_specs=[SM, SM, VM, VM],
        out_specs=(VM,) * 3,
        scratch_shapes=[pltpu.VMEM((ROWS, N), f32)] * 4,
        compiler_params=limit(40),
        cost_estimate=pl.CostEstimate(flops=40_000_000, bytes_accessed=24 * MB, transcendentals=0),
        name="inner_sums",
    )(low, high, density, refine)


def outer_kernel(
    low_ref,
    high_ref,
    d_ref,
    layer_ref,
    other_layer_ref,
    row_ref,
    other_row_ref,
    kappa_ref,
    mask_ref,
    near_ref,
    high_table,
    low_table,
    far_ref,
    next_ref,
    last_ref,
    part_ref,
):
    los = lax.axis_index("zhi") * 4 + lax.axis_index("x")
    v0, v1 = d_ref[0].astype(f32), d_ref[1].astype(f32)
    v6, v7 = d_ref[6].astype(f32), d_ref[7].astype(f32)
    odd = los % 2 == 1
    one, other = layer_ref[0].astype(f32), other_layer_ref[0].astype(f32)
    below = jnp.where(los == 0, v0, jnp.where(odd, other, one))
    above = jnp.where(los == 7, v7, jnp.where(odd, one, other))
    slope0 = 0.125 * (high_ref[0] - low_ref[0])
    slope7 = 0.125 * (high_ref[7] - low_ref[7])
    tz = slope0 * minmod(v1 - v0, v0 - below) + slope7 * minmod(above - v7, v7 - v6)
    mask = mask_ref[...]
    marked = jnp.broadcast_to(mask[:, None, :], (8, 8, N)).reshape(ROWS, N)
    smooth = smooth_y(marked * tz)
    layer = lax.broadcasted_iota(jnp.int32, (LAYERS, 1), 0)
    average = jnp.zeros((LAYERS, 1), f32)
    for z in range(LAYERS):
        average = jnp.where(layer == z, 0.5 * (low_ref[z] + high_ref[z]), average)
    r0, r1, r62, r63 = near_ref[0], near_ref[1], near_ref[2], near_ref[3]
    even = lax.axis_index("sky") % 2 == 0
    before = jnp.where(even, other_row_ref[...], row_ref[...])
    after = jnp.where(even, row_ref[...], other_row_ref[...])
    e0 = jnp.sum(average * minmod(r1 - r0, r0 - before), axis=0, keepdims=True)
    e63 = jnp.sum(average * minmod(after - r63, r63 - r62), axis=0, keepdims=True)
    row = lax.broadcasted_iota(jnp.int32, (8, N), 0)
    e0 = smooth_y(jnp.where(row == 0, mask[0:1] * e0, 0.0)) * (1.0 / 32.0)
    e63 = smooth_y(jnp.where(row == 7, mask[7:8] * e63, 0.0)) * (1.0 / 32.0)
    first = pltpu.roll(e0, 1, 0)
    last = pltpu.roll(e63, 7, 0)
    spill = jnp.where(row == 0, pltpu.roll(e63, 1, 0), -pltpu.roll(e0, 7, 0))
    sides = jnp.concatenate([first, jnp.zeros((ROWS - 16, N), f32), -last, spill], axis=0)
    eighth = longer(0.125 * smooth)
    kappa = (
        (kappa_ref[...] + sides)
        + longer(0.75 * smooth)
        + (pltpu.roll(eighth, 1, 0) + pltpu.roll(eighth, ROWS + 7, 0))
    )
    part = [kappa[:, 128 * a : 128 * a + 128] for a in range(16)]
    even = [part[a] + part[16 - a] for a in range(1, 8)]
    odd = [part[a] - part[16 - a] for a in range(1, 8)]

    def weigh(pairs):
        total = None
        for factor, value in pairs:
            if abs(factor) < 1e-9:
                continue
            term = value if abs(factor - 1) < 1e-9 else factor * value
            total = term if total is None else total + term
        return total

    def cosines(k):
        first = part[0] + part[8] if k % 2 == 0 else part[0] - part[8]
        return first + weigh((float(np.cos(np.pi * k * a / 8)), even[a - 1]) for a in range(1, 8))

    def sines(k):
        return weigh((float(-np.sin(np.pi * k * a / 8)), odd[a - 1]) for a in range(1, 8))

    for tile in range(8):
        second = sines(tile) if tile else cosines(8)
        value = jnp.concatenate([cosines(tile), second], axis=1)
        value = jnp.concatenate([value, jnp.zeros((8, 256), f32)], axis=0)
        part_ref[tile] = stacked(value)
    transform_for(2, part_ref, high_table, low_table, far_ref)
    transform_for(1, part_ref, high_table, low_table, next_ref)
    transform_for(3, part_ref, high_table, low_table, last_ref)


def transform_for(ahead, part_ref, high_table, low_table, out_ref):
    target = (lax.axis_index("x") + ahead) % 4
    for half in range(2):
        tile = 2 * target + half
        value = dot3_stacked(part_ref[tile], high_table[tile], low_table[tile])
        out_ref[:, 256 * half : 256 * half + 256] = value[:72]


def rest_kernel(part_ref, high_table, low_table, own_ref):
    transform_for(0, part_ref, high_table, low_table, own_ref)


def outer_sums(low, high, density, layers, rows, inner, tables):
    piece = jax.ShapeDtypeStruct((72, 512), f32)
    two, one, three, parts = pl.pallas_call(
        outer_kernel,
        out_shape=(piece, piece, piece, jax.ShapeDtypeStruct((8, 160, 256), bf16)),
        in_specs=[SM, SM] + [VM] * 10,
        out_specs=(VM,) * 4,
        compiler_params=limit(32),
        name="outer_sums",
    )(low, high, density, *layers, *rows, *inner, *tables)
    own = pl.pallas_call(
        rest_kernel,
        out_shape=piece,
        in_specs=[VM] * 3,
        out_specs=VM,
        compiler_params=limit(24),
        name="other_sums",
    )(parts, *tables)
    return own, one, two, three


def turn_kernel(a_ref, b_ref, c_ref, d_ref, out_ref):
    total = (a_ref[...] + b_ref[...]) + (c_ref[...] + d_ref[...])
    turned = jnp.concatenate([total, jnp.zeros((56, 512), f32)], axis=0).T
    lane = lax.broadcasted_iota(jnp.int32, (SKY, 128), 1)
    for half in range(2):
        at = slice(SKY * half, SKY * half + SKY)
        spill = jnp.zeros((SKY, 128), f32)
        for c in range(4):
            first = 256 * half + 64 * c
            real, imag = turned[first : first + SKY], turned[first + SKY : first + 2 * SKY]
            out_ref[at, 0, 128 * c : 128 * c + 128] = jnp.where(
                lane < 64, real, pltpu.roll(imag, 64, 1)
            )
            for sub, part in ((c, real), (4 + c, imag)):
                up = (128 - 16 * sub) % 128
                down = (up + 63) % 128
                spill = jnp.where(lane == up, pltpu.roll(part, (up - 64) % 128, 1), spill)
                spill = jnp.where(lane == down, pltpu.roll(part, (down - 71) % 128, 1), spill)
        out_ref[at, 0, 512:640] = spill


def turn(pieces):
    return pl.pallas_call(
        turn_kernel,
        out_shape=jax.ShapeDtypeStruct((64, 1, 640), f32),
        in_specs=[VM] * 4,
        out_specs=VM,
        compiler_params=limit(24),
        name="turn",
    )(*pieces)


def dft_32(values):
    even = [values[s] + values[32 - s] for s in range(1, 16)]
    odd = [values[s] - values[32 - s] for s in range(1, 16)]
    ends = [values[0] + values[16], values[0] - values[16]]
    cosine, sine = [None] * 17, [None] * 17
    for k in range(9):
        plain = ends[k % 2]
        turned = None
        for s in range(1, 16):
            term = float(np.cos(np.pi * k * s / 16)) * even[s - 1]
            if s % 2 == 0:
                plain = plain + term
            else:
                turned = term if turned is None else turned + term
        cosine[k] = plain + turned
        cosine[16 - k] = plain - turned
    for k in range(1, 9):
        plain, turned = None, None
        for s in range(1, 16):
            term = float(np.sin(np.pi * k * s / 16)) * odd[s - 1]
            if s % 2 == 0:
                plain = term if plain is None else plain + term
            else:
                turned = term if turned is None else turned + term
        sine[k] = turned + plain
        sine[16 - k] = turned - plain
    return cosine, sine


def solve_kernel(in_ref, cos_ref, sin_ref, high_table, low_table, out_ref):
    sky = lax.axis_index("sky")
    tile = 2 * lax.axis_index("x") + lax.axis_index("zhi")
    lane = lax.broadcasted_iota(jnp.int32, (8, 128), 1)
    sub = lax.broadcasted_iota(jnp.int32, (8, 128), 0)
    lower = lane < 64
    sign = jnp.where(sub < 4, 1.0, -1.0)
    first = jnp.logical_and(tile == 0, sky == 0)
    packed = jnp.logical_and(sub % 4 == 0, first)

    def swap(v):
        return pltpu.roll(v, 4, v.ndim - 2)

    def bent(v):
        return swap(v) * sign

    main, spill = [], []
    for s in range(SKY):
        rows = [
            jnp.broadcast_to(in_ref[s, :, lanes] + in_ref[SKY + s, :, lanes], (8, 128))
            for lanes in (slice(128 * c, 128 * c + 128) for c in range(5))
        ]
        v = rows[3]
        for c in range(3):
            v = jnp.where(sub % 4 == c, rows[c], v)
        main.append(jnp.where(sub < 4, v, pltpu.roll(v, 64, 1)))
        spill.append(pltpu.roll(rows[4], 0, 1, stride=16, stride_axis=0))
    values = []
    for s in range(SKY):
        up, down = spill[(s - 1) % SKY], spill[(s + 1) % SKY]
        v = main[s] + jnp.where(lane == 0, up, jnp.where(lane == 63, down, 0.0))
        v = jnp.where(lower, v, pltpu.roll(v, 64, 1))
        apart = jnp.where(sub == 4, 0.0, jnp.where(lower, v, swap(v)))
        values.append(jnp.where(packed, apart, v))
    cosine, sine = dft_32(values)
    spectrum = [None] * 32
    spectrum[0], spectrum[16] = cosine[0], cosine[16]
    for k in range(1, 16):
        turned = bent(sine[k])
        spectrum[k], spectrum[32 - k] = cosine[k] + turned, cosine[k] - turned
    twisted = [spectrum[k] * cos_ref[k] + swap(spectrum[k]) * sin_ref[k] for k in range(32)]
    rows = jnp.concatenate(twisted, axis=0)
    pair = dot3(rows, high_table[...], low_table[...])
    pair_c = pair[:, :128].reshape(32, 8, 128)
    pair_s = pair[:, 128:].reshape(32, 8, 128)

    k1 = lax.broadcasted_iota(jnp.int32, (32, 8, 128), 0)
    k2 = lax.broadcasted_iota(jnp.int32, (32, 8, 128), 2) % 64
    nx = k1 + 32 * k2
    nx = jnp.where(nx < N // 2, nx, nx - N)
    n = 4 * sky + sub % 4
    ny = jnp.where(tile > 0, tile + 16 * n, jnp.where(n < 64, 16 * n, 8 + 16 * (n - 64)))
    ny = jnp.where(ny < N // 2, ny, ny - N)
    ny = jnp.where(jnp.logical_and(packed, jnp.logical_not(lower)), -(N // 2), ny)
    along_x = jnp.logical_or(packed, lower)[None]
    squared = nx * nx + (ny * ny)[None]
    wave = jnp.where(along_x, jnp.where(nx == -(N // 2), 0, nx), ny[None])
    unit = 2.0 * np.pi / N
    scale = float(-2.0 / unit / 64.0 / N / N)
    factor = scale * wave.astype(f32) / jnp.maximum(squared, 1).astype(f32)
    kappa_hat = pair_c + swap(pair_s) * sign[None]
    field = factor * (swap(kappa_hat) * (-sign)[None])
    pair = dot3(field.reshape(256, 128), high_table[...], low_table[...])
    values = []
    for k in range(32):
        v = pair[8 * k : 8 * k + 8, :128] - bent(pair[8 * k : 8 * k + 8, 128:])
        values.append(v * cos_ref[k] - swap(v) * sin_ref[k])
    cosine, sine = dft_32(values)
    for s in range(17):
        turned = bent(sine[s]) if 0 < s < 16 else None
        for at in (s,) if turned is None else (s, 32 - s):
            v = cosine[s]
            if turned is not None:
                v = v - turned if at == s else v + turned
            other = swap(pltpu.roll(v, 64, 1))
            joined = jnp.where(lower, jnp.where(sub == 4, other, v), 0.0)
            v = jnp.where(packed, joined, v)
            out_ref[at] = v
            out_ref[SKY + at] = v


def solve(pieces, tables):
    return pl.pallas_call(
        solve_kernel,
        out_shape=jax.ShapeDtypeStruct((64, 8, 128), f32),
        in_specs=[VM] * 5,
        out_specs=VM,
        compiler_params=limit(24),
        name="solve",
    )(pieces, *tables)


def back_for(ahead, eighth_ref, plain, bent, high_table, low_table, out_ref):
    zhi, column = lax.axis_index("zhi"), lax.axis_index("x")
    target = (column + ahead) % 4
    parts = []
    for half in range(2):
        lanes = slice(256 * half, 256 * half + 256)
        turns = (2 * column + half) * (4 * zhi + target) % 8
        cosine, sine = eighth_ref[turns], eighth_ref[8 + turns]
        parts.append(cosine * plain[:, lanes] + sine * bent[:, lanes])
    value = stacked(jnp.concatenate(parts, axis=1))
    out_ref[...] = dot3_stacked(value, high_table[column], low_table[column])


def back_kernel(
    eighth_ref, in_ref, high_table, low_table, far_ref, next_ref, last_ref, plain_ref, bent_ref
):
    value = in_ref[...]
    sub = lax.broadcasted_iota(jnp.int32, (64, 8, 128), 1)
    bent = pltpu.roll(value, 4, 1) * jnp.where(sub < 4, -1.0, 1.0)
    plain, bent = value.reshape(512, 128).T, bent.reshape(512, 128).T
    plain_ref[...] = plain
    bent_ref[...] = bent
    back_for(2, eighth_ref, plain, bent, high_table, low_table, far_ref)
    back_for(1, eighth_ref, plain, bent, high_table, low_table, next_ref)
    back_for(3, eighth_ref, plain, bent, high_table, low_table, last_ref)


def back_rest_kernel(eighth_ref, plain_ref, bent_ref, high_table, low_table, own_ref):
    back_for(0, eighth_ref, plain_ref[...], bent_ref[...], high_table, low_table, own_ref)


def back(pieces, tables):
    turns = np.arange(8) * (2 * np.pi / 8)
    eighth = np.concatenate([np.cos(turns), np.sin(turns)]).astype(np.float32)
    piece = jax.ShapeDtypeStruct((128, 256), f32)
    held = jax.ShapeDtypeStruct((128, 512), f32)
    two, one, three, plain, bent = pl.pallas_call(
        back_kernel,
        out_shape=(piece, piece, piece, held, held),
        in_specs=[SM, VM, VM, VM],
        out_specs=(VM,) * 5,
        compiler_params=limit(24),
        name="back",
    )(eighth, pieces, *tables)
    own = pl.pallas_call(
        back_rest_kernel,
        out_shape=piece,
        in_specs=[SM] + [VM] * 4,
        out_specs=VM,
        compiler_params=limit(24),
        name="back_rest",
    )(eighth, plain, bent, *tables)
    return own, one, two, three


def final_kernel(a_ref, b_ref, c_ref, d_ref, x_ref, y_ref):
    total = (a_ref[...] + b_ref[...]) + (c_ref[...] + d_ref[...])
    x_ref[...] = total[:ROWS]
    y_ref[...] = total[ROWS:]


def final(pieces):
    shape = jax.ShapeDtypeStruct((ROWS, 256), f32)
    return pl.pallas_call(
        final_kernel,
        out_shape=(shape, shape),
        in_specs=[VM] * 4,
        out_specs=(VM, VM),
        compiler_params=limit(24),
        name="final",
    )(*pieces)


def deliver(pieces):
    return [pieces[0]] + [
        lax.ppermute(pieces[a], "x", [(i, (i + a) % 4) for i in range(4)]) for a in (2, 1, 3)
    ]


def body(density, refine, weight_low, weight_high):
    def swap(array, axes, pairs):
        return lax.ppermute(array, axes, pairs + [(b, a) for a, b in pairs])

    odd = lax.axis_index("x") % 2 == 1
    layer = lax.dynamic_slice_in_dim(density, jnp.where(odd, LAYERS - 1, 0), 1, 0)
    layer = swap(layer, LOS, [(1, 2), (3, 4), (5, 6)])
    row, other_row, other_layer = edge_rows(density)
    other_layer = swap(other_layer, LOS, [(0, 1), (2, 3), (4, 5), (6, 7)])
    row = swap(row, "sky", [(i, i + 1) for i in range(0, SKY, 2)])
    other_row = swap(other_row, "sky", [(i, (i + 1) % SKY) for i in range(1, SKY, 2)])
    inner = inner_sums(weight_low, weight_high, density, refine)
    tables = halves(forward_table())
    summed = outer_sums(
        weight_low, weight_high, density, (layer, other_layer), (row, other_row), inner, tables
    )
    summed = deliver(summed)
    pieces = lax.all_to_all(turn(summed), ("zhi", "sky"), 0, 0, tiled=True)
    pieces = solve(pieces, twists() + halves(row_table()))
    pieces = lax.all_to_all(pieces, ("zhi", "sky"), 0, 0, tiled=True)
    fields = back(pieces, halves(inverse_table()))
    return final(deliver(fields))


def solution(mesh):
    devices = mesh.devices.reshape(2, 4, SKY)
    inner = Mesh(devices, ("zhi", "x", "sky"))
    placed = (P(LOS, "sky", None), P(LOS, "sky", None), P(LOS), P(LOS))
    return jax.shard_map(
        body,
        mesh=inner,
        in_specs=placed,
        out_specs=(P("sky", LOS), P("sky", LOS)),
        check_vma=False,
    )
```

```python
import functools

import jax
import jax.numpy as jnp
import ml_dtypes
import numpy as np
from jax import lax
from jax.experimental import pallas as pl
from jax.experimental.pallas import tpu as pltpu
from jax.sharding import Mesh, PartitionSpec as P

f32 = jnp.float32
bf16 = jnp.bfloat16
N = 2048
ROWS = 64
SKY = 32
LAYERS = 8
LOS = ("zhi", "x")
MB = 1024 * 1024


def halves(table):
    high = table.astype(np.float32).astype(ml_dtypes.bfloat16)
    low = (table - high.astype(np.float64)).astype(np.float32).astype(ml_dtypes.bfloat16)
    return high, low


def tile_modes(tile):
    n = np.arange(128)
    if tile:
        return tile + 16 * n
    return np.where(n < 64, 16 * n, 8 + 16 * (n - 64))


def tile_order(real, imag):
    pair = np.stack([real.reshape(SKY, 4, -1), imag.reshape(SKY, 4, -1)], axis=1)
    return pair.reshape(256, -1)


def tile_groups(real, imag):
    pair = np.stack([real.reshape(SKY, 4, -1), imag.reshape(SKY, 4, -1)], axis=1)
    return pair.transpose(2, 1, 0, 3).reshape(256, -1)


def forward_table():
    b = np.arange(128)
    tiles = []
    for tile in range(8):
        angle = (tile_modes(tile)[:, None] * b[None, :] % N) * (2 * np.pi / N)
        cosine, sine = np.cos(angle), np.sin(angle)
        if tile:
            real = np.concatenate([cosine, sine], 1)
            imag = np.concatenate([-sine, cosine], 1)
        else:
            zero = np.zeros((64, 128))
            real = np.block([[cosine[:64], zero], [zero, cosine[64:]]])
            imag = np.block([[-sine[:64], zero], [zero, -sine[64:]]])
            imag[0, :128] = (-1.0) ** b
        tiles.append(tile_groups(real, imag).T)
    return np.stack(tiles)


def inverse_table():
    j = np.arange(256)
    tiles = []
    for tile in range(8):
        angle = (tile_modes(tile)[:, None] * j[None, :] % N) * (2 * np.pi / N)
        real, imag = 2 * np.cos(angle), -2 * np.sin(angle)
        if not tile:
            real[0] = 1.0
            imag[0] = (-1.0) ** j
        tiles.append(tile_order(real, imag))
    return np.stack(tiles).reshape(4, 512, 256)


def row_table():
    r = np.arange(64)
    angle = (r[:, None] * r[None, :] % 64) * (2 * np.pi / 64)
    both = np.eye(2)
    return np.concatenate([np.kron(both, np.cos(angle)), np.kron(both, np.sin(angle))], 1)


def twists():
    angle = (np.arange(32)[:, None] * (np.arange(128) % 64)[None, :]) * (2 * np.pi / N)
    sign = np.where(np.arange(8) < 4, 1.0, -1.0)
    cosine = np.broadcast_to(np.cos(angle)[:, None, :], (32, 8, 128))
    sine = np.sin(angle)[:, None, :] * sign[None, :, None]
    return cosine.astype(np.float32), sine.astype(np.float32)


def minmod(a, b):
    return jnp.maximum(jnp.minimum(a, b), 0.0) + jnp.minimum(jnp.maximum(a, b), 0.0)


def split(value):
    high = value.astype(bf16)
    return high, (value - high.astype(f32)).astype(bf16)


def dot3(value, high_table, low_table):
    high, low = split(value)
    dot = functools.partial(jnp.dot, preferred_element_type=f32)
    return dot(high, high_table) + (dot(low, high_table) + dot(high, low_table))


def stacked(value):
    return jnp.concatenate(split(value), axis=0)


def dot3_stacked(parts, high_table, low_table):
    rows = parts.shape[0] // 2
    dot = functools.partial(jnp.dot, preferred_element_type=f32)
    both = dot(parts, high_table)
    return both[:rows] + (both[rows:] + dot(parts[:rows], low_table))


def limit(mib):
    return pltpu.CompilerParams(vmem_limit_bytes=mib * MB)


VM = pl.BlockSpec(memory_space=pltpu.VMEM)
SM = pl.BlockSpec(memory_space=pltpu.SMEM)


def rows_kernel(d_ref, near_ref, far_ref, layer_ref):
    layer_ref[0] = jnp.where(lax.axis_index("x") % 2 == 1, d_ref[0], d_ref[LAYERS - 1])
    even = lax.axis_index("sky") % 2 == 0
    for z in range(LAYERS):
        first = d_ref[z, 0:16, :].astype(f32)[0:1]
        last = d_ref[z, 48:64, :].astype(f32)[15:16]
        near_ref[z : z + 1, :] = jnp.where(even, last, first)
        far_ref[z : z + 1, :] = jnp.where(even, first, last)


def edge_rows(density):
    shape = jax.ShapeDtypeStruct((LAYERS, N), f32)
    return pl.pallas_call(
        rows_kernel,
        out_shape=(shape, shape, jax.ShapeDtypeStruct((1, ROWS, N), bf16)),
        in_specs=[VM],
        out_specs=(VM, VM, VM),
        compiler_params=limit(8),
        name="edge_rows",
    )(density)


def longer(field):
    return jnp.concatenate([field, jnp.zeros((8, N), f32)], axis=0)


def smooth_y(field):
    return 0.75 * field + 0.125 * (pltpu.roll(field, 1, 1) + pltpu.roll(field, N - 1, 1))


CHUNK = 512


def inner_kernel(
    low_ref,
    high_ref,
    d_ref,
    refine_ref,
    kappa_ref,
    mask_ref,
    near_ref,
    calm_ref,
    lifted_ref,
    tx_ref,
    ty_ref,
):
    block = lax.broadcasted_iota(jnp.int32, (256, N), 0)
    lane = lax.broadcasted_iota(jnp.int32, (256, N), 1)
    grow = jnp.where(lane // 8 == block, 1.0, 0.0).astype(bf16)
    coarse = refine_ref[0].astype(f32).astype(bf16)
    mask_ref[...] = jnp.dot(coarse, grow, preferred_element_type=f32)
    for z in range(LAYERS):
        first = d_ref[z, 0:16, :].astype(f32)
        last = d_ref[z, 48:64, :].astype(f32)
        near_ref[0, z : z + 1, :] = first[0:1]
        near_ref[1, z : z + 1, :] = first[1:2]
        near_ref[2, z : z + 1, :] = last[14:15]
        near_ref[3, z : z + 1, :] = last[15:16]

    wide = CHUNK + 256
    row = lax.broadcasted_iota(jnp.int32, (ROWS, CHUNK), 0)
    inside = jnp.logical_and(row > 0, row < ROWS - 1)

    def chunk(i, carry):
        start = pl.multiple_of(i * CHUNK, CHUNK)
        left = pl.multiple_of((start + N - 128) % N, 128)
        right = pl.multiple_of((start + CHUNK) % N, 128)
        base = jnp.zeros((ROWS, CHUNK), f32)
        tz, tx, ty = base, base, base
        centre, step = None, None
        for z in range(LAYERS):
            average = 0.5 * (low_ref[z] + high_ref[z])
            former = centre
            around = jnp.concatenate(
                [
                    d_ref[z, :, pl.ds(left, 128)],
                    d_ref[z, :, pl.ds(start, CHUNK)],
                    d_ref[z, :, pl.ds(right, 128)],
                ],
                axis=1,
            ).astype(f32)
            centre = around[:, 128 : 128 + CHUNK]
            base = base + average * centre
            dy = pltpu.roll(around, wide - 1, 1) - around
            gy = minmod(dy, pltpu.roll(dy, 1, 1))[:, 128 : 128 + CHUNK]
            ty = ty + average * gy
            dx = pltpu.roll(centre, ROWS - 1, 0) - centre
            tx = tx + average * minmod(dx, pltpu.roll(dx, 1, 0))
            if z > 0:
                latter = centre - former
                if step is not None:
                    slope = 0.125 * (high_ref[z - 1] - low_ref[z - 1])
                    tz = tz + slope * minmod(latter, step)
                step = latter
        marked = mask_ref[:, pl.ds(start, CHUNK)]
        marked = jnp.broadcast_to(marked[:, None, :], (8, 8, CHUNK)).reshape(ROWS, CHUNK)
        at = pl.ds(start, CHUNK)
        calm_ref[:, at] = base - marked * base
        lifted_ref[:, at] = marked * (base + tz)
        tx_ref[:, at] = jnp.where(inside, marked * tx, 0.0)
        ty_ref[:, at] = marked * ty
        return carry

    lax.fori_loop(0, N // CHUNK, chunk, 0)
    lifted, tx = lifted_ref[...], tx_ref[...]
    eighth, tilt = 0.125 * lifted, ty_ref[...] * (1.0 / 32.0)
    smooth = 0.75 * lifted + pltpu.roll(eighth + tilt, 1, 1) + pltpu.roll(eighth - tilt, N - 1, 1)
    eighth, tilt = 0.125 * smooth, smooth_y(tx) * (1.0 / 32.0)
    kappa_ref[...] = (
        longer(calm_ref[...] + 0.75 * smooth)
        + pltpu.roll(longer(eighth + tilt), 1, 0)
        + pltpu.roll(longer(eighth - tilt), ROWS + 7, 0)
    )


def inner_sums(low, high, density, refine):
    return pl.pallas_call(
        inner_kernel,
        out_shape=(
            jax.ShapeDtypeStruct((ROWS + 8, N), f32),
            jax.ShapeDtypeStruct((8, N), f32),
            jax.ShapeDtypeStruct((4, LAYERS, N), f32),
        ),
        in_specs=[SM, SM, VM, VM],
        out_specs=(VM,) * 3,
        scratch_shapes=[pltpu.VMEM((ROWS, N), f32)] * 4,
        compiler_params=limit(40),
        cost_estimate=pl.CostEstimate(flops=40_000_000, bytes_accessed=24 * MB, transcendentals=0),
        name="inner_sums",
    )(low, high, density, refine)


def outer_kernel(
    low_ref,
    high_ref,
    d_ref,
    layer_ref,
    other_layer_ref,
    row_ref,
    other_row_ref,
    kappa_ref,
    mask_ref,
    near_ref,
    high_table,
    low_table,
    far_ref,
    next_ref,
    last_ref,
    part_ref,
):
    los = lax.axis_index("zhi") * 4 + lax.axis_index("x")
    v0, v1 = d_ref[0].astype(f32), d_ref[1].astype(f32)
    v6, v7 = d_ref[6].astype(f32), d_ref[7].astype(f32)
    odd = los % 2 == 1
    one, other = layer_ref[0].astype(f32), other_layer_ref[0].astype(f32)
    below = jnp.where(los == 0, v0, jnp.where(odd, other, one))
    above = jnp.where(los == 7, v7, jnp.where(odd, one, other))
    slope0 = 0.125 * (high_ref[0] - low_ref[0])
    slope7 = 0.125 * (high_ref[7] - low_ref[7])
    tz = slope0 * minmod(v1 - v0, v0 - below) + slope7 * minmod(above - v7, v7 - v6)
    mask = mask_ref[...]
    marked = jnp.broadcast_to(mask[:, None, :], (8, 8, N)).reshape(ROWS, N)
    smooth = smooth_y(marked * tz)
    layer = lax.broadcasted_iota(jnp.int32, (LAYERS, 1), 0)
    average = jnp.zeros((LAYERS, 1), f32)
    for z in range(LAYERS):
        average = jnp.where(layer == z, 0.5 * (low_ref[z] + high_ref[z]), average)
    r0, r1, r62, r63 = near_ref[0], near_ref[1], near_ref[2], near_ref[3]
    even = lax.axis_index("sky") % 2 == 0
    before = jnp.where(even, other_row_ref[...], row_ref[...])
    after = jnp.where(even, row_ref[...], other_row_ref[...])
    e0 = jnp.sum(average * minmod(r1 - r0, r0 - before), axis=0, keepdims=True)
    e63 = jnp.sum(average * minmod(after - r63, r63 - r62), axis=0, keepdims=True)
    row = lax.broadcasted_iota(jnp.int32, (8, N), 0)
    e0 = smooth_y(jnp.where(row == 0, mask[0:1] * e0, 0.0)) * (1.0 / 32.0)
    e63 = smooth_y(jnp.where(row == 7, mask[7:8] * e63, 0.0)) * (1.0 / 32.0)
    first = pltpu.roll(e0, 1, 0)
    last = pltpu.roll(e63, 7, 0)
    spill = jnp.where(row == 0, pltpu.roll(e63, 1, 0), -pltpu.roll(e0, 7, 0))
    sides = jnp.concatenate([first, jnp.zeros((ROWS - 16, N), f32), -last, spill], axis=0)
    eighth = longer(0.125 * smooth)
    kappa = (
        (kappa_ref[...] + sides)
        + longer(0.75 * smooth)
        + (pltpu.roll(eighth, 1, 0) + pltpu.roll(eighth, ROWS + 7, 0))
    )
    part = [kappa[:, 128 * a : 128 * a + 128] for a in range(16)]
    even = [part[a] + part[16 - a] for a in range(1, 8)]
    odd = [part[a] - part[16 - a] for a in range(1, 8)]

    def weigh(pairs):
        total = None
        for factor, value in pairs:
            if abs(factor) < 1e-9:
                continue
            term = value if abs(factor - 1) < 1e-9 else factor * value
            total = term if total is None else total + term
        return total

    def cosines(k):
        first = part[0] + part[8] if k % 2 == 0 else part[0] - part[8]
        return first + weigh((float(np.cos(np.pi * k * a / 8)), even[a - 1]) for a in range(1, 8))

    def sines(k):
        return weigh((float(-np.sin(np.pi * k * a / 8)), odd[a - 1]) for a in range(1, 8))

    for tile in range(8):
        second = sines(tile) if tile else cosines(8)
        value = jnp.concatenate([cosines(tile), second], axis=1)
        value = jnp.concatenate([value, jnp.zeros((8, 256), f32)], axis=0)
        part_ref[tile] = stacked(value)
    transform_for(2, part_ref, high_table, low_table, far_ref)
    transform_for(1, part_ref, high_table, low_table, next_ref)
    transform_for(3, part_ref, high_table, low_table, last_ref)


def transform_for(ahead, part_ref, high_table, low_table, out_ref):
    target = (lax.axis_index("x") + ahead) % 4
    for half in range(2):
        tile = 2 * target + half
        value = dot3_stacked(part_ref[tile], high_table[tile], low_table[tile])
        for block in (2 * half, 2 * half + 1):
            part = value[:, 128 * (block % 2) : 128 * (block % 2) + 128]
            out_ref[ROWS * block : ROWS * block + ROWS] = part[:ROWS]
            out_ref[4 * ROWS + block : 4 * ROWS + block + 1] = part[ROWS : ROWS + 1]
            out_ref[4 * ROWS + 4 + block : 4 * ROWS + 5 + block] = part[ROWS + 7 : ROWS + 8]


def rest_kernel(part_ref, high_table, low_table, own_ref):
    transform_for(0, part_ref, high_table, low_table, own_ref)


def outer_sums(low, high, density, layers, rows, inner, tables):
    piece = jax.ShapeDtypeStruct((4 * ROWS + 8, 128), f32)
    two, one, three, parts = pl.pallas_call(
        outer_kernel,
        out_shape=(piece, piece, piece, jax.ShapeDtypeStruct((8, 160, 256), bf16)),
        in_specs=[SM, SM] + [VM] * 10,
        out_specs=(VM,) * 4,
        compiler_params=limit(32),
        name="outer_sums",
    )(low, high, density, *layers, *rows, *inner, *tables)
    own = pl.pallas_call(
        rest_kernel,
        out_shape=piece,
        in_specs=[VM] * 3,
        out_specs=VM,
        compiler_params=limit(24),
        name="other_sums",
    )(parts, *tables)
    return own, one, two, three


def turn_kernel(a_ref, b_ref, c_ref, d_ref, out_ref):
    total = (a_ref[...] + b_ref[...]) + (c_ref[...] + d_ref[...])
    none = jnp.zeros((56, 128), f32)
    turned = [
        jnp.concatenate([total[ROWS * block : ROWS * block + ROWS], total[4 * ROWS :], none], axis=0).T
        for block in range(4)
    ]
    lane = lax.broadcasted_iota(jnp.int32, (SKY, 128), 1)
    for half in range(2):
        at = slice(SKY * half, SKY * half + SKY)
        spill = jnp.zeros((SKY, 128), f32)
        for c in range(4):
            block, first = 2 * half + c // 2, 64 * (c % 2)
            real = turned[block][first : first + SKY]
            imag = turned[block][first + SKY : first + 2 * SKY]
            out_ref[at, 0, 128 * c : 128 * c + 128] = jnp.where(
                lane < 64, real, pltpu.roll(imag, 64, 1)
            )
            for sub, part in ((c, real), (4 + c, imag)):
                up = (128 - 16 * sub) % 128
                down = (up + 63) % 128
                spill = jnp.where(lane == up, pltpu.roll(part, (up - 64 - block) % 128, 1), spill)
                spill = jnp.where(
                    lane == down, pltpu.roll(part, (down - 68 - block) % 128, 1), spill
                )
        out_ref[at, 0, 512:640] = spill


def turn(pieces):
    return pl.pallas_call(
        turn_kernel,
        out_shape=jax.ShapeDtypeStruct((64, 1, 640), f32),
        in_specs=[VM] * 4,
        out_specs=VM,
        compiler_params=limit(24),
        name="turn",
    )(*pieces)


def dft_32(values):
    even = [values[s] + values[32 - s] for s in range(1, 16)]
    odd = [values[s] - values[32 - s] for s in range(1, 16)]
    ends = [values[0] + values[16], values[0] - values[16]]
    cosine, sine = [None] * 17, [None] * 17
    for k in range(9):
        plain = ends[k % 2]
        turned = None
        for s in range(1, 16):
            term = float(np.cos(np.pi * k * s / 16)) * even[s - 1]
            if s % 2 == 0:
                plain = plain + term
            else:
                turned = term if turned is None else turned + term
        cosine[k] = plain + turned
        cosine[16 - k] = plain - turned
    for k in range(1, 9):
        plain, turned = None, None
        for s in range(1, 16):
            term = float(np.sin(np.pi * k * s / 16)) * odd[s - 1]
            if s % 2 == 0:
                plain = term if plain is None else plain + term
            else:
                turned = term if turned is None else turned + term
        sine[k] = turned + plain
        sine[16 - k] = turned - plain
    return cosine, sine


def solve_kernel(in_ref, cos_ref, sin_ref, high_table, low_table, out_ref):
    sky = lax.axis_index("sky")
    tile = 2 * lax.axis_index("x") + lax.axis_index("zhi")
    lane = lax.broadcasted_iota(jnp.int32, (8, 128), 1)
    sub = lax.broadcasted_iota(jnp.int32, (8, 128), 0)
    lower = lane < 64
    sign = jnp.where(sub < 4, 1.0, -1.0)
    first = jnp.logical_and(tile == 0, sky == 0)
    packed = jnp.logical_and(sub % 4 == 0, first)

    def swap(v):
        return pltpu.roll(v, 4, v.ndim - 2)

    def bent(v):
        return swap(v) * sign

    main, spill = [], []
    for s in range(SKY):
        rows = [
            jnp.broadcast_to(in_ref[s, :, lanes] + in_ref[SKY + s, :, lanes], (8, 128))
            for lanes in (slice(128 * c, 128 * c + 128) for c in range(5))
        ]
        v = rows[3]
        for c in range(3):
            v = jnp.where(sub % 4 == c, rows[c], v)
        main.append(jnp.where(sub < 4, v, pltpu.roll(v, 64, 1)))
        spill.append(pltpu.roll(rows[4], 0, 1, stride=16, stride_axis=0))
    values = []
    for s in range(SKY):
        up, down = spill[(s - 1) % SKY], spill[(s + 1) % SKY]
        v = main[s] + jnp.where(lane == 0, up, jnp.where(lane == 63, down, 0.0))
        v = jnp.where(lower, v, pltpu.roll(v, 64, 1))
        apart = jnp.where(sub == 4, 0.0, jnp.where(lower, v, swap(v)))
        values.append(jnp.where(packed, apart, v))
    cosine, sine = dft_32(values)
    spectrum = [None] * 32
    spectrum[0], spectrum[16] = cosine[0], cosine[16]
    for k in range(1, 16):
        turned = bent(sine[k])
        spectrum[k], spectrum[32 - k] = cosine[k] + turned, cosine[k] - turned
    twisted = [spectrum[k] * cos_ref[k] + swap(spectrum[k]) * sin_ref[k] for k in range(32)]
    rows = jnp.concatenate(twisted, axis=0)
    pair = dot3(rows, high_table[...], low_table[...])
    pair_c = pair[:, :128].reshape(32, 8, 128)
    pair_s = pair[:, 128:].reshape(32, 8, 128)

    k1 = lax.broadcasted_iota(jnp.int32, (32, 8, 128), 0)
    k2 = lax.broadcasted_iota(jnp.int32, (32, 8, 128), 2) % 64
    nx = k1 + 32 * k2
    nx = jnp.where(nx < N // 2, nx, nx - N)
    n = 4 * sky + sub % 4
    ny = jnp.where(tile > 0, tile + 16 * n, jnp.where(n < 64, 16 * n, 8 + 16 * (n - 64)))
    ny = jnp.where(ny < N // 2, ny, ny - N)
    ny = jnp.where(jnp.logical_and(packed, jnp.logical_not(lower)), -(N // 2), ny)
    along_x = jnp.logical_or(packed, lower)[None]
    squared = nx * nx + (ny * ny)[None]
    wave = jnp.where(along_x, jnp.where(nx == -(N // 2), 0, nx), ny[None])
    unit = 2.0 * np.pi / N
    scale = float(-2.0 / unit / 64.0 / N / N)
    factor = scale * wave.astype(f32) / jnp.maximum(squared, 1).astype(f32)
    kappa_hat = pair_c + swap(pair_s) * sign[None]
    field = factor * (swap(kappa_hat) * (-sign)[None])
    pair = dot3(field.reshape(256, 128), high_table[...], low_table[...])
    values = []
    for k in range(32):
        v = pair[8 * k : 8 * k + 8, :128] - bent(pair[8 * k : 8 * k + 8, 128:])
        values.append(v * cos_ref[k] - swap(v) * sin_ref[k])
    cosine, sine = dft_32(values)
    for s in range(17):
        turned = bent(sine[s]) if 0 < s < 16 else None
        for at in (s,) if turned is None else (s, 32 - s):
            v = cosine[s]
            if turned is not None:
                v = v - turned if at == s else v + turned
            other = swap(pltpu.roll(v, 64, 1))
            joined = jnp.where(lower, jnp.where(sub == 4, other, v), 0.0)
            v = jnp.where(packed, joined, v)
            out_ref[at] = v
            out_ref[SKY + at] = v


def solve(pieces, tables):
    return pl.pallas_call(
        solve_kernel,
        out_shape=jax.ShapeDtypeStruct((64, 8, 128), f32),
        in_specs=[VM] * 5,
        out_specs=VM,
        compiler_params=limit(24),
        name="solve",
    )(pieces, *tables)


def back_for(ahead, eighth_ref, plain, bent, high_table, low_table, out_ref):
    zhi, column = lax.axis_index("zhi"), lax.axis_index("x")
    target = (column + ahead) % 4
    parts = []
    for half in range(2):
        lanes = slice(256 * half, 256 * half + 256)
        turns = (2 * column + half) * (4 * zhi + target) % 8
        cosine, sine = eighth_ref[turns], eighth_ref[8 + turns]
        parts.append(cosine * plain[:, lanes] + sine * bent[:, lanes])
    value = stacked(jnp.concatenate(parts, axis=1))
    out_ref[...] = dot3_stacked(value, high_table[column], low_table[column])


def back_kernel(
    eighth_ref, in_ref, high_table, low_table, far_ref, next_ref, last_ref, plain_ref, bent_ref
):
    value = in_ref[...]
    sub = lax.broadcasted_iota(jnp.int32, (64, 8, 128), 1)
    bent = pltpu.roll(value, 4, 1) * jnp.where(sub < 4, -1.0, 1.0)
    plain, bent = value.reshape(512, 128).T, bent.reshape(512, 128).T
    plain_ref[...] = plain
    bent_ref[...] = bent
    back_for(2, eighth_ref, plain, bent, high_table, low_table, far_ref)
    back_for(1, eighth_ref, plain, bent, high_table, low_table, next_ref)
    back_for(3, eighth_ref, plain, bent, high_table, low_table, last_ref)


def back_rest_kernel(eighth_ref, plain_ref, bent_ref, high_table, low_table, own_ref):
    back_for(0, eighth_ref, plain_ref[...], bent_ref[...], high_table, low_table, own_ref)


def back(pieces, tables):
    turns = np.arange(8) * (2 * np.pi / 8)
    eighth = np.concatenate([np.cos(turns), np.sin(turns)]).astype(np.float32)
    piece = jax.ShapeDtypeStruct((128, 256), f32)
    held = jax.ShapeDtypeStruct((128, 512), f32)
    two, one, three, plain, bent = pl.pallas_call(
        back_kernel,
        out_shape=(piece, piece, piece, held, held),
        in_specs=[SM, VM, VM, VM],
        out_specs=(VM,) * 5,
        compiler_params=limit(24),
        name="back",
    )(eighth, pieces, *tables)
    own = pl.pallas_call(
        back_rest_kernel,
        out_shape=piece,
        in_specs=[SM] + [VM] * 4,
        out_specs=VM,
        compiler_params=limit(24),
        name="back_rest",
    )(eighth, plain, bent, *tables)
    return own, one, two, three


def final_kernel(a_ref, b_ref, c_ref, d_ref, x_ref, y_ref):
    total = (a_ref[...] + b_ref[...]) + (c_ref[...] + d_ref[...])
    x_ref[...] = total[:ROWS]
    y_ref[...] = total[ROWS:]


def final(pieces):
    shape = jax.ShapeDtypeStruct((ROWS, 256), f32)
    return pl.pallas_call(
        final_kernel,
        out_shape=(shape, shape),
        in_specs=[VM] * 4,
        out_specs=(VM, VM),
        compiler_params=limit(24),
        name="final",
    )(*pieces)


def deliver(pieces):
    return [pieces[0]] + [
        lax.ppermute(pieces[a], "x", [(i, (i + a) % 4) for i in range(4)]) for a in (2, 1, 3)
    ]


def body(density, refine, weight_low, weight_high):
    def swap(array, axes, pairs):
        return lax.ppermute(array, axes, pairs + [(b, a) for a, b in pairs])

    odd = lax.axis_index("x") % 2 == 1
    layer = lax.dynamic_slice_in_dim(density, jnp.where(odd, LAYERS - 1, 0), 1, 0)
    layer = swap(layer, LOS, [(1, 2), (3, 4), (5, 6)])
    row, other_row, other_layer = edge_rows(density)
    other_layer = swap(other_layer, LOS, [(0, 1), (2, 3), (4, 5), (6, 7)])
    row = swap(row, "sky", [(i, i + 1) for i in range(0, SKY, 2)])
    other_row = swap(other_row, "sky", [(i, (i + 1) % SKY) for i in range(1, SKY, 2)])
    inner = inner_sums(weight_low, weight_high, density, refine)
    tables = halves(forward_table())
    summed = outer_sums(
        weight_low, weight_high, density, (layer, other_layer), (row, other_row), inner, tables
    )
    summed = deliver(summed)
    pieces = lax.all_to_all(turn(summed), ("zhi", "sky"), 0, 0, tiled=True)
    pieces = solve(pieces, twists() + halves(row_table()))
    pieces = lax.all_to_all(pieces, ("zhi", "sky"), 0, 0, tiled=True)
    fields = back(pieces, halves(inverse_table()))
    return final(deliver(fields))


def solution(mesh):
    devices = mesh.devices.reshape(2, 4, SKY)
    inner = Mesh(devices, ("zhi", "x", "sky"))
    placed = (P(LOS, "sky", None), P(LOS, "sky", None), P(LOS), P(LOS))
    return jax.shard_map(
        body,
        mesh=inner,
        in_specs=placed,
        out_specs=(P("sky", LOS), P("sky", LOS)),
        check_vma=False,
    )
```

```python
import functools

import jax
import jax.numpy as jnp
import ml_dtypes
import numpy as np
from jax import lax
from jax.experimental import pallas as pl
from jax.experimental.pallas import tpu as pltpu
from jax.sharding import Mesh, PartitionSpec as P

f32 = jnp.float32
bf16 = jnp.bfloat16
N = 2048
ROWS = 64
SKY = 32
LAYERS = 8
LOS = ("zhi", "x")
MB = 1024 * 1024


def halves(table):
    high = table.astype(np.float32).astype(ml_dtypes.bfloat16)
    low = (table - high.astype(np.float64)).astype(np.float32).astype(ml_dtypes.bfloat16)
    return high, low


def tile_modes(tile):
    n = np.arange(128)
    if tile:
        return tile + 16 * n
    return np.where(n < 64, 16 * n, 8 + 16 * (n - 64))


def tile_order(real, imag):
    pair = np.stack([real.reshape(SKY, 4, -1), imag.reshape(SKY, 4, -1)], axis=1)
    return pair.reshape(256, -1)


def tile_groups(real, imag):
    pair = np.stack([real.reshape(SKY, 4, -1), imag.reshape(SKY, 4, -1)], axis=1)
    return pair.transpose(2, 1, 0, 3).reshape(256, -1)


def forward_table():
    b = np.arange(128)
    tiles = []
    for tile in range(8):
        angle = (tile_modes(tile)[:, None] * b[None, :] % N) * (2 * np.pi / N)
        cosine, sine = np.cos(angle), np.sin(angle)
        if tile:
            real = np.concatenate([cosine, sine], 1)
            imag = np.concatenate([-sine, cosine], 1)
        else:
            zero = np.zeros((64, 128))
            real = np.block([[cosine[:64], zero], [zero, cosine[64:]]])
            imag = np.block([[-sine[:64], zero], [zero, -sine[64:]]])
            imag[0, :128] = (-1.0) ** b
        tiles.append(tile_groups(real, imag).T)
    return np.stack(tiles)


def inverse_table():
    j = np.arange(256)
    tiles = []
    for tile in range(8):
        angle = (tile_modes(tile)[:, None] * j[None, :] % N) * (2 * np.pi / N)
        real, imag = 2 * np.cos(angle), -2 * np.sin(angle)
        if not tile:
            real[0] = 1.0
            imag[0] = (-1.0) ** j
        tiles.append(tile_order(real, imag))
    return np.stack(tiles).reshape(4, 512, 256)


def row_table():
    r = np.arange(64)
    angle = (r[:, None] * r[None, :] % 64) * (2 * np.pi / 64)
    both = np.eye(2)
    return np.concatenate([np.kron(both, np.cos(angle)), np.kron(both, np.sin(angle))], 1)


def twists():
    angle = (np.arange(32)[:, None] * (np.arange(128) % 64)[None, :]) * (2 * np.pi / N)
    sign = np.where(np.arange(8) < 4, 1.0, -1.0)
    cosine = np.broadcast_to(np.cos(angle)[:, None, :], (32, 8, 128))
    sine = np.sin(angle)[:, None, :] * sign[None, :, None]
    return cosine.astype(np.float32), sine.astype(np.float32)


def minmod(a, b):
    return jnp.maximum(jnp.minimum(a, b), 0.0) + jnp.minimum(jnp.maximum(a, b), 0.0)


def split(value):
    high = value.astype(bf16)
    return high, (value - high.astype(f32)).astype(bf16)


def dot3(value, high_table, low_table):
    high, low = split(value)
    dot = functools.partial(jnp.dot, preferred_element_type=f32)
    return dot(high, high_table) + (dot(low, high_table) + dot(high, low_table))


def stacked(value):
    return jnp.concatenate(split(value), axis=0)


def dot3_stacked(parts, high_table, low_table):
    rows = parts.shape[0] // 2
    dot = functools.partial(jnp.dot, preferred_element_type=f32)
    both = dot(parts, high_table)
    return both[:rows] + (both[rows:] + dot(parts[:rows], low_table))


def limit(mib):
    return pltpu.CompilerParams(vmem_limit_bytes=mib * MB)


VM = pl.BlockSpec(memory_space=pltpu.VMEM)
SM = pl.BlockSpec(memory_space=pltpu.SMEM)


def rows_kernel(d_ref, near_ref, far_ref, layer_ref, other_layer_ref):
    odd = lax.axis_index("x") % 2
    layer_ref[0] = d_ref[(LAYERS - 1) * odd]
    other_layer_ref[0] = d_ref[(LAYERS - 1) * (1 - odd)]
    even = lax.axis_index("sky") % 2 == 0
    for z in range(LAYERS):
        first = d_ref[z, 0:16, :].astype(f32)[0:1]
        last = d_ref[z, 48:64, :].astype(f32)[15:16]
        near_ref[z : z + 1, :] = jnp.where(even, last, first)
        far_ref[z : z + 1, :] = jnp.where(even, first, last)


def edge_rows(density):
    shape = jax.ShapeDtypeStruct((LAYERS, N), f32)
    return pl.pallas_call(
        rows_kernel,
        out_shape=(shape, shape) + (jax.ShapeDtypeStruct((1, ROWS, N), bf16),) * 2,
        in_specs=[VM],
        out_specs=(VM,) * 4,
        compiler_params=limit(8),
        name="edge_rows",
    )(density)


def longer(field):
    return jnp.concatenate([field, jnp.zeros((8, N), f32)], axis=0)


def smooth_y(field):
    return 0.75 * field + 0.125 * (pltpu.roll(field, 1, 1) + pltpu.roll(field, N - 1, 1))


CHUNK = 512


def inner_kernel(
    low_ref,
    high_ref,
    d_ref,
    refine_ref,
    kappa_ref,
    mask_ref,
    near_ref,
    calm_ref,
    lifted_ref,
    tx_ref,
    ty_ref,
):
    block = lax.broadcasted_iota(jnp.int32, (256, N), 0)
    lane = lax.broadcasted_iota(jnp.int32, (256, N), 1)
    grow = jnp.where(lane // 8 == block, 1.0, 0.0).astype(bf16)
    coarse = refine_ref[0].astype(f32).astype(bf16)
    mask_ref[...] = jnp.dot(coarse, grow, preferred_element_type=f32)
    for z in range(LAYERS):
        first = d_ref[z, 0:16, :].astype(f32)
        last = d_ref[z, 48:64, :].astype(f32)
        near_ref[0, z : z + 1, :] = first[0:1]
        near_ref[1, z : z + 1, :] = first[1:2]
        near_ref[2, z : z + 1, :] = last[14:15]
        near_ref[3, z : z + 1, :] = last[15:16]

    wide = CHUNK + 256
    row = lax.broadcasted_iota(jnp.int32, (ROWS, CHUNK), 0)
    inside = jnp.logical_and(row > 0, row < ROWS - 1)

    def chunk(i, carry):
        start = pl.multiple_of(i * CHUNK, CHUNK)
        left = pl.multiple_of((start + N - 128) % N, 128)
        right = pl.multiple_of((start + CHUNK) % N, 128)
        base = jnp.zeros((ROWS, CHUNK), f32)
        tz, tx, ty = base, base, base
        centre, step = None, None
        for z in range(LAYERS):
            average = 0.5 * (low_ref[z] + high_ref[z])
            former = centre
            around = jnp.concatenate(
                [
                    d_ref[z, :, pl.ds(left, 128)],
                    d_ref[z, :, pl.ds(start, CHUNK)],
                    d_ref[z, :, pl.ds(right, 128)],
                ],
                axis=1,
            ).astype(f32)
            centre = around[:, 128 : 128 + CHUNK]
            base = base + average * centre
            dy = pltpu.roll(around, wide - 1, 1) - around
            gy = minmod(dy, pltpu.roll(dy, 1, 1))[:, 128 : 128 + CHUNK]
            ty = ty + average * gy
            dx = pltpu.roll(centre, ROWS - 1, 0) - centre
            tx = tx + average * minmod(dx, pltpu.roll(dx, 1, 0))
            if z > 0:
                latter = centre - former
                if step is not None:
                    slope = 0.125 * (high_ref[z - 1] - low_ref[z - 1])
                    tz = tz + slope * minmod(latter, step)
                step = latter
        marked = mask_ref[:, pl.ds(start, CHUNK)]
        marked = jnp.broadcast_to(marked[:, None, :], (8, 8, CHUNK)).reshape(ROWS, CHUNK)
        at = pl.ds(start, CHUNK)
        calm_ref[:, at] = base - marked * base
        lifted_ref[:, at] = marked * (base + tz)
        tx_ref[:, at] = jnp.where(inside, marked * tx, 0.0)
        ty_ref[:, at] = marked * ty
        return carry

    lax.fori_loop(0, N // CHUNK, chunk, 0)
    lifted, tx = lifted_ref[...], tx_ref[...]
    eighth, tilt = 0.125 * lifted, ty_ref[...] * (1.0 / 32.0)
    smooth = 0.75 * lifted + pltpu.roll(eighth + tilt, 1, 1) + pltpu.roll(eighth - tilt, N - 1, 1)
    eighth, tilt = 0.125 * smooth, smooth_y(tx) * (1.0 / 32.0)
    kappa_ref[...] = (
        longer(calm_ref[...] + 0.75 * smooth)
        + pltpu.roll(longer(eighth + tilt), 1, 0)
        + pltpu.roll(longer(eighth - tilt), ROWS + 7, 0)
    )


def inner_sums(low, high, density, refine):
    return pl.pallas_call(
        inner_kernel,
        out_shape=(
            jax.ShapeDtypeStruct((ROWS + 8, N), f32),
            jax.ShapeDtypeStruct((8, N), f32),
            jax.ShapeDtypeStruct((4, LAYERS, N), f32),
        ),
        in_specs=[SM, SM, VM, VM],
        out_specs=(VM,) * 3,
        scratch_shapes=[pltpu.VMEM((ROWS, N), f32)] * 4,
        compiler_params=limit(40),
        cost_estimate=pl.CostEstimate(flops=40_000_000, bytes_accessed=24 * MB, transcendentals=0),
        name="inner_sums",
    )(low, high, density, refine)


def outer_kernel(
    low_ref,
    high_ref,
    d_ref,
    cross_ref,
    layer_ref,
    other_layer_ref,
    row_ref,
    other_row_ref,
    kappa_ref,
    mask_ref,
    near_ref,
    high_table,
    low_table,
    far_ref,
    next_ref,
    last_ref,
    part_ref,
):
    los = lax.axis_index("zhi") * 4 + lax.axis_index("x")
    v0, v1 = d_ref[0].astype(f32), d_ref[1].astype(f32)
    v6, v7 = d_ref[6].astype(f32), d_ref[7].astype(f32)
    odd = los % 2 == 1
    crossing = jnp.logical_or(los == 3, los == 4)
    one = jnp.where(crossing, cross_ref[0], layer_ref[0]).astype(f32)
    other = other_layer_ref[0].astype(f32)
    below = jnp.where(los == 0, v0, jnp.where(odd, other, one))
    above = jnp.where(los == 7, v7, jnp.where(odd, one, other))
    slope0 = 0.125 * (high_ref[0] - low_ref[0])
    slope7 = 0.125 * (high_ref[7] - low_ref[7])
    tz = slope0 * minmod(v1 - v0, v0 - below) + slope7 * minmod(above - v7, v7 - v6)
    mask = mask_ref[...]
    marked = jnp.broadcast_to(mask[:, None, :], (8, 8, N)).reshape(ROWS, N)
    smooth = smooth_y(marked * tz)
    layer = lax.broadcasted_iota(jnp.int32, (LAYERS, 1), 0)
    average = jnp.zeros((LAYERS, 1), f32)
    for z in range(LAYERS):
        average = jnp.where(layer == z, 0.5 * (low_ref[z] + high_ref[z]), average)
    r0, r1, r62, r63 = near_ref[0], near_ref[1], near_ref[2], near_ref[3]
    even = lax.axis_index("sky") % 2 == 0
    before = jnp.where(even, other_row_ref[...], row_ref[...])
    after = jnp.where(even, row_ref[...], other_row_ref[...])
    e0 = jnp.sum(average * minmod(r1 - r0, r0 - before), axis=0, keepdims=True)
    e63 = jnp.sum(average * minmod(after - r63, r63 - r62), axis=0, keepdims=True)
    row = lax.broadcasted_iota(jnp.int32, (8, N), 0)
    e0 = smooth_y(jnp.where(row == 0, mask[0:1] * e0, 0.0)) * (1.0 / 32.0)
    e63 = smooth_y(jnp.where(row == 7, mask[7:8] * e63, 0.0)) * (1.0 / 32.0)
    first = pltpu.roll(e0, 1, 0)
    last = pltpu.roll(e63, 7, 0)
    spill = jnp.where(row == 0, pltpu.roll(e63, 1, 0), -pltpu.roll(e0, 7, 0))
    sides = jnp.concatenate([first, jnp.zeros((ROWS - 16, N), f32), -last, spill], axis=0)
    eighth = longer(0.125 * smooth)
    kappa = (
        (kappa_ref[...] + sides)
        + longer(0.75 * smooth)
        + (pltpu.roll(eighth, 1, 0) + pltpu.roll(eighth, ROWS + 7, 0))
    )
    part = [kappa[:, 128 * a : 128 * a + 128] for a in range(16)]
    even = [part[a] + part[16 - a] for a in range(1, 8)]
    odd = [part[a] - part[16 - a] for a in range(1, 8)]

    def weigh(pairs):
        total = None
        for factor, value in pairs:
            if abs(factor) < 1e-9:
                continue
            term = value if abs(factor - 1) < 1e-9 else factor * value
            total = term if total is None else total + term
        return total

    def cosines(k):
        first = part[0] + part[8] if k % 2 == 0 else part[0] - part[8]
        return first + weigh((float(np.cos(np.pi * k * a / 8)), even[a - 1]) for a in range(1, 8))

    def sines(k):
        return weigh((float(-np.sin(np.pi * k * a / 8)), odd[a - 1]) for a in range(1, 8))

    for tile in range(8):
        second = sines(tile) if tile else cosines(8)
        value = jnp.concatenate([cosines(tile), second], axis=1)
        value = jnp.concatenate([value, jnp.zeros((8, 256), f32)], axis=0)
        part_ref[tile] = stacked(value)
    transform_for(2, part_ref, high_table, low_table, far_ref)
    transform_for(1, part_ref, high_table, low_table, next_ref)
    transform_for(3, part_ref, high_table, low_table, last_ref)


def transform_for(ahead, part_ref, high_table, low_table, out_ref):
    target = (lax.axis_index("x") + ahead) % 4
    for half in range(2):
        tile = 2 * target + half
        value = dot3_stacked(part_ref[tile], high_table[tile], low_table[tile])
        for block in (2 * half, 2 * half + 1):
            part = value[:, 128 * (block % 2) : 128 * (block % 2) + 128]
            out_ref[ROWS * block : ROWS * block + ROWS] = part[:ROWS]
            out_ref[4 * ROWS + block : 4 * ROWS + block + 1] = part[ROWS : ROWS + 1]
            out_ref[4 * ROWS + 4 + block : 4 * ROWS + 5 + block] = part[ROWS + 7 : ROWS + 8]


def rest_kernel(part_ref, high_table, low_table, own_ref):
    transform_for(0, part_ref, high_table, low_table, own_ref)


def outer_sums(low, high, density, layers, rows, inner, tables):
    piece = jax.ShapeDtypeStruct((4 * ROWS + 8, 128), f32)
    two, one, three, parts = pl.pallas_call(
        outer_kernel,
        out_shape=(piece, piece, piece, jax.ShapeDtypeStruct((8, 160, 256), bf16)),
        in_specs=[SM, SM] + [VM] * 11,
        out_specs=(VM,) * 4,
        compiler_params=limit(32),
        name="outer_sums",
    )(low, high, density, *layers, *rows, *inner, *tables)
    own = pl.pallas_call(
        rest_kernel,
        out_shape=piece,
        in_specs=[VM] * 3,
        out_specs=VM,
        compiler_params=limit(24),
        name="other_sums",
    )(parts, *tables)
    return own, one, two, three


def turn_kernel(a_ref, b_ref, c_ref, d_ref, out_ref):
    total = (a_ref[...] + b_ref[...]) + (c_ref[...] + d_ref[...])
    none = jnp.zeros((56, 128), f32)
    turned = [
        jnp.concatenate([total[ROWS * block : ROWS * block + ROWS], total[4 * ROWS :], none], axis=0).T
        for block in range(4)
    ]
    lane = lax.broadcasted_iota(jnp.int32, (SKY, 128), 1)
    for half in range(2):
        at = slice(SKY * half, SKY * half + SKY)
        spill = jnp.zeros((SKY, 128), f32)
        for c in range(4):
            block, first = 2 * half + c // 2, 64 * (c % 2)
            real = turned[block][first : first + SKY]
            imag = turned[block][first + SKY : first + 2 * SKY]
            out_ref[at, 0, 128 * c : 128 * c + 128] = jnp.where(
                lane < 64, real, pltpu.roll(imag, 64, 1)
            )
            for sub, part in ((c, real), (4 + c, imag)):
                up = (128 - 16 * sub) % 128
                down = (up + 63) % 128
                spill = jnp.where(lane == up, pltpu.roll(part, (up - 64 - block) % 128, 1), spill)
                spill = jnp.where(
                    lane == down, pltpu.roll(part, (down - 68 - block) % 128, 1), spill
                )
        out_ref[at, 0, 512:640] = spill


def turn(pieces):
    return pl.pallas_call(
        turn_kernel,
        out_shape=jax.ShapeDtypeStruct((64, 1, 640), f32),
        in_specs=[VM] * 4,
        out_specs=VM,
        compiler_params=limit(24),
        name="turn",
    )(*pieces)


def dft_32(values):
    even = [values[s] + values[32 - s] for s in range(1, 16)]
    odd = [values[s] - values[32 - s] for s in range(1, 16)]
    ends = [values[0] + values[16], values[0] - values[16]]
    cosine, sine = [None] * 17, [None] * 17
    for k in range(9):
        plain = ends[k % 2]
        turned = None
        for s in range(1, 16):
            term = float(np.cos(np.pi * k * s / 16)) * even[s - 1]
            if s % 2 == 0:
                plain = plain + term
            else:
                turned = term if turned is None else turned + term
        cosine[k] = plain + turned
        cosine[16 - k] = plain - turned
    for k in range(1, 9):
        plain, turned = None, None
        for s in range(1, 16):
            term = float(np.sin(np.pi * k * s / 16)) * odd[s - 1]
            if s % 2 == 0:
                plain = term if plain is None else plain + term
            else:
                turned = term if turned is None else turned + term
        sine[k] = turned + plain
        sine[16 - k] = turned - plain
    return cosine, sine


def solve_kernel(in_ref, cos_ref, sin_ref, high_table, low_table, out_ref):
    sky = lax.axis_index("sky")
    tile = 2 * lax.axis_index("x") + lax.axis_index("zhi")
    lane = lax.broadcasted_iota(jnp.int32, (8, 128), 1)
    sub = lax.broadcasted_iota(jnp.int32, (8, 128), 0)
    lower = lane < 64
    sign = jnp.where(sub < 4, 1.0, -1.0)
    first = jnp.logical_and(tile == 0, sky == 0)
    packed = jnp.logical_and(sub % 4 == 0, first)

    def swap(v):
        return pltpu.roll(v, 4, v.ndim - 2)

    def bent(v):
        return swap(v) * sign

    main, spill = [], []
    for s in range(SKY):
        rows = [
            jnp.broadcast_to(in_ref[s, :, lanes] + in_ref[SKY + s, :, lanes], (8, 128))
            for lanes in (slice(128 * c, 128 * c + 128) for c in range(5))
        ]
        v = rows[3]
        for c in range(3):
            v = jnp.where(sub % 4 == c, rows[c], v)
        main.append(jnp.where(sub < 4, v, pltpu.roll(v, 64, 1)))
        spill.append(pltpu.roll(rows[4], 0, 1, stride=16, stride_axis=0))
    values = []
    for s in range(SKY):
        up, down = spill[(s - 1) % SKY], spill[(s + 1) % SKY]
        v = main[s] + jnp.where(lane == 0, up, jnp.where(lane == 63, down, 0.0))
        v = jnp.where(lower, v, pltpu.roll(v, 64, 1))
        apart = jnp.where(sub == 4, 0.0, jnp.where(lower, v, swap(v)))
        values.append(jnp.where(packed, apart, v))
    cosine, sine = dft_32(values)
    spectrum = [None] * 32
    spectrum[0], spectrum[16] = cosine[0], cosine[16]
    for k in range(1, 16):
        turned = bent(sine[k])
        spectrum[k], spectrum[32 - k] = cosine[k] + turned, cosine[k] - turned
    twisted = [spectrum[k] * cos_ref[k] + swap(spectrum[k]) * sin_ref[k] for k in range(32)]
    rows = jnp.concatenate(twisted, axis=0)
    pair = dot3(rows, high_table[...], low_table[...])
    pair_c = pair[:, :128].reshape(32, 8, 128)
    pair_s = pair[:, 128:].reshape(32, 8, 128)

    k1 = lax.broadcasted_iota(jnp.int32, (32, 8, 128), 0)
    k2 = lax.broadcasted_iota(jnp.int32, (32, 8, 128), 2) % 64
    nx = k1 + 32 * k2
    nx = jnp.where(nx < N // 2, nx, nx - N)
    n = 4 * sky + sub % 4
    ny = jnp.where(tile > 0, tile + 16 * n, jnp.where(n < 64, 16 * n, 8 + 16 * (n - 64)))
    ny = jnp.where(ny < N // 2, ny, ny - N)
    ny = jnp.where(jnp.logical_and(packed, jnp.logical_not(lower)), -(N // 2), ny)
    along_x = jnp.logical_or(packed, lower)[None]
    squared = nx * nx + (ny * ny)[None]
    wave = jnp.where(along_x, jnp.where(nx == -(N // 2), 0, nx), ny[None])
    unit = 2.0 * np.pi / N
    scale = float(-2.0 / unit / 64.0 / N / N)
    factor = scale * wave.astype(f32) / jnp.maximum(squared, 1).astype(f32)
    kappa_hat = pair_c + swap(pair_s) * sign[None]
    field = factor * (swap(kappa_hat) * (-sign)[None])
    pair = dot3(field.reshape(256, 128), high_table[...], low_table[...])
    values = []
    for k in range(32):
        v = pair[8 * k : 8 * k + 8, :128] - bent(pair[8 * k : 8 * k + 8, 128:])
        values.append(v * cos_ref[k] - swap(v) * sin_ref[k])
    cosine, sine = dft_32(values)
    for s in range(17):
        turned = bent(sine[s]) if 0 < s < 16 else None
        for at in (s,) if turned is None else (s, 32 - s):
            v = cosine[s]
            if turned is not None:
                v = v - turned if at == s else v + turned
            other = swap(pltpu.roll(v, 64, 1))
            joined = jnp.where(lower, jnp.where(sub == 4, other, v), 0.0)
            v = jnp.where(packed, joined, v)
            out_ref[at] = v
            out_ref[SKY + at] = v


def solve(pieces, tables):
    return pl.pallas_call(
        solve_kernel,
        out_shape=jax.ShapeDtypeStruct((64, 8, 128), f32),
        in_specs=[VM] * 5,
        out_specs=VM,
        compiler_params=limit(24),
        name="solve",
    )(pieces, *tables)


def back_for(ahead, eighth_ref, plain, bent, high_table, low_table, out_ref):
    zhi, column = lax.axis_index("zhi"), lax.axis_index("x")
    target = (column + ahead) % 4
    parts = []
    for half in range(2):
        lanes = slice(256 * half, 256 * half + 256)
        turns = (2 * column + half) * (4 * zhi + target) % 8
        cosine, sine = eighth_ref[turns], eighth_ref[8 + turns]
        parts.append(cosine * plain[:, lanes] + sine * bent[:, lanes])
    value = stacked(jnp.concatenate(parts, axis=1))
    out_ref[...] = dot3_stacked(value, high_table[column], low_table[column])


def back_kernel(
    eighth_ref, in_ref, high_table, low_table, far_ref, next_ref, last_ref, plain_ref, bent_ref
):
    value = in_ref[...]
    sub = lax.broadcasted_iota(jnp.int32, (64, 8, 128), 1)
    bent = pltpu.roll(value, 4, 1) * jnp.where(sub < 4, -1.0, 1.0)
    plain, bent = value.reshape(512, 128).T, bent.reshape(512, 128).T
    plain_ref[...] = plain
    bent_ref[...] = bent
    back_for(2, eighth_ref, plain, bent, high_table, low_table, far_ref)
    back_for(1, eighth_ref, plain, bent, high_table, low_table, next_ref)
    back_for(3, eighth_ref, plain, bent, high_table, low_table, last_ref)


def back_rest_kernel(eighth_ref, plain_ref, bent_ref, high_table, low_table, own_ref):
    back_for(0, eighth_ref, plain_ref[...], bent_ref[...], high_table, low_table, own_ref)


def back(pieces, tables):
    turns = np.arange(8) * (2 * np.pi / 8)
    eighth = np.concatenate([np.cos(turns), np.sin(turns)]).astype(np.float32)
    piece = jax.ShapeDtypeStruct((128, 256), f32)
    held = jax.ShapeDtypeStruct((128, 512), f32)
    two, one, three, plain, bent = pl.pallas_call(
        back_kernel,
        out_shape=(piece, piece, piece, held, held),
        in_specs=[SM, VM, VM, VM],
        out_specs=(VM,) * 5,
        compiler_params=limit(24),
        name="back",
    )(eighth, pieces, *tables)
    own = pl.pallas_call(
        back_rest_kernel,
        out_shape=piece,
        in_specs=[SM] + [VM] * 4,
        out_specs=VM,
        compiler_params=limit(24),
        name="back_rest",
    )(eighth, plain, bent, *tables)
    return own, one, two, three


def final_kernel(a_ref, b_ref, c_ref, d_ref, x_ref, y_ref):
    total = (a_ref[...] + b_ref[...]) + (c_ref[...] + d_ref[...])
    x_ref[...] = total[:ROWS]
    y_ref[...] = total[ROWS:]


def final(pieces):
    shape = jax.ShapeDtypeStruct((ROWS, 256), f32)
    return pl.pallas_call(
        final_kernel,
        out_shape=(shape, shape),
        in_specs=[VM] * 4,
        out_specs=(VM, VM),
        compiler_params=limit(24),
        name="final",
    )(*pieces)


def deliver(pieces):
    return [pieces[0]] + [
        lax.ppermute(pieces[a], "x", [(i, (i + a) % 4) for i in range(4)]) for a in (2, 1, 3)
    ]


def body(density, refine, weight_low, weight_high):
    def swap(array, axes, pairs):
        return lax.ppermute(array, axes, pairs + [(b, a) for a, b in pairs])

    odd = lax.axis_index("x") % 2 == 1
    cross = lax.dynamic_slice_in_dim(density, jnp.where(odd, LAYERS - 1, 0), 1, 0)
    cross = swap(cross, LOS, [(3, 4)])
    row, other_row, layer, other_layer = edge_rows(density)
    layer = swap(layer, LOS, [(1, 2), (5, 6)])
    other_layer = swap(other_layer, LOS, [(0, 1), (2, 3), (4, 5), (6, 7)])
    row = swap(row, "sky", [(i, i + 1) for i in range(0, SKY, 2)])
    other_row = swap(other_row, "sky", [(i, (i + 1) % SKY) for i in range(1, SKY, 2)])
    inner = inner_sums(weight_low, weight_high, density, refine)
    tables = halves(forward_table())
    summed = outer_sums(
        weight_low, weight_high, density, (cross, layer, other_layer), (row, other_row), inner, tables
    )
    summed = deliver(summed)
    pieces = lax.all_to_all(turn(summed), ("zhi", "sky"), 0, 0, tiled=True)
    pieces = solve(pieces, twists() + halves(row_table()))
    pieces = lax.all_to_all(pieces, ("zhi", "sky"), 0, 0, tiled=True)
    fields = back(pieces, halves(inverse_table()))
    return final(deliver(fields))


def solution(mesh):
    devices = mesh.devices.reshape(2, 4, SKY)
    inner = Mesh(devices, ("zhi", "x", "sky"))
    placed = (P(LOS, "sky", None), P(LOS, "sky", None), P(LOS), P(LOS))
    return jax.shard_map(
        body,
        mesh=inner,
        in_specs=placed,
        out_specs=(P("sky", LOS), P("sky", LOS)),
        check_vma=False,
    )
```

```python
import functools

import jax
import jax.numpy as jnp
import ml_dtypes
import numpy as np
from jax import lax
from jax.experimental import pallas as pl
from jax.experimental.pallas import tpu as pltpu
from jax.sharding import Mesh, PartitionSpec as P

f32 = jnp.float32
bf16 = jnp.bfloat16
N = 2048
ROWS = 64
SKY = 32
LAYERS = 8
LOS = ("zhi", "x")
MB = 1024 * 1024


def halves(table):
    high = table.astype(np.float32).astype(ml_dtypes.bfloat16)
    low = (table - high.astype(np.float64)).astype(np.float32).astype(ml_dtypes.bfloat16)
    return high, low


def tile_modes(tile):
    n = np.arange(128)
    if tile:
        return tile + 16 * n
    return np.where(n < 64, 16 * n, 8 + 16 * (n - 64))


def tile_order(real, imag):
    pair = np.stack([real.reshape(SKY, 4, -1), imag.reshape(SKY, 4, -1)], axis=1)
    return pair.reshape(256, -1)


def tile_groups(real, imag):
    pair = np.stack([real.reshape(SKY, 4, -1), imag.reshape(SKY, 4, -1)], axis=1)
    return pair.transpose(2, 1, 0, 3).reshape(256, -1)


def forward_table():
    b = np.arange(128)
    tiles = []
    for tile in range(8):
        angle = (tile_modes(tile)[:, None] * b[None, :] % N) * (2 * np.pi / N)
        cosine, sine = np.cos(angle), np.sin(angle)
        if tile:
            real = np.concatenate([cosine, sine], 1)
            imag = np.concatenate([-sine, cosine], 1)
        else:
            zero = np.zeros((64, 128))
            real = np.block([[cosine[:64], zero], [zero, cosine[64:]]])
            imag = np.block([[-sine[:64], zero], [zero, -sine[64:]]])
            imag[0, :128] = (-1.0) ** b
        tiles.append(tile_groups(real, imag).T)
    return np.stack(tiles)


def inverse_table():
    j = np.arange(256)
    tiles = []
    for tile in range(8):
        angle = (tile_modes(tile)[:, None] * j[None, :] % N) * (2 * np.pi / N)
        real, imag = 2 * np.cos(angle), -2 * np.sin(angle)
        if not tile:
            real[0] = 1.0
            imag[0] = (-1.0) ** j
        tiles.append(tile_order(real, imag))
    return np.stack(tiles).reshape(4, 512, 256)


def row_table():
    r = np.arange(64)
    angle = (r[:, None] * r[None, :] % 64) * (2 * np.pi / 64)
    both = np.eye(2)
    return np.concatenate([np.kron(both, np.cos(angle)), np.kron(both, np.sin(angle))], 1)


def twists():
    angle = (np.arange(32)[:, None] * (np.arange(128) % 64)[None, :]) * (2 * np.pi / N)
    sign = np.where(np.arange(8) < 4, 1.0, -1.0)
    cosine = np.broadcast_to(np.cos(angle)[:, None, :], (32, 8, 128))
    sine = np.sin(angle)[:, None, :] * sign[None, :, None]
    return cosine.astype(np.float32), sine.astype(np.float32)


def minmod(a, b):
    return jnp.maximum(jnp.minimum(a, b), 0.0) + jnp.minimum(jnp.maximum(a, b), 0.0)


def split(value):
    high = value.astype(bf16)
    return high, (value - high.astype(f32)).astype(bf16)


def dot3(value, high_table, low_table):
    high, low = split(value)
    dot = functools.partial(jnp.dot, preferred_element_type=f32)
    return dot(high, high_table) + (dot(low, high_table) + dot(high, low_table))


def stacked(value):
    return jnp.concatenate(split(value), axis=0)


def dot3_stacked(parts, high_table, low_table):
    rows = parts.shape[0] // 2
    dot = functools.partial(jnp.dot, preferred_element_type=f32)
    both = dot(parts, high_table)
    return both[:rows] + (both[rows:] + dot(parts[:rows], low_table))


def limit(mib):
    return pltpu.CompilerParams(vmem_limit_bytes=mib * MB)


VM = pl.BlockSpec(memory_space=pltpu.VMEM)
SM = pl.BlockSpec(memory_space=pltpu.SMEM)


def rows_kernel(d_ref, near_ref, far_ref, layer_ref, other_layer_ref):
    odd = lax.axis_index("x") % 2
    layer_ref[0] = d_ref[(LAYERS - 1) * odd]
    other_layer_ref[0] = d_ref[(LAYERS - 1) * (1 - odd)]
    even = lax.axis_index("sky") % 2 == 0
    for z in range(LAYERS):
        first = d_ref[z, 0:16, :].astype(f32)[0:1]
        last = d_ref[z, 48:64, :].astype(f32)[15:16]
        near_ref[z : z + 1, :] = jnp.where(even, last, first)
        far_ref[z : z + 1, :] = jnp.where(even, first, last)


def edge_rows(density):
    shape = jax.ShapeDtypeStruct((LAYERS, N), f32)
    return pl.pallas_call(
        rows_kernel,
        out_shape=(shape, shape) + (jax.ShapeDtypeStruct((1, ROWS, N), bf16),) * 2,
        in_specs=[VM],
        out_specs=(VM,) * 4,
        compiler_params=limit(8),
        name="edge_rows",
    )(density)


def longer(field):
    return jnp.concatenate([field, jnp.zeros((8, N), f32)], axis=0)


def smooth_y(field):
    return 0.75 * field + 0.125 * (pltpu.roll(field, 1, 1) + pltpu.roll(field, N - 1, 1))


CHUNK = 512


def inner_kernel(
    low_ref,
    high_ref,
    d_ref,
    refine_ref,
    kappa_ref,
    mask_ref,
    near_ref,
    calm_ref,
    lifted_ref,
    tx_ref,
    ty_ref,
):
    block = lax.broadcasted_iota(jnp.int32, (256, N), 0)
    lane = lax.broadcasted_iota(jnp.int32, (256, N), 1)
    grow = jnp.where(lane // 8 == block, 1.0, 0.0).astype(bf16)
    coarse = refine_ref[0].astype(f32).astype(bf16)
    mask_ref[...] = jnp.dot(coarse, grow, preferred_element_type=f32)
    for z in range(LAYERS):
        first = d_ref[z, 0:16, :].astype(f32)
        last = d_ref[z, 48:64, :].astype(f32)
        near_ref[0, z : z + 1, :] = first[0:1]
        near_ref[1, z : z + 1, :] = first[1:2]
        near_ref[2, z : z + 1, :] = last[14:15]
        near_ref[3, z : z + 1, :] = last[15:16]

    wide = CHUNK + 256
    row = lax.broadcasted_iota(jnp.int32, (ROWS, CHUNK), 0)
    inside = jnp.logical_and(row > 0, row < ROWS - 1)

    def chunk(i, carry):
        start = pl.multiple_of(i * CHUNK, CHUNK)
        left = pl.multiple_of((start + N - 128) % N, 128)
        right = pl.multiple_of((start + CHUNK) % N, 128)
        base = jnp.zeros((ROWS, CHUNK), f32)
        tz, tx, ty = base, base, base
        centre, step = None, None
        for z in range(LAYERS):
            average = 0.5 * (low_ref[z] + high_ref[z])
            former = centre
            around = jnp.concatenate(
                [
                    d_ref[z, :, pl.ds(left, 128)],
                    d_ref[z, :, pl.ds(start, CHUNK)],
                    d_ref[z, :, pl.ds(right, 128)],
                ],
                axis=1,
            ).astype(f32)
            centre = around[:, 128 : 128 + CHUNK]
            base = base + average * centre
            dy = pltpu.roll(around, wide - 1, 1) - around
            gy = minmod(dy, pltpu.roll(dy, 1, 1))[:, 128 : 128 + CHUNK]
            ty = ty + average * gy
            dx = pltpu.roll(centre, ROWS - 1, 0) - centre
            tx = tx + average * minmod(dx, pltpu.roll(dx, 1, 0))
            if z > 0:
                latter = centre - former
                if step is not None:
                    slope = 0.125 * (high_ref[z - 1] - low_ref[z - 1])
                    tz = tz + slope * minmod(latter, step)
                step = latter
        marked = mask_ref[:, pl.ds(start, CHUNK)]
        marked = jnp.broadcast_to(marked[:, None, :], (8, 8, CHUNK)).reshape(ROWS, CHUNK)
        at = pl.ds(start, CHUNK)
        calm_ref[:, at] = base - marked * base
        lifted_ref[:, at] = marked * (base + tz)
        tx_ref[:, at] = jnp.where(inside, marked * tx, 0.0)
        ty_ref[:, at] = marked * ty
        return carry

    lax.fori_loop(0, N // CHUNK, chunk, 0)
    lifted, tx = lifted_ref[...], tx_ref[...]
    eighth, tilt = 0.125 * lifted, ty_ref[...] * (1.0 / 32.0)
    smooth = 0.75 * lifted + pltpu.roll(eighth + tilt, 1, 1) + pltpu.roll(eighth - tilt, N - 1, 1)
    eighth, tilt = 0.125 * smooth, smooth_y(tx) * (1.0 / 32.0)
    kappa_ref[...] = (
        longer(calm_ref[...] + 0.75 * smooth)
        + pltpu.roll(longer(eighth + tilt), 1, 0)
        + pltpu.roll(longer(eighth - tilt), ROWS + 7, 0)
    )


def inner_sums(low, high, density, refine):
    return pl.pallas_call(
        inner_kernel,
        out_shape=(
            jax.ShapeDtypeStruct((ROWS + 8, N), f32),
            jax.ShapeDtypeStruct((8, N), f32),
            jax.ShapeDtypeStruct((4, LAYERS, N), f32),
        ),
        in_specs=[SM, SM, VM, VM],
        out_specs=(VM,) * 3,
        scratch_shapes=[pltpu.VMEM((ROWS, N), f32)] * 4,
        compiler_params=limit(40),
        cost_estimate=pl.CostEstimate(flops=40_000_000, bytes_accessed=24 * MB, transcendentals=0),
        name="inner_sums",
    )(low, high, density, refine)


def outer_kernel(
    low_ref,
    high_ref,
    d_ref,
    cross_ref,
    layer_ref,
    other_layer_ref,
    row_ref,
    other_row_ref,
    kappa_ref,
    mask_ref,
    near_ref,
    high_table,
    low_table,
    far_ref,
    next_ref,
    last_ref,
    part_ref,
):
    los = lax.axis_index("zhi") * 4 + lax.axis_index("x")
    v0, v1 = d_ref[0].astype(f32), d_ref[1].astype(f32)
    v6, v7 = d_ref[6].astype(f32), d_ref[7].astype(f32)
    odd = los % 2 == 1
    crossing = jnp.logical_or(los == 3, los == 4)
    one = jnp.where(crossing, cross_ref[0], layer_ref[0]).astype(f32)
    other = other_layer_ref[0].astype(f32)
    below = jnp.where(los == 0, v0, jnp.where(odd, other, one))
    above = jnp.where(los == 7, v7, jnp.where(odd, one, other))
    slope0 = 0.125 * (high_ref[0] - low_ref[0])
    slope7 = 0.125 * (high_ref[7] - low_ref[7])
    tz = slope0 * minmod(v1 - v0, v0 - below) + slope7 * minmod(above - v7, v7 - v6)
    mask = mask_ref[...]
    marked = jnp.broadcast_to(mask[:, None, :], (8, 8, N)).reshape(ROWS, N)
    smooth = smooth_y(marked * tz)
    layer = lax.broadcasted_iota(jnp.int32, (LAYERS, 1), 0)
    average = jnp.zeros((LAYERS, 1), f32)
    for z in range(LAYERS):
        average = jnp.where(layer == z, 0.5 * (low_ref[z] + high_ref[z]), average)
    r0, r1, r62, r63 = near_ref[0], near_ref[1], near_ref[2], near_ref[3]
    even = lax.axis_index("sky") % 2 == 0
    before = jnp.where(even, other_row_ref[...], row_ref[...])
    after = jnp.where(even, row_ref[...], other_row_ref[...])
    e0 = jnp.sum(average * minmod(r1 - r0, r0 - before), axis=0, keepdims=True)
    e63 = jnp.sum(average * minmod(after - r63, r63 - r62), axis=0, keepdims=True)
    row = lax.broadcasted_iota(jnp.int32, (8, N), 0)
    e0 = smooth_y(jnp.where(row == 0, mask[0:1] * e0, 0.0)) * (1.0 / 32.0)
    e63 = smooth_y(jnp.where(row == 7, mask[7:8] * e63, 0.0)) * (1.0 / 32.0)
    first = pltpu.roll(e0, 1, 0)
    last = pltpu.roll(e63, 7, 0)
    spill = jnp.where(row == 0, pltpu.roll(e63, 1, 0), -pltpu.roll(e0, 7, 0))
    sides = jnp.concatenate([first, jnp.zeros((ROWS - 16, N), f32), -last, spill], axis=0)
    eighth = longer(0.125 * smooth)
    kappa = (
        (kappa_ref[...] + sides)
        + longer(0.75 * smooth)
        + (pltpu.roll(eighth, 1, 0) + pltpu.roll(eighth, ROWS + 7, 0))
    )
    part = [kappa[:, 128 * a : 128 * a + 128] for a in range(16)]
    even = [part[a] + part[16 - a] for a in range(1, 8)]
    odd = [part[a] - part[16 - a] for a in range(1, 8)]

    def weigh(pairs):
        total = None
        for factor, value in pairs:
            if abs(factor) < 1e-9:
                continue
            term = value if abs(factor - 1) < 1e-9 else factor * value
            total = term if total is None else total + term
        return total

    def cosines(k):
        first = part[0] + part[8] if k % 2 == 0 else part[0] - part[8]
        return first + weigh((float(np.cos(np.pi * k * a / 8)), even[a - 1]) for a in range(1, 8))

    def sines(k):
        return weigh((float(-np.sin(np.pi * k * a / 8)), odd[a - 1]) for a in range(1, 8))

    for tile in range(8):
        second = sines(tile) if tile else cosines(8)
        value = jnp.concatenate([cosines(tile), second], axis=1)
        value = jnp.concatenate([value, jnp.zeros((8, 256), f32)], axis=0)
        part_ref[tile] = stacked(value)
    transform_for(2, part_ref, high_table, low_table, far_ref)
    transform_for(1, part_ref, high_table, low_table, next_ref)
    transform_for(3, part_ref, high_table, low_table, last_ref)


def transform_for(ahead, part_ref, high_table, low_table, out_ref):
    target = (lax.axis_index("x") + ahead) % 4
    for half in range(2):
        tile = 2 * target + half
        value = dot3_stacked(part_ref[tile], high_table[tile], low_table[tile])
        for block in (2 * half, 2 * half + 1):
            part = value[:, 128 * (block % 2) : 128 * (block % 2) + 128]
            out_ref[ROWS * block : ROWS * block + ROWS] = part[:ROWS]
            out_ref[4 * ROWS + block : 4 * ROWS + block + 1] = part[ROWS : ROWS + 1]
            out_ref[4 * ROWS + 4 + block : 4 * ROWS + 5 + block] = part[ROWS + 7 : ROWS + 8]


def rest_kernel(part_ref, high_table, low_table, own_ref):
    transform_for(0, part_ref, high_table, low_table, own_ref)


def outer_sums(low, high, density, layers, rows, inner, tables):
    piece = jax.ShapeDtypeStruct((4 * ROWS + 8, 128), f32)
    two, one, three, parts = pl.pallas_call(
        outer_kernel,
        out_shape=(piece, piece, piece, jax.ShapeDtypeStruct((8, 160, 256), bf16)),
        in_specs=[SM, SM] + [VM] * 11,
        out_specs=(VM,) * 4,
        compiler_params=limit(32),
        name="outer_sums",
    )(low, high, density, *layers, *rows, *inner, *tables)
    own = pl.pallas_call(
        rest_kernel,
        out_shape=piece,
        in_specs=[VM] * 3,
        out_specs=VM,
        compiler_params=limit(24),
        name="other_sums",
    )(parts, *tables)
    return own, one, two, three


def turn_kernel(a_ref, b_ref, c_ref, d_ref, out_ref):
    total = (a_ref[...] + b_ref[...]) + (c_ref[...] + d_ref[...])
    none = jnp.zeros((56, 128), f32)
    turned = [
        jnp.concatenate([total[ROWS * block : ROWS * block + ROWS], total[4 * ROWS :], none], axis=0).T
        for block in range(4)
    ]
    lane = lax.broadcasted_iota(jnp.int32, (SKY, 128), 1)
    for half in range(2):
        at = slice(SKY * half, SKY * half + SKY)
        spill = jnp.zeros((SKY, 128), f32)
        for c in range(4):
            block, first = 2 * half + c // 2, 64 * (c % 2)
            real = turned[block][first : first + SKY]
            imag = turned[block][first + SKY : first + 2 * SKY]
            out_ref[at, 0, 128 * c : 128 * c + 128] = jnp.where(
                lane < 64, real, pltpu.roll(imag, 64, 1)
            )
            for sub, part in ((c, real), (4 + c, imag)):
                up = (128 - 16 * sub) % 128
                down = (up + 63) % 128
                spill = jnp.where(lane == up, pltpu.roll(part, (up - 64 - block) % 128, 1), spill)
                spill = jnp.where(
                    lane == down, pltpu.roll(part, (down - 68 - block) % 128, 1), spill
                )
        out_ref[at, 0, 512:640] = spill


def turn(pieces):
    return pl.pallas_call(
        turn_kernel,
        out_shape=jax.ShapeDtypeStruct((64, 1, 640), f32),
        in_specs=[VM] * 4,
        out_specs=VM,
        compiler_params=limit(24),
        name="turn",
    )(*pieces)


def dft_32(values):
    even = [values[s] + values[32 - s] for s in range(1, 16)]
    odd = [values[s] - values[32 - s] for s in range(1, 16)]
    ends = [values[0] + values[16], values[0] - values[16]]
    cosine, sine = [None] * 17, [None] * 17
    for k in range(9):
        plain = ends[k % 2]
        turned = None
        for s in range(1, 16):
            term = float(np.cos(np.pi * k * s / 16)) * even[s - 1]
            if s % 2 == 0:
                plain = plain + term
            else:
                turned = term if turned is None else turned + term
        cosine[k] = plain + turned
        cosine[16 - k] = plain - turned
    for k in range(1, 9):
        plain, turned = None, None
        for s in range(1, 16):
            term = float(np.sin(np.pi * k * s / 16)) * odd[s - 1]
            if s % 2 == 0:
                plain = term if plain is None else plain + term
            else:
                turned = term if turned is None else turned + term
        sine[k] = turned + plain
        sine[16 - k] = turned - plain
    return cosine, sine


def solve_kernel(in_ref, cos_ref, sin_ref, high_table, low_table, out_ref):
    sky = lax.axis_index("sky")
    tile = 2 * lax.axis_index("x") + lax.axis_index("zhi")
    lane = lax.broadcasted_iota(jnp.int32, (8, 128), 1)
    sub = lax.broadcasted_iota(jnp.int32, (8, 128), 0)
    lower = lane < 64
    sign = jnp.where(sub < 4, 1.0, -1.0)
    first = jnp.logical_and(tile == 0, sky == 0)
    packed = jnp.logical_and(sub % 4 == 0, first)

    def swap(v):
        return pltpu.roll(v, 4, v.ndim - 2)

    def bent(v):
        return swap(v) * sign

    main, spill = [], []
    for s in range(SKY):
        rows = [
            jnp.broadcast_to(in_ref[s, :, lanes] + in_ref[SKY + s, :, lanes], (8, 128))
            for lanes in (slice(128 * c, 128 * c + 128) for c in range(5))
        ]
        v = rows[3]
        for c in range(3):
            v = jnp.where(sub % 4 == c, rows[c], v)
        main.append(jnp.where(sub < 4, v, pltpu.roll(v, 64, 1)))
        spill.append(pltpu.roll(rows[4], 0, 1, stride=16, stride_axis=0))
    values = []
    for s in range(SKY):
        up, down = spill[(s - 1) % SKY], spill[(s + 1) % SKY]
        v = main[s] + jnp.where(lane == 0, up, jnp.where(lane == 63, down, 0.0))
        v = jnp.where(lower, v, pltpu.roll(v, 64, 1))
        apart = jnp.where(sub == 4, 0.0, jnp.where(lower, v, swap(v)))
        values.append(jnp.where(packed, apart, v))
    cosine, sine = dft_32(values)
    spectrum = [None] * 32
    spectrum[0], spectrum[16] = cosine[0], cosine[16]
    for k in range(1, 16):
        turned = bent(sine[k])
        spectrum[k], spectrum[32 - k] = cosine[k] + turned, cosine[k] - turned
    twisted = [spectrum[k] * cos_ref[k] + swap(spectrum[k]) * sin_ref[k] for k in range(32)]
    rows = jnp.concatenate(twisted, axis=0)
    pair = dot3(rows, high_table[...], low_table[...])
    pair_c = pair[:, :128].reshape(32, 8, 128)
    pair_s = pair[:, 128:].reshape(32, 8, 128)

    k1 = lax.broadcasted_iota(jnp.int32, (32, 8, 128), 0)
    k2 = lax.broadcasted_iota(jnp.int32, (32, 8, 128), 2) % 64
    nx = k1 + 32 * k2
    nx = jnp.where(nx < N // 2, nx, nx - N)
    n = 4 * sky + sub % 4
    ny = jnp.where(tile > 0, tile + 16 * n, jnp.where(n < 64, 16 * n, 8 + 16 * (n - 64)))
    ny = jnp.where(ny < N // 2, ny, ny - N)
    ny = jnp.where(jnp.logical_and(packed, jnp.logical_not(lower)), -(N // 2), ny)
    along_x = jnp.logical_or(packed, lower)[None]
    squared = nx * nx + (ny * ny)[None]
    wave = jnp.where(along_x, jnp.where(nx == -(N // 2), 0, nx), ny[None])
    unit = 2.0 * np.pi / N
    scale = float(-2.0 / unit / 64.0 / N / N)
    factor = scale * wave.astype(f32) / jnp.maximum(squared, 1).astype(f32)
    kappa_hat = pair_c + swap(pair_s) * sign[None]
    field = factor * (swap(kappa_hat) * (-sign)[None])
    pair = dot3(field.reshape(256, 128), high_table[...], low_table[...])
    values = []
    for k in range(32):
        v = pair[8 * k : 8 * k + 8, :128] - bent(pair[8 * k : 8 * k + 8, 128:])
        values.append(v * cos_ref[k] - swap(v) * sin_ref[k])
    cosine, sine = dft_32(values)
    for s in range(17):
        turned = bent(sine[s]) if 0 < s < 16 else None
        for at in (s,) if turned is None else (s, 32 - s):
            v = cosine[s]
            if turned is not None:
                v = v - turned if at == s else v + turned
            other = swap(pltpu.roll(v, 64, 1))
            joined = jnp.where(lower, jnp.where(sub == 4, other, v), 0.0)
            v = jnp.where(packed, joined, v)
            out_ref[at] = v
            out_ref[SKY + at] = v


def solve(pieces, tables):
    return pl.pallas_call(
        solve_kernel,
        out_shape=jax.ShapeDtypeStruct((64, 8, 128), f32),
        in_specs=[VM] * 5,
        out_specs=VM,
        compiler_params=limit(24),
        name="solve",
    )(pieces, *tables)


def back_for(ahead, eighth_ref, plain, bent, high_table, low_table, out_ref):
    zhi, column = lax.axis_index("zhi"), lax.axis_index("x")
    target = (column + ahead) % 4
    parts = []
    for half in range(2):
        lanes = slice(256 * half, 256 * half + 256)
        turns = (2 * column + half) * (4 * zhi + target) % 8
        cosine, sine = eighth_ref[turns], eighth_ref[8 + turns]
        parts.append(cosine * plain[:, lanes] + sine * bent[:, lanes])
    value = stacked(jnp.concatenate(parts, axis=1))
    out_ref[...] = dot3_stacked(value, high_table[column], low_table[column])


def back_kernel(
    eighth_ref, in_ref, high_table, low_table, far_ref, next_ref, last_ref, plain_ref, bent_ref
):
    value = in_ref[...]
    sub = lax.broadcasted_iota(jnp.int32, (64, 8, 128), 1)
    bent = pltpu.roll(value, 4, 1) * jnp.where(sub < 4, -1.0, 1.0)
    plain, bent = value.reshape(512, 128).T, bent.reshape(512, 128).T
    plain_ref[...] = plain
    bent_ref[...] = bent
    back_for(2, eighth_ref, plain, bent, high_table, low_table, far_ref)
    back_for(1, eighth_ref, plain, bent, high_table, low_table, next_ref)
    back_for(3, eighth_ref, plain, bent, high_table, low_table, last_ref)


def back_rest_kernel(eighth_ref, plain_ref, bent_ref, high_table, low_table, own_ref):
    back_for(0, eighth_ref, plain_ref[...], bent_ref[...], high_table, low_table, own_ref)


def back(pieces, tables):
    turns = np.arange(8) * (2 * np.pi / 8)
    eighth = np.concatenate([np.cos(turns), np.sin(turns)]).astype(np.float32)
    piece = jax.ShapeDtypeStruct((128, 256), f32)
    held = jax.ShapeDtypeStruct((128, 512), f32)
    two, one, three, plain, bent = pl.pallas_call(
        back_kernel,
        out_shape=(piece, piece, piece, held, held),
        in_specs=[SM, VM, VM, VM],
        out_specs=(VM,) * 5,
        compiler_params=limit(24),
        name="back",
    )(eighth, pieces, *tables)
    own = pl.pallas_call(
        back_rest_kernel,
        out_shape=piece,
        in_specs=[SM] + [VM] * 4,
        out_specs=VM,
        compiler_params=limit(24),
        name="back_rest",
    )(eighth, plain, bent, *tables)
    return own, one, two, three


def final_kernel(a_ref, b_ref, c_ref, d_ref, x_ref, y_ref):
    total = (a_ref[...] + b_ref[...]) + (c_ref[...] + d_ref[...])
    x_ref[...] = total[:ROWS]
    y_ref[...] = total[ROWS:]


def final(pieces):
    shape = jax.ShapeDtypeStruct((ROWS, 256), f32)
    return pl.pallas_call(
        final_kernel,
        out_shape=(shape, shape),
        in_specs=[VM] * 4,
        out_specs=(VM, VM),
        compiler_params=limit(24),
        name="final",
    )(*pieces)


def deliver(pieces):
    return [pieces[0]] + [
        lax.ppermute(pieces[a], "x", [(i, (i + a) % 4) for i in range(4)]) for a in (2, 1, 3)
    ]


def body(density, refine, weight_low, weight_high):
    def swap(array, axes, pairs):
        return lax.ppermute(array, axes, pairs + [(b, a) for a, b in pairs])

    def swap(array, axes, pairs):
        return lax.ppermute(array, axes, pairs + [(b, a) for a, b in pairs])

    row, other_row, layer, other_layer = edge_rows(density)
    other_layer = swap(other_layer, LOS, [(0, 1), (2, 3), (4, 5), (6, 7)])
    cross = swap(layer, LOS, [(3, 4)])
    layer = swap(layer, LOS, [(1, 2), (5, 6)])
    row = swap(row, "sky", [(i, i + 1) for i in range(0, SKY, 2)])
    other_row = swap(other_row, "sky", [(i, (i + 1) % SKY) for i in range(1, SKY, 2)])
    inner = inner_sums(weight_low, weight_high, density, refine)
    tables = halves(forward_table())
    summed = outer_sums(
        weight_low, weight_high, density, (cross, layer, other_layer), (row, other_row), inner, tables
    )
    summed = deliver(summed)
    pieces = lax.all_to_all(turn(summed), ("zhi", "sky"), 0, 0, tiled=True)
    pieces = solve(pieces, twists() + halves(row_table()))
    pieces = lax.all_to_all(pieces, ("zhi", "sky"), 0, 0, tiled=True)
    fields = back(pieces, halves(inverse_table()))
    return final(deliver(fields))


def solution(mesh):
    devices = mesh.devices.reshape(2, 4, SKY)
    inner = Mesh(devices, ("zhi", "x", "sky"))
    placed = (P(LOS, "sky", None), P(LOS, "sky", None), P(LOS), P(LOS))
    return jax.shard_map(
        body,
        mesh=inner,
        in_specs=placed,
        out_specs=(P("sky", LOS), P("sky", LOS)),
        check_vma=False,
    )
```

```python
import functools

import jax
import jax.numpy as jnp
import ml_dtypes
import numpy as np
from jax import lax
from jax.experimental import pallas as pl
from jax.experimental.pallas import tpu as pltpu
from jax.sharding import Mesh, PartitionSpec as P

f32 = jnp.float32
bf16 = jnp.bfloat16
N = 2048
ROWS = 64
SKY = 32
LAYERS = 8
LOS = ("zhi", "x")
MB = 1024 * 1024


def halves(table):
    high = table.astype(np.float32).astype(ml_dtypes.bfloat16)
    low = (table - high.astype(np.float64)).astype(np.float32).astype(ml_dtypes.bfloat16)
    return high, low


def tile_modes(tile):
    n = np.arange(128)
    if tile:
        return tile + 16 * n
    return np.where(n < 64, 16 * n, 8 + 16 * (n - 64))


def tile_order(real, imag):
    pair = np.stack([real.reshape(SKY, 4, -1), imag.reshape(SKY, 4, -1)], axis=1)
    return pair.reshape(256, -1)


def tile_groups(real, imag):
    pair = np.stack([real.reshape(SKY, 4, -1), imag.reshape(SKY, 4, -1)], axis=1)
    return pair.transpose(2, 1, 0, 3).reshape(256, -1)


def forward_table():
    b = np.arange(128)
    tiles = []
    for tile in range(8):
        angle = (tile_modes(tile)[:, None] * b[None, :] % N) * (2 * np.pi / N)
        cosine, sine = np.cos(angle), np.sin(angle)
        if tile:
            real = np.concatenate([cosine, sine], 1)
            imag = np.concatenate([-sine, cosine], 1)
        else:
            zero = np.zeros((64, 128))
            real = np.block([[cosine[:64], zero], [zero, cosine[64:]]])
            imag = np.block([[-sine[:64], zero], [zero, -sine[64:]]])
            imag[0, :128] = (-1.0) ** b
        tiles.append(tile_groups(real, imag).T)
    return np.stack(tiles)


def inverse_table():
    j = np.arange(256)
    tiles = []
    for tile in range(8):
        angle = (tile_modes(tile)[:, None] * j[None, :] % N) * (2 * np.pi / N)
        real, imag = 2 * np.cos(angle), -2 * np.sin(angle)
        if not tile:
            real[0] = 1.0
            imag[0] = (-1.0) ** j
        tiles.append(tile_order(real, imag))
    return np.stack(tiles).reshape(4, 512, 256)


def row_table():
    r = np.arange(64)
    angle = (r[:, None] * r[None, :] % 64) * (2 * np.pi / 64)
    both = np.eye(2)
    return np.concatenate([np.kron(both, np.cos(angle)), np.kron(both, np.sin(angle))], 1)


def twists():
    angle = (np.arange(32)[:, None] * (np.arange(128) % 64)[None, :]) * (2 * np.pi / N)
    sign = np.where(np.arange(8) < 4, 1.0, -1.0)
    cosine = np.broadcast_to(np.cos(angle)[:, None, :], (32, 8, 128))
    sine = np.sin(angle)[:, None, :] * sign[None, :, None]
    return cosine.astype(np.float32), sine.astype(np.float32)


def minmod(a, b):
    return jnp.maximum(jnp.minimum(a, b), 0.0) + jnp.minimum(jnp.maximum(a, b), 0.0)


def split(value):
    high = value.astype(bf16)
    return high, (value - high.astype(f32)).astype(bf16)


def dot3(value, high_table, low_table):
    high, low = split(value)
    dot = functools.partial(jnp.dot, preferred_element_type=f32)
    return dot(high, high_table) + (dot(low, high_table) + dot(high, low_table))


def stacked(value):
    return jnp.concatenate(split(value), axis=0)


def dot3_stacked(parts, high_table, low_table):
    rows = parts.shape[0] // 2
    dot = functools.partial(jnp.dot, preferred_element_type=f32)
    both = dot(parts, high_table)
    return both[:rows] + (both[rows:] + dot(parts[:rows], low_table))


def limit(mib):
    return pltpu.CompilerParams(vmem_limit_bytes=mib * MB)


VM = pl.BlockSpec(memory_space=pltpu.VMEM)
SM = pl.BlockSpec(memory_space=pltpu.SMEM)


def rows_kernel(d_ref, near_ref, far_ref, layer_ref, other_layer_ref):
    odd = lax.axis_index("x") % 2
    layer_ref[0] = d_ref[(LAYERS - 1) * odd]
    other_layer_ref[0] = d_ref[(LAYERS - 1) * (1 - odd)]
    even = lax.axis_index("sky") % 2 == 0
    for z in range(LAYERS):
        first = d_ref[z, 0:16, :].astype(f32)[0:1]
        last = d_ref[z, 48:64, :].astype(f32)[15:16]
        near_ref[z : z + 1, :] = jnp.where(even, last, first)
        far_ref[z : z + 1, :] = jnp.where(even, first, last)


def edge_rows(density):
    shape = jax.ShapeDtypeStruct((LAYERS, N), f32)
    return pl.pallas_call(
        rows_kernel,
        out_shape=(shape, shape) + (jax.ShapeDtypeStruct((1, ROWS, N), bf16),) * 2,
        in_specs=[VM],
        out_specs=(VM,) * 4,
        compiler_params=limit(8),
        name="edge_rows",
    )(density)


def longer(field):
    return jnp.concatenate([field, jnp.zeros((8, N), f32)], axis=0)


def smooth_y(field):
    return 0.75 * field + 0.125 * (pltpu.roll(field, 1, 1) + pltpu.roll(field, N - 1, 1))


CHUNK = 512


def inner_kernel(
    low_ref,
    high_ref,
    d_ref,
    refine_ref,
    kappa_ref,
    mask_ref,
    near_ref,
    calm_ref,
    lifted_ref,
    tx_ref,
    ty_ref,
):
    block = lax.broadcasted_iota(jnp.int32, (256, N), 0)
    lane = lax.broadcasted_iota(jnp.int32, (256, N), 1)
    grow = jnp.where(lane // 8 == block, 1.0, 0.0).astype(bf16)
    coarse = refine_ref[0].astype(f32).astype(bf16)
    mask_ref[...] = jnp.dot(coarse, grow, preferred_element_type=f32)
    for z in range(LAYERS):
        first = d_ref[z, 0:16, :].astype(f32)
        last = d_ref[z, 48:64, :].astype(f32)
        near_ref[0, z : z + 1, :] = first[0:1]
        near_ref[1, z : z + 1, :] = first[1:2]
        near_ref[2, z : z + 1, :] = last[14:15]
        near_ref[3, z : z + 1, :] = last[15:16]

    wide = CHUNK + 256
    row = lax.broadcasted_iota(jnp.int32, (ROWS, CHUNK), 0)
    inside = jnp.logical_and(row > 0, row < ROWS - 1)

    def chunk(i, carry):
        start = pl.multiple_of(i * CHUNK, CHUNK)
        left = pl.multiple_of((start + N - 128) % N, 128)
        right = pl.multiple_of((start + CHUNK) % N, 128)
        base = jnp.zeros((ROWS, CHUNK), f32)
        tz, tx, ty = base, base, base
        centre, step = None, None
        for z in range(LAYERS):
            average = 0.5 * (low_ref[z] + high_ref[z])
            former = centre
            around = jnp.concatenate(
                [
                    d_ref[z, :, pl.ds(left, 128)],
                    d_ref[z, :, pl.ds(start, CHUNK)],
                    d_ref[z, :, pl.ds(right, 128)],
                ],
                axis=1,
            ).astype(f32)
            centre = around[:, 128 : 128 + CHUNK]
            base = base + average * centre
            dy = pltpu.roll(around, wide - 1, 1) - around
            gy = minmod(dy, pltpu.roll(dy, 1, 1))[:, 128 : 128 + CHUNK]
            ty = ty + average * gy
            dx = pltpu.roll(centre, ROWS - 1, 0) - centre
            tx = tx + average * minmod(dx, pltpu.roll(dx, 1, 0))
            if z > 0:
                latter = centre - former
                if step is not None:
                    slope = 0.125 * (high_ref[z - 1] - low_ref[z - 1])
                    tz = tz + slope * minmod(latter, step)
                step = latter
        marked = mask_ref[:, pl.ds(start, CHUNK)]
        marked = jnp.broadcast_to(marked[:, None, :], (8, 8, CHUNK)).reshape(ROWS, CHUNK)
        at = pl.ds(start, CHUNK)
        calm_ref[:, at] = base - marked * base
        lifted_ref[:, at] = marked * (base + tz)
        tx_ref[:, at] = jnp.where(inside, marked * tx, 0.0)
        ty_ref[:, at] = marked * ty
        return carry

    lax.fori_loop(0, N // CHUNK, chunk, 0)
    lifted, tx = lifted_ref[...], tx_ref[...]
    eighth, tilt = 0.125 * lifted, ty_ref[...] * (1.0 / 32.0)
    smooth = 0.75 * lifted + pltpu.roll(eighth + tilt, 1, 1) + pltpu.roll(eighth - tilt, N - 1, 1)
    eighth, tilt = 0.125 * smooth, smooth_y(tx) * (1.0 / 32.0)
    kappa_ref[...] = (
        longer(calm_ref[...] + 0.75 * smooth)
        + pltpu.roll(longer(eighth + tilt), 1, 0)
        + pltpu.roll(longer(eighth - tilt), ROWS + 7, 0)
    )


def inner_sums(low, high, density, refine):
    return pl.pallas_call(
        inner_kernel,
        out_shape=(
            jax.ShapeDtypeStruct((ROWS + 8, N), f32),
            jax.ShapeDtypeStruct((8, N), f32),
            jax.ShapeDtypeStruct((4, LAYERS, N), f32),
        ),
        in_specs=[SM, SM, VM, VM],
        out_specs=(VM,) * 3,
        scratch_shapes=[pltpu.VMEM((ROWS, N), f32)] * 4,
        compiler_params=limit(40),
        cost_estimate=pl.CostEstimate(flops=40_000_000, bytes_accessed=24 * MB, transcendentals=0),
        name="inner_sums",
    )(low, high, density, refine)


def outer_kernel(
    low_ref,
    high_ref,
    d_ref,
    cross_ref,
    layer_ref,
    other_layer_ref,
    row_ref,
    other_row_ref,
    kappa_ref,
    mask_ref,
    near_ref,
    high_table,
    low_table,
    far_ref,
    next_ref,
    last_ref,
    part_ref,
):
    los = lax.axis_index("zhi") * 4 + lax.axis_index("x")
    v0, v1 = d_ref[0].astype(f32), d_ref[1].astype(f32)
    v6, v7 = d_ref[6].astype(f32), d_ref[7].astype(f32)
    odd = los % 2 == 1
    crossing = jnp.logical_or(los == 3, los == 4)
    one = jnp.where(crossing, cross_ref[0], layer_ref[0]).astype(f32)
    other = other_layer_ref[0].astype(f32)
    below = jnp.where(los == 0, v0, jnp.where(odd, other, one))
    above = jnp.where(los == 7, v7, jnp.where(odd, one, other))
    slope0 = 0.125 * (high_ref[0] - low_ref[0])
    slope7 = 0.125 * (high_ref[7] - low_ref[7])
    tz = slope0 * minmod(v1 - v0, v0 - below) + slope7 * minmod(above - v7, v7 - v6)
    mask = mask_ref[...]
    marked = jnp.broadcast_to(mask[:, None, :], (8, 8, N)).reshape(ROWS, N)
    smooth = smooth_y(marked * tz)
    layer = lax.broadcasted_iota(jnp.int32, (LAYERS, 1), 0)
    average = jnp.zeros((LAYERS, 1), f32)
    for z in range(LAYERS):
        average = jnp.where(layer == z, 0.5 * (low_ref[z] + high_ref[z]), average)
    r0, r1, r62, r63 = near_ref[0], near_ref[1], near_ref[2], near_ref[3]
    even = lax.axis_index("sky") % 2 == 0
    before = jnp.where(even, other_row_ref[...], row_ref[...])
    after = jnp.where(even, row_ref[...], other_row_ref[...])
    e0 = jnp.sum(average * minmod(r1 - r0, r0 - before), axis=0, keepdims=True)
    e63 = jnp.sum(average * minmod(after - r63, r63 - r62), axis=0, keepdims=True)
    row = lax.broadcasted_iota(jnp.int32, (8, N), 0)
    e0 = smooth_y(jnp.where(row == 0, mask[0:1] * e0, 0.0)) * (1.0 / 32.0)
    e63 = smooth_y(jnp.where(row == 7, mask[7:8] * e63, 0.0)) * (1.0 / 32.0)
    first = pltpu.roll(e0, 1, 0)
    last = pltpu.roll(e63, 7, 0)
    spill = jnp.where(row == 0, pltpu.roll(e63, 1, 0), -pltpu.roll(e0, 7, 0))
    sides = jnp.concatenate([first, jnp.zeros((ROWS - 16, N), f32), -last, spill], axis=0)
    eighth = longer(0.125 * smooth)
    kappa = (
        (kappa_ref[...] + sides)
        + longer(0.75 * smooth)
        + (pltpu.roll(eighth, 1, 0) + pltpu.roll(eighth, ROWS + 7, 0))
    )
    part = [kappa[:, 128 * a : 128 * a + 128] for a in range(16)]
    even = [part[a] + part[16 - a] for a in range(1, 8)]
    odd = [part[a] - part[16 - a] for a in range(1, 8)]

    def weigh(pairs):
        total = None
        for factor, value in pairs:
            if abs(factor) < 1e-9:
                continue
            term = value if abs(factor - 1) < 1e-9 else factor * value
            total = term if total is None else total + term
        return total

    ends = (part[0] + part[8], part[0] - part[8])
    cosine, sine = [None] * 9, [None] * 9
    for k in range(5):
        factors = [float(np.cos(np.pi * k * a / 8)) for a in range(1, 8)]
        plain = ends[k % 2] + weigh([(factors[a - 1], even[a - 1]) for a in (2, 4, 6)])
        turned = weigh([(factors[a - 1], even[a - 1]) for a in (1, 3, 5, 7)])
        cosine[k] = plain if turned is None else plain + turned
        if k < 4:
            cosine[8 - k] = plain - turned
    for k in range(1, 5):
        factors = [float(-np.sin(np.pi * k * a / 8)) for a in range(1, 8)]
        plain = weigh([(factors[a - 1], odd[a - 1]) for a in (2, 4, 6)])
        turned = weigh([(factors[a - 1], odd[a - 1]) for a in (1, 3, 5, 7)])
        sine[k] = turned if plain is None else turned + plain
        if k < 4:
            sine[8 - k] = turned - plain
    for tile in range(8):
        second = sine[tile] if tile else cosine[8]
        value = jnp.concatenate([cosine[tile], second], axis=1)
        value = jnp.concatenate([value, jnp.zeros((8, 256), f32)], axis=0)
        part_ref[tile] = stacked(value)
    transform_for(2, part_ref, high_table, low_table, far_ref)
    transform_for(1, part_ref, high_table, low_table, next_ref)
    transform_for(3, part_ref, high_table, low_table, last_ref)


def transform_for(ahead, part_ref, high_table, low_table, out_ref):
    target = (lax.axis_index("x") + ahead) % 4
    for half in range(2):
        tile = 2 * target + half
        value = dot3_stacked(part_ref[tile], high_table[tile], low_table[tile])
        for block in (2 * half, 2 * half + 1):
            part = value[:, 128 * (block % 2) : 128 * (block % 2) + 128]
            out_ref[ROWS * block : ROWS * block + ROWS] = part[:ROWS]
            out_ref[4 * ROWS + block : 4 * ROWS + block + 1] = part[ROWS : ROWS + 1]
            out_ref[4 * ROWS + 4 + block : 4 * ROWS + 5 + block] = part[ROWS + 7 : ROWS + 8]


def rest_kernel(part_ref, high_table, low_table, own_ref):
    transform_for(0, part_ref, high_table, low_table, own_ref)


def outer_sums(low, high, density, layers, rows, inner, tables):
    piece = jax.ShapeDtypeStruct((4 * ROWS + 8, 128), f32)
    two, one, three, parts = pl.pallas_call(
        outer_kernel,
        out_shape=(piece, piece, piece, jax.ShapeDtypeStruct((8, 160, 256), bf16)),
        in_specs=[SM, SM] + [VM] * 11,
        out_specs=(VM,) * 4,
        compiler_params=limit(32),
        name="outer_sums",
    )(low, high, density, *layers, *rows, *inner, *tables)
    own = pl.pallas_call(
        rest_kernel,
        out_shape=piece,
        in_specs=[VM] * 3,
        out_specs=VM,
        compiler_params=limit(24),
        name="other_sums",
    )(parts, *tables)
    return own, one, two, three


def turn_kernel(a_ref, b_ref, c_ref, d_ref, out_ref):
    total = (a_ref[...] + b_ref[...]) + (c_ref[...] + d_ref[...])
    none = jnp.zeros((56, 128), f32)
    turned = [
        jnp.concatenate([total[ROWS * block : ROWS * block + ROWS], total[4 * ROWS :], none], axis=0).T
        for block in range(4)
    ]
    lane = lax.broadcasted_iota(jnp.int32, (SKY, 128), 1)
    for half in range(2):
        at = slice(SKY * half, SKY * half + SKY)
        spill = jnp.zeros((SKY, 128), f32)
        for c in range(4):
            block, first = 2 * half + c // 2, 64 * (c % 2)
            real = turned[block][first : first + SKY]
            imag = turned[block][first + SKY : first + 2 * SKY]
            out_ref[at, 0, 128 * c : 128 * c + 128] = jnp.where(
                lane < 64, real, pltpu.roll(imag, 64, 1)
            )
            for sub, part in ((c, real), (4 + c, imag)):
                up = (128 - 16 * sub) % 128
                down = (up + 63) % 128
                spill = jnp.where(lane == up, pltpu.roll(part, (up - 64 - block) % 128, 1), spill)
                spill = jnp.where(
                    lane == down, pltpu.roll(part, (down - 68 - block) % 128, 1), spill
                )
        out_ref[at, 0, 512:640] = spill


def turn(pieces):
    return pl.pallas_call(
        turn_kernel,
        out_shape=jax.ShapeDtypeStruct((64, 1, 640), f32),
        in_specs=[VM] * 4,
        out_specs=VM,
        compiler_params=limit(24),
        name="turn",
    )(*pieces)


def dft_32(values):
    even = [values[s] + values[32 - s] for s in range(1, 16)]
    odd = [values[s] - values[32 - s] for s in range(1, 16)]
    ends = [values[0] + values[16], values[0] - values[16]]
    cosine, sine = [None] * 17, [None] * 17
    for k in range(9):
        plain = ends[k % 2]
        turned = None
        for s in range(1, 16):
            term = float(np.cos(np.pi * k * s / 16)) * even[s - 1]
            if s % 2 == 0:
                plain = plain + term
            else:
                turned = term if turned is None else turned + term
        cosine[k] = plain + turned
        cosine[16 - k] = plain - turned
    for k in range(1, 9):
        plain, turned = None, None
        for s in range(1, 16):
            term = float(np.sin(np.pi * k * s / 16)) * odd[s - 1]
            if s % 2 == 0:
                plain = term if plain is None else plain + term
            else:
                turned = term if turned is None else turned + term
        sine[k] = turned + plain
        sine[16 - k] = turned - plain
    return cosine, sine


def solve_kernel(in_ref, cos_ref, sin_ref, high_table, low_table, out_ref):
    sky = lax.axis_index("sky")
    tile = 2 * lax.axis_index("x") + lax.axis_index("zhi")
    lane = lax.broadcasted_iota(jnp.int32, (8, 128), 1)
    sub = lax.broadcasted_iota(jnp.int32, (8, 128), 0)
    lower = lane < 64
    sign = jnp.where(sub < 4, 1.0, -1.0)
    first = jnp.logical_and(tile == 0, sky == 0)
    packed = jnp.logical_and(sub % 4 == 0, first)

    def swap(v):
        return pltpu.roll(v, 4, v.ndim - 2)

    def bent(v):
        return swap(v) * sign

    main, spill = [], []
    for s in range(SKY):
        rows = [
            jnp.broadcast_to(in_ref[s, :, lanes] + in_ref[SKY + s, :, lanes], (8, 128))
            for lanes in (slice(128 * c, 128 * c + 128) for c in range(5))
        ]
        v = rows[3]
        for c in range(3):
            v = jnp.where(sub % 4 == c, rows[c], v)
        main.append(jnp.where(sub < 4, v, pltpu.roll(v, 64, 1)))
        spill.append(pltpu.roll(rows[4], 0, 1, stride=16, stride_axis=0))
    values = []
    for s in range(SKY):
        up, down = spill[(s - 1) % SKY], spill[(s + 1) % SKY]
        v = main[s] + jnp.where(lane == 0, up, jnp.where(lane == 63, down, 0.0))
        v = jnp.where(lower, v, pltpu.roll(v, 64, 1))
        apart = jnp.where(sub == 4, 0.0, jnp.where(lower, v, swap(v)))
        values.append(jnp.where(packed, apart, v))
    cosine, sine = dft_32(values)
    spectrum = [None] * 32
    spectrum[0], spectrum[16] = cosine[0], cosine[16]
    for k in range(1, 16):
        turned = bent(sine[k])
        spectrum[k], spectrum[32 - k] = cosine[k] + turned, cosine[k] - turned
    twisted = [spectrum[k] * cos_ref[k] + swap(spectrum[k]) * sin_ref[k] for k in range(32)]
    rows = jnp.concatenate(twisted, axis=0)
    pair = dot3(rows, high_table[...], low_table[...])
    pair_c = pair[:, :128].reshape(32, 8, 128)
    pair_s = pair[:, 128:].reshape(32, 8, 128)

    k1 = lax.broadcasted_iota(jnp.int32, (32, 8, 128), 0)
    k2 = lax.broadcasted_iota(jnp.int32, (32, 8, 128), 2) % 64
    nx = k1 + 32 * k2
    nx = jnp.where(nx < N // 2, nx, nx - N)
    n = 4 * sky + sub % 4
    ny = jnp.where(tile > 0, tile + 16 * n, jnp.where(n < 64, 16 * n, 8 + 16 * (n - 64)))
    ny = jnp.where(ny < N // 2, ny, ny - N)
    ny = jnp.where(jnp.logical_and(packed, jnp.logical_not(lower)), -(N // 2), ny)
    along_x = jnp.logical_or(packed, lower)[None]
    squared = nx * nx + (ny * ny)[None]
    wave = jnp.where(along_x, jnp.where(nx == -(N // 2), 0, nx), ny[None])
    unit = 2.0 * np.pi / N
    scale = float(-2.0 / unit / 64.0 / N / N)
    factor = scale * wave.astype(f32) / jnp.maximum(squared, 1).astype(f32)
    kappa_hat = pair_c + swap(pair_s) * sign[None]
    field = factor * (swap(kappa_hat) * (-sign)[None])
    pair = dot3(field.reshape(256, 128), high_table[...], low_table[...])
    values = []
    for k in range(32):
        v = pair[8 * k : 8 * k + 8, :128] - bent(pair[8 * k : 8 * k + 8, 128:])
        values.append(v * cos_ref[k] - swap(v) * sin_ref[k])
    cosine, sine = dft_32(values)
    for s in range(17):
        turned = bent(sine[s]) if 0 < s < 16 else None
        for at in (s,) if turned is None else (s, 32 - s):
            v = cosine[s]
            if turned is not None:
                v = v - turned if at == s else v + turned
            other = swap(pltpu.roll(v, 64, 1))
            joined = jnp.where(lower, jnp.where(sub == 4, other, v), 0.0)
            v = jnp.where(packed, joined, v)
            out_ref[at] = v
            out_ref[SKY + at] = v


def solve(pieces, tables):
    return pl.pallas_call(
        solve_kernel,
        out_shape=jax.ShapeDtypeStruct((64, 8, 128), f32),
        in_specs=[VM] * 5,
        out_specs=VM,
        compiler_params=limit(24),
        name="solve",
    )(pieces, *tables)


def back_for(ahead, eighth_ref, plain, bent, high_table, low_table, out_ref):
    zhi, column = lax.axis_index("zhi"), lax.axis_index("x")
    target = (column + ahead) % 4
    parts = []
    for half in range(2):
        lanes = slice(256 * half, 256 * half + 256)
        turns = (2 * column + half) * (4 * zhi + target) % 8
        cosine, sine = eighth_ref[turns], eighth_ref[8 + turns]
        parts.append(cosine * plain[:, lanes] + sine * bent[:, lanes])
    value = stacked(jnp.concatenate(parts, axis=1))
    out_ref[...] = dot3_stacked(value, high_table[column], low_table[column])


def back_kernel(
    eighth_ref, in_ref, high_table, low_table, far_ref, next_ref, last_ref, plain_ref, bent_ref
):
    value = in_ref[...]
    sub = lax.broadcasted_iota(jnp.int32, (64, 8, 128), 1)
    bent = pltpu.roll(value, 4, 1) * jnp.where(sub < 4, -1.0, 1.0)
    plain, bent = value.reshape(512, 128).T, bent.reshape(512, 128).T
    plain_ref[...] = plain
    bent_ref[...] = bent
    back_for(2, eighth_ref, plain, bent, high_table, low_table, far_ref)
    back_for(1, eighth_ref, plain, bent, high_table, low_table, next_ref)
    back_for(3, eighth_ref, plain, bent, high_table, low_table, last_ref)


def back_rest_kernel(eighth_ref, plain_ref, bent_ref, high_table, low_table, own_ref):
    back_for(0, eighth_ref, plain_ref[...], bent_ref[...], high_table, low_table, own_ref)


def back(pieces, tables):
    turns = np.arange(8) * (2 * np.pi / 8)
    eighth = np.concatenate([np.cos(turns), np.sin(turns)]).astype(np.float32)
    piece = jax.ShapeDtypeStruct((128, 256), f32)
    held = jax.ShapeDtypeStruct((128, 512), f32)
    two, one, three, plain, bent = pl.pallas_call(
        back_kernel,
        out_shape=(piece, piece, piece, held, held),
        in_specs=[SM, VM, VM, VM],
        out_specs=(VM,) * 5,
        compiler_params=limit(24),
        name="back",
    )(eighth, pieces, *tables)
    own = pl.pallas_call(
        back_rest_kernel,
        out_shape=piece,
        in_specs=[SM] + [VM] * 4,
        out_specs=VM,
        compiler_params=limit(24),
        name="back_rest",
    )(eighth, plain, bent, *tables)
    return own, one, two, three


def final_kernel(a_ref, b_ref, c_ref, d_ref, x_ref, y_ref):
    total = (a_ref[...] + b_ref[...]) + (c_ref[...] + d_ref[...])
    x_ref[...] = total[:ROWS]
    y_ref[...] = total[ROWS:]


def final(pieces):
    shape = jax.ShapeDtypeStruct((ROWS, 256), f32)
    return pl.pallas_call(
        final_kernel,
        out_shape=(shape, shape),
        in_specs=[VM] * 4,
        out_specs=(VM, VM),
        compiler_params=limit(24),
        name="final",
    )(*pieces)


def deliver(pieces):
    return [pieces[0]] + [
        lax.ppermute(pieces[a], "x", [(i, (i + a) % 4) for i in range(4)]) for a in (1, 2, 3)
    ]


def body(density, refine, weight_low, weight_high):
    def swap(array, axes, pairs):
        return lax.ppermute(array, axes, pairs + [(b, a) for a, b in pairs])

    odd = lax.axis_index("x") % 2 == 1
    cross = lax.dynamic_slice_in_dim(density, jnp.where(odd, LAYERS - 1, 0), 1, 0)
    cross = swap(cross, LOS, [(3, 4)])
    row, other_row, layer, other_layer = edge_rows(density)
    layer = swap(layer, LOS, [(1, 2), (5, 6)])
    other_layer = swap(other_layer, LOS, [(0, 1), (2, 3), (4, 5), (6, 7)])
    row = swap(row, "sky", [(i, i + 1) for i in range(0, SKY, 2)])
    other_row = swap(other_row, "sky", [(i, (i + 1) % SKY) for i in range(1, SKY, 2)])
    inner = inner_sums(weight_low, weight_high, density, refine)
    tables = halves(forward_table())
    summed = outer_sums(
        weight_low, weight_high, density, (cross, layer, other_layer), (row, other_row), inner, tables
    )
    summed = deliver(summed)
    pieces = lax.all_to_all(turn(summed), ("zhi", "sky"), 0, 0, tiled=True)
    pieces = solve(pieces, twists() + halves(row_table()))
    pieces = lax.all_to_all(pieces, ("zhi", "sky"), 0, 0, tiled=True)
    fields = back(pieces, halves(inverse_table()))
    return final(deliver(fields))


def solution(mesh):
    devices = mesh.devices.reshape(2, 4, SKY)
    inner = Mesh(devices, ("zhi", "x", "sky"))
    placed = (P(LOS, "sky", None), P(LOS, "sky", None), P(LOS), P(LOS))
    return jax.shard_map(
        body,
        mesh=inner,
        in_specs=placed,
        out_specs=(P("sky", LOS), P("sky", LOS)),
        check_vma=False,
    )
```

```python
import functools

import jax
import jax.numpy as jnp
import ml_dtypes
import numpy as np
from jax import lax
from jax.experimental import pallas as pl
from jax.experimental.pallas import tpu as pltpu
from jax.sharding import Mesh, PartitionSpec as P

f32 = jnp.float32
bf16 = jnp.bfloat16
N = 2048
ROWS = 64
SKY = 32
LAYERS = 8
LOS = ("zhi", "x")
MB = 1024 * 1024


def halves(table):
    high = table.astype(np.float32).astype(ml_dtypes.bfloat16)
    low = (table - high.astype(np.float64)).astype(np.float32).astype(ml_dtypes.bfloat16)
    return high, low


def tile_modes(tile):
    n = np.arange(128)
    if tile:
        return tile + 16 * n
    return np.where(n < 64, 16 * n, 8 + 16 * (n - 64))


def tile_order(real, imag):
    pair = np.stack([real.reshape(SKY, 4, -1), imag.reshape(SKY, 4, -1)], axis=1)
    return pair.reshape(256, -1)


def tile_groups(real, imag):
    pair = np.stack([real.reshape(SKY, 4, -1), imag.reshape(SKY, 4, -1)], axis=1)
    return pair.transpose(2, 1, 0, 3).reshape(256, -1)


def forward_table():
    b = np.arange(128)
    tiles = []
    for tile in range(8):
        angle = (tile_modes(tile)[:, None] * b[None, :] % N) * (2 * np.pi / N)
        cosine, sine = np.cos(angle), np.sin(angle)
        if tile:
            real = np.concatenate([cosine, sine], 1)
            imag = np.concatenate([-sine, cosine], 1)
        else:
            zero = np.zeros((64, 128))
            real = np.block([[cosine[:64], zero], [zero, cosine[64:]]])
            imag = np.block([[-sine[:64], zero], [zero, -sine[64:]]])
            imag[0, :128] = (-1.0) ** b
        tiles.append(tile_groups(real, imag).T)
    return np.stack(tiles)


def inverse_table():
    j = np.arange(256)
    tiles = []
    for tile in range(8):
        angle = (tile_modes(tile)[:, None] * j[None, :] % N) * (2 * np.pi / N)
        real, imag = 2 * np.cos(angle), -2 * np.sin(angle)
        if not tile:
            real[0] = 1.0
            imag[0] = (-1.0) ** j
        tiles.append(tile_order(real, imag))
    return np.stack(tiles).reshape(4, 512, 256)


def row_table():
    r = np.arange(64)
    angle = (r[:, None] * r[None, :] % 64) * (2 * np.pi / 64)
    both = np.eye(2)
    return np.concatenate([np.kron(both, np.cos(angle)), np.kron(both, np.sin(angle))], 1)


def twists():
    angle = (np.arange(32)[:, None] * (np.arange(128) % 64)[None, :]) * (2 * np.pi / N)
    sign = np.where(np.arange(8) < 4, 1.0, -1.0)
    cosine = np.broadcast_to(np.cos(angle)[:, None, :], (32, 8, 128))
    sine = np.sin(angle)[:, None, :] * sign[None, :, None]
    return cosine.astype(np.float32), sine.astype(np.float32)


def minmod(a, b):
    return jnp.maximum(jnp.minimum(a, b), 0.0) + jnp.minimum(jnp.maximum(a, b), 0.0)


def split(value):
    high = value.astype(bf16)
    return high, (value - high.astype(f32)).astype(bf16)


def dot3(value, high_table, low_table):
    high, low = split(value)
    dot = functools.partial(jnp.dot, preferred_element_type=f32)
    return dot(high, high_table) + (dot(low, high_table) + dot(high, low_table))


def stacked(value):
    return jnp.concatenate(split(value), axis=0)


def dot3_stacked(parts, high_table, low_table):
    rows = parts.shape[0] // 2
    dot = functools.partial(jnp.dot, preferred_element_type=f32)
    both = dot(parts, high_table)
    return both[:rows] + (both[rows:] + dot(parts[:rows], low_table))


def limit(mib):
    return pltpu.CompilerParams(vmem_limit_bytes=mib * MB)


VM = pl.BlockSpec(memory_space=pltpu.VMEM)
SM = pl.BlockSpec(memory_space=pltpu.SMEM)


def rows_kernel(d_ref, near_ref, far_ref, layer_ref, other_layer_ref):
    odd = lax.axis_index("x") % 2
    layer_ref[0] = d_ref[(LAYERS - 1) * odd]
    other_layer_ref[0] = d_ref[(LAYERS - 1) * (1 - odd)]
    even = lax.axis_index("sky") % 2 == 0
    for z in range(LAYERS):
        first = d_ref[z, 0:16, :].astype(f32)[0:1]
        last = d_ref[z, 48:64, :].astype(f32)[15:16]
        near_ref[z : z + 1, :] = jnp.where(even, last, first)
        far_ref[z : z + 1, :] = jnp.where(even, first, last)


def edge_rows(density):
    shape = jax.ShapeDtypeStruct((LAYERS, N), f32)
    return pl.pallas_call(
        rows_kernel,
        out_shape=(shape, shape) + (jax.ShapeDtypeStruct((1, ROWS, N), bf16),) * 2,
        in_specs=[VM],
        out_specs=(VM,) * 4,
        compiler_params=limit(8),
        name="edge_rows",
    )(density)


def longer(field):
    return jnp.concatenate([field, jnp.zeros((8, N), f32)], axis=0)


def smooth_y(field):
    return 0.75 * field + 0.125 * (pltpu.roll(field, 1, 1) + pltpu.roll(field, N - 1, 1))


CHUNK = 512


def inner_kernel(
    low_ref,
    high_ref,
    d_ref,
    refine_ref,
    kappa_ref,
    mask_ref,
    near_ref,
    calm_ref,
    lifted_ref,
    tx_ref,
    ty_ref,
):
    block = lax.broadcasted_iota(jnp.int32, (256, N), 0)
    lane = lax.broadcasted_iota(jnp.int32, (256, N), 1)
    grow = jnp.where(lane // 8 == block, 1.0, 0.0).astype(bf16)
    coarse = refine_ref[0].astype(f32).astype(bf16)
    mask_ref[...] = jnp.dot(coarse, grow, preferred_element_type=f32)
    for z in range(LAYERS):
        first = d_ref[z, 0:16, :].astype(f32)
        last = d_ref[z, 48:64, :].astype(f32)
        near_ref[0, z : z + 1, :] = first[0:1]
        near_ref[1, z : z + 1, :] = first[1:2]
        near_ref[2, z : z + 1, :] = last[14:15]
        near_ref[3, z : z + 1, :] = last[15:16]

    wide = CHUNK + 256
    row = lax.broadcasted_iota(jnp.int32, (ROWS, CHUNK), 0)
    inside = jnp.logical_and(row > 0, row < ROWS - 1)

    def chunk(i, carry):
        start = pl.multiple_of(i * CHUNK, CHUNK)
        left = pl.multiple_of((start + N - 128) % N, 128)
        right = pl.multiple_of((start + CHUNK) % N, 128)
        base = jnp.zeros((ROWS, CHUNK), f32)
        tz, tx, ty = base, base, base
        centre, step = None, None
        for z in range(LAYERS):
            average = 0.5 * (low_ref[z] + high_ref[z])
            former = centre
            around = jnp.concatenate(
                [
                    d_ref[z, :, pl.ds(left, 128)],
                    d_ref[z, :, pl.ds(start, CHUNK)],
                    d_ref[z, :, pl.ds(right, 128)],
                ],
                axis=1,
            ).astype(f32)
            centre = around[:, 128 : 128 + CHUNK]
            base = base + average * centre
            dy = pltpu.roll(around, wide - 1, 1) - around
            gy = minmod(dy, pltpu.roll(dy, 1, 1))[:, 128 : 128 + CHUNK]
            ty = ty + average * gy
            dx = pltpu.roll(centre, ROWS - 1, 0) - centre
            tx = tx + average * minmod(dx, pltpu.roll(dx, 1, 0))
            if z > 0:
                latter = centre - former
                if step is not None:
                    slope = 0.125 * (high_ref[z - 1] - low_ref[z - 1])
                    tz = tz + slope * minmod(latter, step)
                step = latter
        marked = mask_ref[:, pl.ds(start, CHUNK)]
        marked = jnp.broadcast_to(marked[:, None, :], (8, 8, CHUNK)).reshape(ROWS, CHUNK)
        at = pl.ds(start, CHUNK)
        calm_ref[:, at] = base - marked * base
        lifted_ref[:, at] = marked * (base + tz)
        tx_ref[:, at] = jnp.where(inside, marked * tx, 0.0)
        ty_ref[:, at] = marked * ty
        return carry

    lax.fori_loop(0, N // CHUNK, chunk, 0)
    lifted, tx = lifted_ref[...], tx_ref[...]
    eighth, tilt = 0.125 * lifted, ty_ref[...] * (1.0 / 32.0)
    smooth = 0.75 * lifted + pltpu.roll(eighth + tilt, 1, 1) + pltpu.roll(eighth - tilt, N - 1, 1)
    eighth, tilt = 0.125 * smooth, smooth_y(tx) * (1.0 / 32.0)
    kappa_ref[...] = (
        longer(calm_ref[...] + 0.75 * smooth)
        + pltpu.roll(longer(eighth + tilt), 1, 0)
        + pltpu.roll(longer(eighth - tilt), ROWS + 7, 0)
    )


def inner_sums(low, high, density, refine):
    return pl.pallas_call(
        inner_kernel,
        out_shape=(
            jax.ShapeDtypeStruct((ROWS + 8, N), f32),
            jax.ShapeDtypeStruct((8, N), f32),
            jax.ShapeDtypeStruct((4, LAYERS, N), f32),
        ),
        in_specs=[SM, SM, VM, VM],
        out_specs=(VM,) * 3,
        scratch_shapes=[pltpu.VMEM((ROWS, N), f32)] * 4,
        compiler_params=limit(40),
        cost_estimate=pl.CostEstimate(flops=40_000_000, bytes_accessed=24 * MB, transcendentals=0),
        name="inner_sums",
    )(low, high, density, refine)


def outer_kernel(
    low_ref,
    high_ref,
    d_ref,
    cross_ref,
    layer_ref,
    other_layer_ref,
    row_ref,
    other_row_ref,
    kappa_ref,
    mask_ref,
    near_ref,
    high_table,
    low_table,
    far_ref,
    next_ref,
    last_ref,
    part_ref,
):
    los = lax.axis_index("zhi") * 4 + lax.axis_index("x")
    v0, v1 = d_ref[0].astype(f32), d_ref[1].astype(f32)
    v6, v7 = d_ref[6].astype(f32), d_ref[7].astype(f32)
    odd = los % 2 == 1
    crossing = jnp.logical_or(los == 3, los == 4)
    one = jnp.where(crossing, cross_ref[0], layer_ref[0]).astype(f32)
    other = other_layer_ref[0].astype(f32)
    below = jnp.where(los == 0, v0, jnp.where(odd, other, one))
    above = jnp.where(los == 7, v7, jnp.where(odd, one, other))
    slope0 = 0.125 * (high_ref[0] - low_ref[0])
    slope7 = 0.125 * (high_ref[7] - low_ref[7])
    tz = slope0 * minmod(v1 - v0, v0 - below) + slope7 * minmod(above - v7, v7 - v6)
    mask = mask_ref[...]
    marked = jnp.broadcast_to(mask[:, None, :], (8, 8, N)).reshape(ROWS, N)
    smooth = smooth_y(marked * tz)
    layer = lax.broadcasted_iota(jnp.int32, (LAYERS, 1), 0)
    average = jnp.zeros((LAYERS, 1), f32)
    for z in range(LAYERS):
        average = jnp.where(layer == z, 0.5 * (low_ref[z] + high_ref[z]), average)
    r0, r1, r62, r63 = near_ref[0], near_ref[1], near_ref[2], near_ref[3]
    even = lax.axis_index("sky") % 2 == 0
    before = jnp.where(even, other_row_ref[...], row_ref[...])
    after = jnp.where(even, row_ref[...], other_row_ref[...])
    e0 = jnp.sum(average * minmod(r1 - r0, r0 - before), axis=0, keepdims=True)
    e63 = jnp.sum(average * minmod(after - r63, r63 - r62), axis=0, keepdims=True)
    row = lax.broadcasted_iota(jnp.int32, (8, N), 0)
    e0 = smooth_y(jnp.where(row == 0, mask[0:1] * e0, 0.0)) * (1.0 / 32.0)
    e63 = smooth_y(jnp.where(row == 7, mask[7:8] * e63, 0.0)) * (1.0 / 32.0)
    first = pltpu.roll(e0, 1, 0)
    last = pltpu.roll(e63, 7, 0)
    spill = jnp.where(row == 0, pltpu.roll(e63, 1, 0), -pltpu.roll(e0, 7, 0))
    sides = jnp.concatenate([first, jnp.zeros((ROWS - 16, N), f32), -last, spill], axis=0)
    eighth = longer(0.125 * smooth)
    kappa = (
        (kappa_ref[...] + sides)
        + longer(0.75 * smooth)
        + (pltpu.roll(eighth, 1, 0) + pltpu.roll(eighth, ROWS + 7, 0))
    )
    part = [kappa[:, 128 * a : 128 * a + 128] for a in range(16)]
    even = [part[a] + part[16 - a] for a in range(1, 8)]
    odd = [part[a] - part[16 - a] for a in range(1, 8)]

    def weigh(pairs):
        total = None
        for factor, value in pairs:
            if abs(factor) < 1e-9:
                continue
            term = value if abs(factor - 1) < 1e-9 else factor * value
            total = term if total is None else total + term
        return total

    ends = (part[0] + part[8], part[0] - part[8])
    cosine, sine = [None] * 9, [None] * 9
    for k in range(5):
        factors = [float(np.cos(np.pi * k * a / 8)) for a in range(1, 8)]
        plain = ends[k % 2] + weigh([(factors[a - 1], even[a - 1]) for a in (2, 4, 6)])
        turned = weigh([(factors[a - 1], even[a - 1]) for a in (1, 3, 5, 7)])
        cosine[k] = plain if turned is None else plain + turned
        if k < 4:
            cosine[8 - k] = plain - turned
    for k in range(1, 5):
        factors = [float(-np.sin(np.pi * k * a / 8)) for a in range(1, 8)]
        plain = weigh([(factors[a - 1], odd[a - 1]) for a in (2, 4, 6)])
        turned = weigh([(factors[a - 1], odd[a - 1]) for a in (1, 3, 5, 7)])
        sine[k] = turned if plain is None else turned + plain
        if k < 4:
            sine[8 - k] = turned - plain
    for tile in range(8):
        second = sine[tile] if tile else cosine[8]
        value = jnp.concatenate([cosine[tile], second], axis=1)
        value = jnp.concatenate([value, jnp.zeros((8, 256), f32)], axis=0)
        part_ref[tile] = stacked(value)
    transform_for(2, part_ref, high_table, low_table, far_ref)
    transform_for(1, part_ref, high_table, low_table, next_ref)
    transform_for(3, part_ref, high_table, low_table, last_ref)


def transform_for(ahead, part_ref, high_table, low_table, out_ref):
    target = (lax.axis_index("x") + ahead) % 4
    for half in range(2):
        tile = 2 * target + half
        value = dot3_stacked(part_ref[tile], high_table[tile], low_table[tile])
        for block in (2 * half, 2 * half + 1):
            part = value[:, 128 * (block % 2) : 128 * (block % 2) + 128]
            out_ref[ROWS * block : ROWS * block + ROWS] = part[:ROWS]
            out_ref[4 * ROWS + block : 4 * ROWS + block + 1] = part[ROWS : ROWS + 1]
            out_ref[4 * ROWS + 4 + block : 4 * ROWS + 5 + block] = part[ROWS + 7 : ROWS + 8]


def rest_kernel(part_ref, high_table, low_table, own_ref):
    transform_for(0, part_ref, high_table, low_table, own_ref)


def outer_sums(low, high, density, layers, rows, inner, tables):
    piece = jax.ShapeDtypeStruct((4 * ROWS + 8, 128), f32)
    two, one, three, parts = pl.pallas_call(
        outer_kernel,
        out_shape=(piece, piece, piece, jax.ShapeDtypeStruct((8, 160, 256), bf16)),
        in_specs=[SM, SM] + [VM] * 11,
        out_specs=(VM,) * 4,
        compiler_params=limit(32),
        name="outer_sums",
    )(low, high, density, *layers, *rows, *inner, *tables)
    own = pl.pallas_call(
        rest_kernel,
        out_shape=piece,
        in_specs=[VM] * 3,
        out_specs=VM,
        compiler_params=limit(24),
        name="other_sums",
    )(parts, *tables)
    return own, one, two, three


def turn_kernel(a_ref, b_ref, c_ref, d_ref, out_ref):
    total = (a_ref[...] + b_ref[...]) + (c_ref[...] + d_ref[...])
    none = jnp.zeros((56, 128), f32)
    turned = [
        jnp.concatenate([total[ROWS * block : ROWS * block + ROWS], total[4 * ROWS :], none], axis=0).T
        for block in range(4)
    ]
    lane = lax.broadcasted_iota(jnp.int32, (SKY, 128), 1)
    for half in range(2):
        at = slice(SKY * half, SKY * half + SKY)
        spill = jnp.zeros((SKY, 128), f32)
        for c in range(4):
            block, first = 2 * half + c // 2, 64 * (c % 2)
            real = turned[block][first : first + SKY]
            imag = turned[block][first + SKY : first + 2 * SKY]
            out_ref[at, 0, 128 * c : 128 * c + 128] = jnp.where(
                lane < 64, real, pltpu.roll(imag, 64, 1)
            )
            for sub, part in ((c, real), (4 + c, imag)):
                up = (128 - 16 * sub) % 128
                down = (up + 63) % 128
                spill = jnp.where(lane == up, pltpu.roll(part, (up - 64 - block) % 128, 1), spill)
                spill = jnp.where(
                    lane == down, pltpu.roll(part, (down - 68 - block) % 128, 1), spill
                )
        out_ref[at, 0, 512:640] = spill


def turn(pieces):
    return pl.pallas_call(
        turn_kernel,
        out_shape=jax.ShapeDtypeStruct((64, 1, 640), f32),
        in_specs=[VM] * 4,
        out_specs=VM,
        compiler_params=limit(24),
        name="turn",
    )(*pieces)


def dft_32(values):
    even = [values[s] + values[32 - s] for s in range(1, 16)]
    odd = [values[s] - values[32 - s] for s in range(1, 16)]
    ends = [values[0] + values[16], values[0] - values[16]]
    cosine, sine = [None] * 17, [None] * 17
    for k in range(9):
        plain = ends[k % 2]
        turned = None
        for s in range(1, 16):
            term = float(np.cos(np.pi * k * s / 16)) * even[s - 1]
            if s % 2 == 0:
                plain = plain + term
            else:
                turned = term if turned is None else turned + term
        cosine[k] = plain + turned
        cosine[16 - k] = plain - turned
    for k in range(1, 9):
        plain, turned = None, None
        for s in range(1, 16):
            term = float(np.sin(np.pi * k * s / 16)) * odd[s - 1]
            if s % 2 == 0:
                plain = term if plain is None else plain + term
            else:
                turned = term if turned is None else turned + term
        sine[k] = turned + plain
        sine[16 - k] = turned - plain
    return cosine, sine


def solve_kernel(in_ref, cos_ref, sin_ref, high_table, low_table, out_ref):
    sky = lax.axis_index("sky")
    tile = 2 * lax.axis_index("x") + lax.axis_index("zhi")
    lane = lax.broadcasted_iota(jnp.int32, (8, 128), 1)
    sub = lax.broadcasted_iota(jnp.int32, (8, 128), 0)
    lower = lane < 64
    sign = jnp.where(sub < 4, 1.0, -1.0)
    first = jnp.logical_and(tile == 0, sky == 0)
    packed = jnp.logical_and(sub % 4 == 0, first)

    def swap(v):
        return pltpu.roll(v, 4, v.ndim - 2)

    def bent(v):
        return swap(v) * sign

    main, spill = [], []
    for s in range(SKY):
        rows = [
            jnp.broadcast_to(in_ref[s, :, lanes] + in_ref[SKY + s, :, lanes], (8, 128))
            for lanes in (slice(128 * c, 128 * c + 128) for c in range(5))
        ]
        v = rows[3]
        for c in range(3):
            v = jnp.where(sub % 4 == c, rows[c], v)
        main.append(jnp.where(sub < 4, v, pltpu.roll(v, 64, 1)))
        spill.append(pltpu.roll(rows[4], 0, 1, stride=16, stride_axis=0))
    values = []
    for s in range(SKY):
        up, down = spill[(s - 1) % SKY], spill[(s + 1) % SKY]
        v = main[s] + jnp.where(lane == 0, up, jnp.where(lane == 63, down, 0.0))
        v = jnp.where(lower, v, pltpu.roll(v, 64, 1))
        apart = jnp.where(sub == 4, 0.0, jnp.where(lower, v, swap(v)))
        values.append(jnp.where(packed, apart, v))
    cosine, sine = dft_32(values)
    spectrum = [None] * 32
    spectrum[0], spectrum[16] = cosine[0], cosine[16]
    for k in range(1, 16):
        turned = bent(sine[k])
        spectrum[k], spectrum[32 - k] = cosine[k] + turned, cosine[k] - turned
    twisted = [spectrum[k] * cos_ref[k] + swap(spectrum[k]) * sin_ref[k] for k in range(32)]
    rows = jnp.concatenate(twisted, axis=0)
    pair = dot3(rows, high_table[...], low_table[...])
    pair_c = pair[:, :128].reshape(32, 8, 128)
    pair_s = pair[:, 128:].reshape(32, 8, 128)

    k1 = lax.broadcasted_iota(jnp.int32, (32, 8, 128), 0)
    k2 = lax.broadcasted_iota(jnp.int32, (32, 8, 128), 2) % 64
    nx = k1 + 32 * k2
    nx = jnp.where(nx < N // 2, nx, nx - N)
    n = 4 * sky + sub % 4
    ny = jnp.where(tile > 0, tile + 16 * n, jnp.where(n < 64, 16 * n, 8 + 16 * (n - 64)))
    ny = jnp.where(ny < N // 2, ny, ny - N)
    ny = jnp.where(jnp.logical_and(packed, jnp.logical_not(lower)), -(N // 2), ny)
    along_x = jnp.logical_or(packed, lower)[None]
    squared = nx * nx + (ny * ny)[None]
    wave = jnp.where(along_x, jnp.where(nx == -(N // 2), 0, nx), ny[None])
    unit = 2.0 * np.pi / N
    scale = float(-2.0 / unit / 64.0 / N / N)
    factor = scale * wave.astype(f32) / jnp.maximum(squared, 1).astype(f32)
    kappa_hat = pair_c + swap(pair_s) * sign[None]
    field = factor * (swap(kappa_hat) * (-sign)[None])
    pair = dot3(field.reshape(256, 128), high_table[...], low_table[...])
    values = []
    for k in range(32):
        v = pair[8 * k : 8 * k + 8, :128] - bent(pair[8 * k : 8 * k + 8, 128:])
        values.append(v * cos_ref[k] - swap(v) * sin_ref[k])
    cosine, sine = dft_32(values)
    for s in range(17):
        turned = bent(sine[s]) if 0 < s < 16 else None
        for at in (s,) if turned is None else (s, 32 - s):
            v = cosine[s]
            if turned is not None:
                v = v - turned if at == s else v + turned
            other = swap(pltpu.roll(v, 64, 1))
            joined = jnp.where(lower, jnp.where(sub == 4, other, v), 0.0)
            v = jnp.where(packed, joined, v)
            out_ref[at] = v
            out_ref[SKY + at] = v


def solve(pieces, tables):
    return pl.pallas_call(
        solve_kernel,
        out_shape=jax.ShapeDtypeStruct((64, 8, 128), f32),
        in_specs=[VM] * 5,
        out_specs=VM,
        compiler_params=limit(24),
        name="solve",
    )(pieces, *tables)


def back_for(ahead, eighth_ref, plain, bent, high_table, low_table, out_ref):
    zhi, column = lax.axis_index("zhi"), lax.axis_index("x")
    target = (column + ahead) % 4
    parts = []
    for half in range(2):
        lanes = slice(256 * half, 256 * half + 256)
        turns = (2 * column + half) * (4 * zhi + target) % 8
        cosine, sine = eighth_ref[turns], eighth_ref[8 + turns]
        parts.append(cosine * plain[:, lanes] + sine * bent[:, lanes])
    value = stacked(jnp.concatenate(parts, axis=1))
    out_ref[...] = dot3_stacked(value, high_table[column], low_table[column])


def back_kernel(
    eighth_ref, in_ref, high_table, low_table, far_ref, next_ref, last_ref, plain_ref, bent_ref
):
    value = in_ref[...]
    sub = lax.broadcasted_iota(jnp.int32, (64, 8, 128), 1)
    bent = pltpu.roll(value, 4, 1) * jnp.where(sub < 4, -1.0, 1.0)
    plain, bent = value.reshape(512, 128).T, bent.reshape(512, 128).T
    plain_ref[...] = plain
    bent_ref[...] = bent
    back_for(2, eighth_ref, plain, bent, high_table, low_table, far_ref)
    back_for(1, eighth_ref, plain, bent, high_table, low_table, next_ref)
    back_for(3, eighth_ref, plain, bent, high_table, low_table, last_ref)


def back_rest_kernel(eighth_ref, plain_ref, bent_ref, high_table, low_table, own_ref):
    back_for(0, eighth_ref, plain_ref[...], bent_ref[...], high_table, low_table, own_ref)


def back(pieces, tables):
    turns = np.arange(8) * (2 * np.pi / 8)
    eighth = np.concatenate([np.cos(turns), np.sin(turns)]).astype(np.float32)
    piece = jax.ShapeDtypeStruct((128, 256), f32)
    held = jax.ShapeDtypeStruct((128, 512), f32)
    two, one, three, plain, bent = pl.pallas_call(
        back_kernel,
        out_shape=(piece, piece, piece, held, held),
        in_specs=[SM, VM, VM, VM],
        out_specs=(VM,) * 5,
        compiler_params=limit(24),
        name="back",
    )(eighth, pieces, *tables)
    own = pl.pallas_call(
        back_rest_kernel,
        out_shape=piece,
        in_specs=[SM] + [VM] * 4,
        out_specs=VM,
        compiler_params=limit(24),
        name="back_rest",
    )(eighth, plain, bent, *tables)
    return own, one, two, three


def final_kernel(a_ref, b_ref, c_ref, d_ref, x_ref, y_ref):
    total = (a_ref[...] + b_ref[...]) + (c_ref[...] + d_ref[...])
    x_ref[...] = total[:ROWS]
    y_ref[...] = total[ROWS:]


def final(pieces):
    shape = jax.ShapeDtypeStruct((ROWS, 256), f32)
    return pl.pallas_call(
        final_kernel,
        out_shape=(shape, shape),
        in_specs=[VM] * 4,
        out_specs=(VM, VM),
        compiler_params=limit(24),
        name="final",
    )(*pieces)


def deliver(pieces):
    return [pieces[0]] + [
        lax.ppermute(pieces[a], "x", [(i, (i + a) % 4) for i in range(4)]) for a in (2, 1, 3)
    ]


def body(density, refine, weight_low, weight_high):
    def swap(array, axes, pairs):
        return lax.ppermute(array, axes, pairs + [(b, a) for a, b in pairs])

    odd = lax.axis_index("x") % 2 == 1
    cross = lax.dynamic_slice_in_dim(density, jnp.where(odd, LAYERS - 1, 0), 1, 0)
    cross = swap(cross, LOS, [(3, 4)])
    row, other_row, layer, other_layer = edge_rows(density)
    layer = swap(layer, LOS, [(1, 2), (5, 6)])
    other_layer = swap(other_layer, LOS, [(0, 1), (2, 3), (4, 5), (6, 7)])
    row = swap(row, "sky", [(i, i + 1) for i in range(0, SKY, 2)])
    other_row = swap(other_row, "sky", [(i, (i + 1) % SKY) for i in range(1, SKY, 2)])
    inner = inner_sums(weight_low, weight_high, density, refine)
    tables = halves(forward_table())
    summed = outer_sums(
        weight_low, weight_high, density, (cross, layer, other_layer), (row, other_row), inner, tables
    )
    summed = deliver(summed)
    pieces = lax.all_to_all(turn(summed), ("zhi", "sky"), 0, 0, tiled=True)
    pieces = solve(pieces, twists() + halves(row_table()))
    pieces = lax.all_to_all(pieces, ("zhi", "sky"), 0, 0, tiled=True)
    fields = back(pieces, halves(inverse_table()))
    return final(deliver(fields))


def solution(mesh):
    devices = mesh.devices.reshape(2, 4, SKY)
    inner = Mesh(devices, ("zhi", "x", "sky"))
    placed = (P(LOS, "sky", None), P(LOS, "sky", None), P(LOS), P(LOS))
    return jax.shard_map(
        body,
        mesh=inner,
        in_specs=placed,
        out_specs=(P("sky", LOS), P("sky", LOS)),
        check_vma=False,
    )
```

```python
import functools

import jax
import jax.numpy as jnp
import ml_dtypes
import numpy as np
from jax import lax
from jax.experimental import pallas as pl
from jax.experimental.pallas import tpu as pltpu
from jax.sharding import Mesh, PartitionSpec as P

f32 = jnp.float32
bf16 = jnp.bfloat16
N = 2048
ROWS = 64
SKY = 32
LAYERS = 8
LOS = ("zhi", "x")
MB = 1024 * 1024


def halves(table):
    high = table.astype(np.float32).astype(ml_dtypes.bfloat16)
    low = (table - high.astype(np.float64)).astype(np.float32).astype(ml_dtypes.bfloat16)
    return high, low


def tile_modes(tile):
    n = np.arange(128)
    if tile:
        return tile + 16 * n
    return np.where(n < 64, 16 * n, 8 + 16 * (n - 64))


def tile_order(real, imag):
    pair = np.stack([real.reshape(SKY, 4, -1), imag.reshape(SKY, 4, -1)], axis=1)
    return pair.reshape(256, -1)


def tile_groups(real, imag):
    pair = np.stack([real.reshape(SKY, 4, -1), imag.reshape(SKY, 4, -1)], axis=1)
    return pair.transpose(2, 1, 0, 3).reshape(256, -1)


def forward_table():
    b = np.arange(128)
    tiles = []
    for tile in range(8):
        angle = (tile_modes(tile)[:, None] * b[None, :] % N) * (2 * np.pi / N)
        cosine, sine = np.cos(angle), np.sin(angle)
        if tile:
            real = np.concatenate([cosine, sine], 1)
            imag = np.concatenate([-sine, cosine], 1)
        else:
            zero = np.zeros((64, 128))
            real = np.block([[cosine[:64], zero], [zero, cosine[64:]]])
            imag = np.block([[-sine[:64], zero], [zero, -sine[64:]]])
            imag[0, :128] = (-1.0) ** b
        tiles.append(tile_groups(real, imag).T)
    return np.stack(tiles)


def inverse_table():
    j = np.arange(256)
    tiles = []
    for tile in range(8):
        angle = (tile_modes(tile)[:, None] * j[None, :] % N) * (2 * np.pi / N)
        real, imag = 2 * np.cos(angle), -2 * np.sin(angle)
        if not tile:
            real[0] = 1.0
            imag[0] = (-1.0) ** j
        tiles.append(tile_order(real, imag))
    return np.stack(tiles).reshape(4, 512, 256)


def row_table():
    r = np.arange(64)
    angle = (r[:, None] * r[None, :] % 64) * (2 * np.pi / 64)
    both = np.eye(2)
    return np.concatenate([np.kron(both, np.cos(angle)), np.kron(both, np.sin(angle))], 1)


def twists():
    angle = (np.arange(32)[:, None] * (np.arange(128) % 64)[None, :]) * (2 * np.pi / N)
    sign = np.where(np.arange(8) < 4, 1.0, -1.0)
    cosine = np.broadcast_to(np.cos(angle)[:, None, :], (32, 8, 128))
    sine = np.sin(angle)[:, None, :] * sign[None, :, None]
    return cosine.astype(np.float32), sine.astype(np.float32)


def minmod(a, b):
    return jnp.maximum(jnp.minimum(a, b), 0.0) + jnp.minimum(jnp.maximum(a, b), 0.0)


def split(value):
    high = value.astype(bf16)
    return high, (value - high.astype(f32)).astype(bf16)


def dot3(value, high_table, low_table):
    high, low = split(value)
    dot = functools.partial(jnp.dot, preferred_element_type=f32)
    return dot(high, high_table) + (dot(low, high_table) + dot(high, low_table))


def stacked(value):
    return jnp.concatenate(split(value), axis=0)


def dot3_stacked(parts, high_table, low_table):
    rows = parts.shape[0] // 2
    dot = functools.partial(jnp.dot, preferred_element_type=f32)
    both = dot(parts, high_table)
    return both[:rows] + (both[rows:] + dot(parts[:rows], low_table))


def limit(mib):
    return pltpu.CompilerParams(vmem_limit_bytes=mib * MB)


VM = pl.BlockSpec(memory_space=pltpu.VMEM)
SM = pl.BlockSpec(memory_space=pltpu.SMEM)


def rows_kernel(d_ref, near_ref, far_ref, layer_ref, other_layer_ref):
    odd = lax.axis_index("x") % 2
    layer_ref[0] = d_ref[(LAYERS - 1) * odd]
    other_layer_ref[0] = d_ref[(LAYERS - 1) * (1 - odd)]
    even = lax.axis_index("sky") % 2 == 0
    for z in range(LAYERS):
        first = d_ref[z, 0:16, :].astype(f32)[0:1]
        last = d_ref[z, 48:64, :].astype(f32)[15:16]
        near_ref[z : z + 1, :] = jnp.where(even, last, first)
        far_ref[z : z + 1, :] = jnp.where(even, first, last)


def edge_rows(density):
    shape = jax.ShapeDtypeStruct((LAYERS, N), f32)
    return pl.pallas_call(
        rows_kernel,
        out_shape=(shape, shape) + (jax.ShapeDtypeStruct((1, ROWS, N), bf16),) * 2,
        in_specs=[VM],
        out_specs=(VM,) * 4,
        compiler_params=limit(8),
        name="edge_rows",
    )(density)


def longer(field):
    return jnp.concatenate([field, jnp.zeros((8, N), f32)], axis=0)


def smooth_y(field):
    return 0.75 * field + 0.125 * (pltpu.roll(field, 1, 1) + pltpu.roll(field, N - 1, 1))


CHUNK = 512


def inner_kernel(
    low_ref,
    high_ref,
    d_ref,
    refine_ref,
    kappa_ref,
    mask_ref,
    near_ref,
    calm_ref,
    lifted_ref,
    tx_ref,
    ty_ref,
):
    block = lax.broadcasted_iota(jnp.int32, (256, N), 0)
    lane = lax.broadcasted_iota(jnp.int32, (256, N), 1)
    grow = jnp.where(lane // 8 == block, 1.0, 0.0).astype(bf16)
    coarse = refine_ref[0].astype(f32).astype(bf16)
    mask_ref[...] = jnp.dot(coarse, grow, preferred_element_type=f32)
    for z in range(LAYERS):
        first = d_ref[z, 0:16, :].astype(f32)
        last = d_ref[z, 48:64, :].astype(f32)
        near_ref[0, z : z + 1, :] = first[0:1]
        near_ref[1, z : z + 1, :] = first[1:2]
        near_ref[2, z : z + 1, :] = last[14:15]
        near_ref[3, z : z + 1, :] = last[15:16]

    wide = CHUNK + 256
    row = lax.broadcasted_iota(jnp.int32, (ROWS, CHUNK), 0)
    inside = jnp.logical_and(row > 0, row < ROWS - 1)

    def chunk(i, carry):
        start = pl.multiple_of(i * CHUNK, CHUNK)
        left = pl.multiple_of((start + N - 128) % N, 128)
        right = pl.multiple_of((start + CHUNK) % N, 128)
        base = jnp.zeros((ROWS, CHUNK), f32)
        tz, tx, ty = base, base, base
        centre, step = None, None
        for z in range(LAYERS):
            average = 0.5 * (low_ref[z] + high_ref[z])
            former = centre
            around = jnp.concatenate(
                [
                    d_ref[z, :, pl.ds(left, 128)],
                    d_ref[z, :, pl.ds(start, CHUNK)],
                    d_ref[z, :, pl.ds(right, 128)],
                ],
                axis=1,
            ).astype(f32)
            centre = around[:, 128 : 128 + CHUNK]
            base = base + average * centre
            dy = pltpu.roll(around, wide - 1, 1) - around
            gy = minmod(dy, pltpu.roll(dy, 1, 1))[:, 128 : 128 + CHUNK]
            ty = ty + average * gy
            dx = pltpu.roll(centre, ROWS - 1, 0) - centre
            tx = tx + average * minmod(dx, pltpu.roll(dx, 1, 0))
            if z > 0:
                latter = centre - former
                if step is not None:
                    slope = 0.125 * (high_ref[z - 1] - low_ref[z - 1])
                    tz = tz + slope * minmod(latter, step)
                step = latter
        marked = mask_ref[:, pl.ds(start, CHUNK)]
        marked = jnp.broadcast_to(marked[:, None, :], (8, 8, CHUNK)).reshape(ROWS, CHUNK)
        at = pl.ds(start, CHUNK)
        calm_ref[:, at] = base - marked * base
        lifted_ref[:, at] = marked * (base + tz)
        tx_ref[:, at] = jnp.where(inside, marked * tx, 0.0)
        ty_ref[:, at] = marked * ty
        return carry

    lax.fori_loop(0, N // CHUNK, chunk, 0)
    lifted, tx = lifted_ref[...], tx_ref[...]
    eighth, tilt = 0.125 * lifted, ty_ref[...] * (1.0 / 32.0)
    smooth = 0.75 * lifted + pltpu.roll(eighth + tilt, 1, 1) + pltpu.roll(eighth - tilt, N - 1, 1)
    eighth, tilt = 0.125 * smooth, smooth_y(tx) * (1.0 / 32.0)
    kappa_ref[...] = (
        longer(calm_ref[...] + 0.75 * smooth)
        + pltpu.roll(longer(eighth + tilt), 1, 0)
        + pltpu.roll(longer(eighth - tilt), ROWS + 7, 0)
    )


def inner_sums(low, high, density, refine):
    return pl.pallas_call(
        inner_kernel,
        out_shape=(
            jax.ShapeDtypeStruct((ROWS + 8, N), f32),
            jax.ShapeDtypeStruct((8, N), f32),
            jax.ShapeDtypeStruct((4, LAYERS, N), f32),
        ),
        in_specs=[SM, SM, VM, VM],
        out_specs=(VM,) * 3,
        scratch_shapes=[pltpu.VMEM((ROWS, N), f32)] * 4,
        compiler_params=limit(40),
        cost_estimate=pl.CostEstimate(flops=40_000_000, bytes_accessed=24 * MB, transcendentals=0),
        name="inner_sums",
    )(low, high, density, refine)


def outer_kernel(
    low_ref,
    high_ref,
    d_ref,
    cross_ref,
    layer_ref,
    other_layer_ref,
    row_ref,
    other_row_ref,
    kappa_ref,
    mask_ref,
    near_ref,
    high_table,
    low_table,
    far_ref,
    next_ref,
    last_ref,
    part_ref,
):
    los = lax.axis_index("zhi") * 4 + lax.axis_index("x")
    v0, v1 = d_ref[0].astype(f32), d_ref[1].astype(f32)
    v6, v7 = d_ref[6].astype(f32), d_ref[7].astype(f32)
    odd = los % 2 == 1
    crossing = jnp.logical_or(los == 3, los == 4)
    one = jnp.where(crossing, cross_ref[0], layer_ref[0]).astype(f32)
    other = other_layer_ref[0].astype(f32)
    below = jnp.where(los == 0, v0, jnp.where(odd, other, one))
    above = jnp.where(los == 7, v7, jnp.where(odd, one, other))
    slope0 = 0.125 * (high_ref[0] - low_ref[0])
    slope7 = 0.125 * (high_ref[7] - low_ref[7])
    tz = slope0 * minmod(v1 - v0, v0 - below) + slope7 * minmod(above - v7, v7 - v6)
    mask = mask_ref[...]
    marked = jnp.broadcast_to(mask[:, None, :], (8, 8, N)).reshape(ROWS, N)
    smooth = smooth_y(marked * tz)
    layer = lax.broadcasted_iota(jnp.int32, (LAYERS, 1), 0)
    average = jnp.zeros((LAYERS, 1), f32)
    for z in range(LAYERS):
        average = jnp.where(layer == z, 0.5 * (low_ref[z] + high_ref[z]), average)
    r0, r1, r62, r63 = near_ref[0], near_ref[1], near_ref[2], near_ref[3]
    even = lax.axis_index("sky") % 2 == 0
    before = jnp.where(even, other_row_ref[...], row_ref[...])
    after = jnp.where(even, row_ref[...], other_row_ref[...])
    e0 = jnp.sum(average * minmod(r1 - r0, r0 - before), axis=0, keepdims=True)
    e63 = jnp.sum(average * minmod(after - r63, r63 - r62), axis=0, keepdims=True)
    row = lax.broadcasted_iota(jnp.int32, (8, N), 0)
    e0 = smooth_y(jnp.where(row == 0, mask[0:1] * e0, 0.0)) * (1.0 / 32.0)
    e63 = smooth_y(jnp.where(row == 7, mask[7:8] * e63, 0.0)) * (1.0 / 32.0)
    first = pltpu.roll(e0, 1, 0)
    last = pltpu.roll(e63, 7, 0)
    spill = jnp.where(row == 0, pltpu.roll(e63, 1, 0), -pltpu.roll(e0, 7, 0))
    sides = jnp.concatenate([first, jnp.zeros((ROWS - 16, N), f32), -last, spill], axis=0)
    eighth = longer(0.125 * smooth)
    kappa = (
        (kappa_ref[...] + sides)
        + longer(0.75 * smooth)
        + (pltpu.roll(eighth, 1, 0) + pltpu.roll(eighth, ROWS + 7, 0))
    )
    part = [kappa[:, 128 * a : 128 * a + 128] for a in range(16)]
    even = [part[a] + part[16 - a] for a in range(1, 8)]
    odd = [part[a] - part[16 - a] for a in range(1, 8)]

    def weigh(pairs):
        total = None
        for factor, value in pairs:
            if abs(factor) < 1e-9:
                continue
            term = value if abs(factor - 1) < 1e-9 else factor * value
            total = term if total is None else total + term
        return total

    ends = (part[0] + part[8], part[0] - part[8])
    cosine, sine = [None] * 9, [None] * 9
    for k in range(5):
        factors = [float(np.cos(np.pi * k * a / 8)) for a in range(1, 8)]
        plain = ends[k % 2] + weigh([(factors[a - 1], even[a - 1]) for a in (2, 4, 6)])
        turned = weigh([(factors[a - 1], even[a - 1]) for a in (1, 3, 5, 7)])
        cosine[k] = plain if turned is None else plain + turned
        if k < 4:
            cosine[8 - k] = plain - turned
    for k in range(1, 5):
        factors = [float(-np.sin(np.pi * k * a / 8)) for a in range(1, 8)]
        plain = weigh([(factors[a - 1], odd[a - 1]) for a in (2, 4, 6)])
        turned = weigh([(factors[a - 1], odd[a - 1]) for a in (1, 3, 5, 7)])
        sine[k] = turned if plain is None else turned + plain
        if k < 4:
            sine[8 - k] = turned - plain
    for tile in range(8):
        second = sine[tile] if tile else cosine[8]
        value = jnp.concatenate([cosine[tile], second], axis=1)
        value = jnp.concatenate([value, jnp.zeros((8, 256), f32)], axis=0)
        part_ref[tile] = stacked(value)
    transform_for(2, part_ref, high_table, low_table, far_ref)
    transform_for(1, part_ref, high_table, low_table, next_ref)
    transform_for(3, part_ref, high_table, low_table, last_ref)


def transform_for(ahead, part_ref, high_table, low_table, out_ref):
    target = (lax.axis_index("x") + ahead) % 4
    for half in range(2):
        tile = 2 * target + half
        value = dot3_stacked(part_ref[tile], high_table[tile], low_table[tile])
        for block in (2 * half, 2 * half + 1):
            part = value[:, 128 * (block % 2) : 128 * (block % 2) + 128]
            out_ref[ROWS * block : ROWS * block + ROWS] = part[:ROWS]
            out_ref[4 * ROWS + block : 4 * ROWS + block + 1] = part[ROWS : ROWS + 1]
            out_ref[4 * ROWS + 4 + block : 4 * ROWS + 5 + block] = part[ROWS + 7 : ROWS + 8]


def rest_kernel(part_ref, high_table, low_table, own_ref):
    transform_for(0, part_ref, high_table, low_table, own_ref)


def outer_sums(low, high, density, layers, rows, inner, tables):
    piece = jax.ShapeDtypeStruct((4 * ROWS + 8, 128), f32)
    two, one, three, parts = pl.pallas_call(
        outer_kernel,
        out_shape=(piece, piece, piece, jax.ShapeDtypeStruct((8, 160, 256), bf16)),
        in_specs=[SM, SM] + [VM] * 11,
        out_specs=(VM,) * 4,
        compiler_params=limit(32),
        name="outer_sums",
    )(low, high, density, *layers, *rows, *inner, *tables)
    own = pl.pallas_call(
        rest_kernel,
        out_shape=piece,
        in_specs=[VM] * 3,
        out_specs=VM,
        compiler_params=limit(24),
        name="other_sums",
    )(parts, *tables)
    return own, one, two, three


def turn_kernel(a_ref, b_ref, c_ref, d_ref, out_ref):
    total = (a_ref[...] + b_ref[...]) + (c_ref[...] + d_ref[...])
    none = jnp.zeros((56, 128), f32)
    turned = [
        jnp.concatenate([total[ROWS * block : ROWS * block + ROWS], total[4 * ROWS :], none], axis=0).T
        for block in range(4)
    ]
    lane = lax.broadcasted_iota(jnp.int32, (SKY, 128), 1)
    for half in range(2):
        at = slice(SKY * half, SKY * half + SKY)
        spill = jnp.zeros((SKY, 128), f32)
        for c in range(4):
            block, first = 2 * half + c // 2, 64 * (c % 2)
            real = turned[block][first : first + SKY]
            imag = turned[block][first + SKY : first + 2 * SKY]
            out_ref[at, 0, 128 * c : 128 * c + 128] = jnp.where(
                lane < 64, real, pltpu.roll(imag, 64, 1)
            )
            for sub, part in ((c, real), (4 + c, imag)):
                up = (128 - 16 * sub) % 128
                down = (up + 63) % 128
                spill = jnp.where(lane == up, pltpu.roll(part, (up - 64 - block) % 128, 1), spill)
                spill = jnp.where(
                    lane == down, pltpu.roll(part, (down - 68 - block) % 128, 1), spill
                )
        out_ref[at, 0, 512:640] = spill


def turn(pieces):
    return pl.pallas_call(
        turn_kernel,
        out_shape=jax.ShapeDtypeStruct((64, 1, 640), f32),
        in_specs=[VM] * 4,
        out_specs=VM,
        compiler_params=limit(24),
        name="turn",
    )(*pieces)


def dft_32(values):
    even = [values[s] + values[32 - s] for s in range(1, 16)]
    odd = [values[s] - values[32 - s] for s in range(1, 16)]
    ends = [values[0] + values[16], values[0] - values[16]]
    cosine, sine = [None] * 17, [None] * 17
    for k in range(9):
        plain = ends[k % 2]
        turned = None
        for s in range(1, 16):
            term = float(np.cos(np.pi * k * s / 16)) * even[s - 1]
            if s % 2 == 0:
                plain = plain + term
            else:
                turned = term if turned is None else turned + term
        cosine[k] = plain + turned
        cosine[16 - k] = plain - turned
    for k in range(1, 9):
        plain, turned = None, None
        for s in range(1, 16):
            term = float(np.sin(np.pi * k * s / 16)) * odd[s - 1]
            if s % 2 == 0:
                plain = term if plain is None else plain + term
            else:
                turned = term if turned is None else turned + term
        sine[k] = turned + plain
        sine[16 - k] = turned - plain
    return cosine, sine


def solve_kernel(in_ref, cos_ref, sin_ref, high_table, low_table, out_ref):
    sky = lax.axis_index("sky")
    tile = 2 * lax.axis_index("x") + lax.axis_index("zhi")
    lane = lax.broadcasted_iota(jnp.int32, (8, 128), 1)
    sub = lax.broadcasted_iota(jnp.int32, (8, 128), 0)
    lower = lane < 64
    sign = jnp.where(sub < 4, 1.0, -1.0)
    first = jnp.logical_and(tile == 0, sky == 0)
    packed = jnp.logical_and(sub % 4 == 0, first)

    def swap(v):
        return pltpu.roll(v, 4, v.ndim - 2)

    def bent(v):
        return swap(v) * sign

    main, spill = [], []
    for s in range(SKY):
        rows = [
            jnp.broadcast_to(in_ref[s, :, lanes] + in_ref[SKY + s, :, lanes], (8, 128))
            for lanes in (slice(128 * c, 128 * c + 128) for c in range(5))
        ]
        v = rows[3]
        for c in range(3):
            v = jnp.where(sub % 4 == c, rows[c], v)
        main.append(jnp.where(sub < 4, v, pltpu.roll(v, 64, 1)))
        spill.append(pltpu.roll(rows[4], 0, 1, stride=16, stride_axis=0))
    values = []
    for s in range(SKY):
        up, down = spill[(s - 1) % SKY], spill[(s + 1) % SKY]
        v = main[s] + jnp.where(lane == 0, up, jnp.where(lane == 63, down, 0.0))
        v = jnp.where(lower, v, pltpu.roll(v, 64, 1))
        apart = jnp.where(sub == 4, 0.0, jnp.where(lower, v, swap(v)))
        values.append(jnp.where(packed, apart, v))
    cosine, sine = dft_32(values)
    spectrum = [None] * 32
    spectrum[0], spectrum[16] = cosine[0], cosine[16]
    for k in range(1, 16):
        turned = bent(sine[k])
        spectrum[k], spectrum[32 - k] = cosine[k] + turned, cosine[k] - turned
    twisted = [spectrum[k] * cos_ref[k] + swap(spectrum[k]) * sin_ref[k] for k in range(32)]
    rows = jnp.concatenate(twisted, axis=0)
    pair = dot3(rows, high_table[...], low_table[...])
    pair_c = pair[:, :128].reshape(32, 8, 128)
    pair_s = pair[:, 128:].reshape(32, 8, 128)

    k1 = lax.broadcasted_iota(jnp.int32, (32, 8, 128), 0)
    k2 = lax.broadcasted_iota(jnp.int32, (32, 8, 128), 2) % 64
    nx = k1 + 32 * k2
    nx = jnp.where(nx < N // 2, nx, nx - N)
    n = 4 * sky + sub % 4
    ny = jnp.where(tile > 0, tile + 16 * n, jnp.where(n < 64, 16 * n, 8 + 16 * (n - 64)))
    ny = jnp.where(ny < N // 2, ny, ny - N)
    ny = jnp.where(jnp.logical_and(packed, jnp.logical_not(lower)), -(N // 2), ny)
    along_x = jnp.logical_or(packed, lower)[None]
    squared = nx * nx + (ny * ny)[None]
    wave = jnp.where(along_x, jnp.where(nx == -(N // 2), 0, nx), ny[None])
    unit = 2.0 * np.pi / N
    scale = float(-2.0 / unit / 64.0 / N / N)
    factor = scale * wave.astype(f32) / jnp.maximum(squared, 1).astype(f32)
    kappa_hat = pair_c + swap(pair_s) * sign[None]
    field = factor * (swap(kappa_hat) * (-sign)[None])
    pair = dot3(field.reshape(256, 128), high_table[...], low_table[...])
    values = []
    for k in range(32):
        v = pair[8 * k : 8 * k + 8, :128] - bent(pair[8 * k : 8 * k + 8, 128:])
        values.append(v * cos_ref[k] - swap(v) * sin_ref[k])
    cosine, sine = dft_32(values)
    for s in range(17):
        turned = bent(sine[s]) if 0 < s < 16 else None
        for at in (s,) if turned is None else (s, 32 - s):
            v = cosine[s]
            if turned is not None:
                v = v - turned if at == s else v + turned
            other = swap(pltpu.roll(v, 64, 1))
            joined = jnp.where(lower, jnp.where(sub == 4, other, v), 0.0)
            v = jnp.where(packed, joined, v)
            out_ref[at] = v
            out_ref[SKY + at] = v


def solve(pieces, tables):
    return pl.pallas_call(
        solve_kernel,
        out_shape=jax.ShapeDtypeStruct((64, 8, 128), f32),
        in_specs=[VM] * 5,
        out_specs=VM,
        compiler_params=limit(24),
        name="solve",
    )(pieces, *tables)


def back_for(ahead, eighth_ref, plain, bent, high_table, low_table, out_ref):
    zhi, column = lax.axis_index("zhi"), lax.axis_index("x")
    target = (column + ahead) % 4
    parts = []
    for half in range(2):
        lanes = slice(256 * half, 256 * half + 256)
        turns = (2 * column + half) * (4 * zhi + target) % 8
        cosine, sine = eighth_ref[turns], eighth_ref[8 + turns]
        parts.append(cosine * plain[:, lanes] + sine * bent[:, lanes])
    value = stacked(jnp.concatenate(parts, axis=1))
    out_ref[...] = dot3_stacked(value, high_table[column], low_table[column])


def back_kernel(
    eighth_ref, in_ref, high_table, low_table, far_ref, next_ref, last_ref, plain_ref, bent_ref
):
    value = in_ref[...]
    sub = lax.broadcasted_iota(jnp.int32, (64, 8, 128), 1)
    bent = pltpu.roll(value, 4, 1) * jnp.where(sub < 4, -1.0, 1.0)
    plain, bent = value.reshape(512, 128).T, bent.reshape(512, 128).T
    plain_ref[...] = plain
    bent_ref[...] = bent
    back_for(2, eighth_ref, plain, bent, high_table, low_table, far_ref)
    back_for(1, eighth_ref, plain, bent, high_table, low_table, next_ref)
    back_for(3, eighth_ref, plain, bent, high_table, low_table, last_ref)


def back_rest_kernel(eighth_ref, plain_ref, bent_ref, high_table, low_table, own_ref):
    back_for(0, eighth_ref, plain_ref[...], bent_ref[...], high_table, low_table, own_ref)


def back(pieces, tables):
    turns = np.arange(8) * (2 * np.pi / 8)
    eighth = np.concatenate([np.cos(turns), np.sin(turns)]).astype(np.float32)
    piece = jax.ShapeDtypeStruct((128, 256), f32)
    held = jax.ShapeDtypeStruct((128, 512), f32)
    two, one, three, plain, bent = pl.pallas_call(
        back_kernel,
        out_shape=(piece, piece, piece, held, held),
        in_specs=[SM, VM, VM, VM],
        out_specs=(VM,) * 5,
        compiler_params=limit(24),
        name="back",
    )(eighth, pieces, *tables)
    own = pl.pallas_call(
        back_rest_kernel,
        out_shape=piece,
        in_specs=[SM] + [VM] * 4,
        out_specs=VM,
        compiler_params=limit(24),
        name="back_rest",
    )(eighth, plain, bent, *tables)
    return own, one, two, three


def early_kernel(a_ref, b_ref, c_ref, sum_ref):
    sum_ref[...] = (a_ref[...] + b_ref[...]) + c_ref[...]


def final_kernel(sum_ref, last_ref, x_ref, y_ref):
    total = sum_ref[...] + last_ref[...]
    x_ref[...] = total[:ROWS]
    y_ref[...] = total[ROWS:]


def final(pieces):
    early = pl.pallas_call(
        early_kernel,
        out_shape=jax.ShapeDtypeStruct((128, 256), f32),
        in_specs=[VM] * 3,
        out_specs=VM,
        compiler_params=limit(24),
        name="early",
    )(*pieces[:3])
    shape = jax.ShapeDtypeStruct((ROWS, 256), f32)
    return pl.pallas_call(
        final_kernel,
        out_shape=(shape, shape),
        in_specs=[VM] * 2,
        out_specs=(VM, VM),
        compiler_params=limit(24),
        name="final",
    )(early, pieces[3])


def deliver(pieces):
    return [pieces[0]] + [
        lax.ppermute(pieces[a], "x", [(i, (i + a) % 4) for i in range(4)]) for a in (2, 1, 3)
    ]


def body(density, refine, weight_low, weight_high):
    def swap(array, axes, pairs):
        return lax.ppermute(array, axes, pairs + [(b, a) for a, b in pairs])

    odd = lax.axis_index("x") % 2 == 1
    cross = lax.dynamic_slice_in_dim(density, jnp.where(odd, LAYERS - 1, 0), 1, 0)
    cross = swap(cross, LOS, [(3, 4)])
    row, other_row, layer, other_layer = edge_rows(density)
    layer = swap(layer, LOS, [(1, 2), (5, 6)])
    other_layer = swap(other_layer, LOS, [(0, 1), (2, 3), (4, 5), (6, 7)])
    row = swap(row, "sky", [(i, i + 1) for i in range(0, SKY, 2)])
    other_row = swap(other_row, "sky", [(i, (i + 1) % SKY) for i in range(1, SKY, 2)])
    inner = inner_sums(weight_low, weight_high, density, refine)
    tables = halves(forward_table())
    summed = outer_sums(
        weight_low, weight_high, density, (cross, layer, other_layer), (row, other_row), inner, tables
    )
    summed = deliver(summed)
    pieces = lax.all_to_all(turn(summed), ("zhi", "sky"), 0, 0, tiled=True)
    pieces = solve(pieces, twists() + halves(row_table()))
    pieces = lax.all_to_all(pieces, ("zhi", "sky"), 0, 0, tiled=True)
    fields = back(pieces, halves(inverse_table()))
    return final(deliver(fields))


def solution(mesh):
    devices = mesh.devices.reshape(2, 4, SKY)
    inner = Mesh(devices, ("zhi", "x", "sky"))
    placed = (P(LOS, "sky", None), P(LOS, "sky", None), P(LOS), P(LOS))
    return jax.shard_map(
        body,
        mesh=inner,
        in_specs=placed,
        out_specs=(P("sky", LOS), P("sky", LOS)),
        check_vma=False,
    )
```

```python
import functools

import jax
import jax.numpy as jnp
import ml_dtypes
import numpy as np
from jax import lax
from jax.experimental import pallas as pl
from jax.experimental.pallas import tpu as pltpu
from jax.sharding import Mesh, PartitionSpec as P

f32 = jnp.float32
bf16 = jnp.bfloat16
N = 2048
ROWS = 64
SKY = 32
LAYERS = 8
LOS = ("zhi", "x")
MB = 1024 * 1024


def halves(table):
    high = table.astype(np.float32).astype(ml_dtypes.bfloat16)
    low = (table - high.astype(np.float64)).astype(np.float32).astype(ml_dtypes.bfloat16)
    return high, low


def tile_modes(tile):
    n = np.arange(128)
    if tile:
        return tile + 16 * n
    return np.where(n < 64, 16 * n, 8 + 16 * (n - 64))


def tile_order(real, imag):
    pair = np.stack([real.reshape(SKY, 4, -1), imag.reshape(SKY, 4, -1)], axis=1)
    return pair.reshape(256, -1)


def tile_groups(real, imag):
    pair = np.stack([real.reshape(SKY, 4, -1), imag.reshape(SKY, 4, -1)], axis=1)
    return pair.transpose(2, 1, 0, 3).reshape(256, -1)


def forward_table():
    b = np.arange(128)
    tiles = []
    for tile in range(8):
        angle = (tile_modes(tile)[:, None] * b[None, :] % N) * (2 * np.pi / N)
        cosine, sine = np.cos(angle), np.sin(angle)
        if tile:
            real = np.concatenate([cosine, sine], 1)
            imag = np.concatenate([-sine, cosine], 1)
        else:
            zero = np.zeros((64, 128))
            real = np.block([[cosine[:64], zero], [zero, cosine[64:]]])
            imag = np.block([[-sine[:64], zero], [zero, -sine[64:]]])
            imag[0, :128] = (-1.0) ** b
        tiles.append(tile_groups(real, imag).T)
    return np.stack(tiles)


def inverse_table():
    j = np.arange(256)
    tiles = []
    for tile in range(8):
        angle = (tile_modes(tile)[:, None] * j[None, :] % N) * (2 * np.pi / N)
        real, imag = 2 * np.cos(angle), -2 * np.sin(angle)
        if not tile:
            real[0] = 1.0
            imag[0] = (-1.0) ** j
        tiles.append(tile_order(real, imag))
    return np.stack(tiles).reshape(4, 512, 256)


def row_table():
    r = np.arange(64)
    angle = (r[:, None] * r[None, :] % 64) * (2 * np.pi / 64)
    both = np.eye(2)
    return np.concatenate([np.kron(both, np.cos(angle)), np.kron(both, np.sin(angle))], 1)


def twists():
    angle = (np.arange(32)[:, None] * (np.arange(128) % 64)[None, :]) * (2 * np.pi / N)
    sign = np.where(np.arange(8) < 4, 1.0, -1.0)
    cosine = np.broadcast_to(np.cos(angle)[:, None, :], (32, 8, 128))
    sine = np.sin(angle)[:, None, :] * sign[None, :, None]
    return cosine.astype(np.float32), sine.astype(np.float32)


def minmod(a, b):
    return jnp.maximum(jnp.minimum(a, b), 0.0) + jnp.minimum(jnp.maximum(a, b), 0.0)


def split(value):
    high = value.astype(bf16)
    return high, (value - high.astype(f32)).astype(bf16)


def dot3(value, high_table, low_table):
    high, low = split(value)
    dot = functools.partial(jnp.dot, preferred_element_type=f32)
    return dot(high, high_table) + (dot(low, high_table) + dot(high, low_table))


def stacked(value):
    return jnp.concatenate(split(value), axis=0)


def dot3_stacked(parts, high_table, low_table):
    rows = parts.shape[0] // 2
    dot = functools.partial(jnp.dot, preferred_element_type=f32)
    both = dot(parts, high_table)
    return both[:rows] + (both[rows:] + dot(parts[:rows], low_table))


def limit(mib):
    return pltpu.CompilerParams(vmem_limit_bytes=mib * MB)


VM = pl.BlockSpec(memory_space=pltpu.VMEM)
SM = pl.BlockSpec(memory_space=pltpu.SMEM)


def rows_kernel(d_ref, near_ref, far_ref, layer_ref, other_layer_ref):
    odd = lax.axis_index("x") % 2
    layer_ref[0] = d_ref[(LAYERS - 1) * odd]
    other_layer_ref[0] = d_ref[(LAYERS - 1) * (1 - odd)]
    even = lax.axis_index("sky") % 2 == 0
    for z in range(LAYERS):
        first = d_ref[z, 0:16, :].astype(f32)[0:1]
        last = d_ref[z, 48:64, :].astype(f32)[15:16]
        near_ref[z : z + 1, :] = jnp.where(even, last, first)
        far_ref[z : z + 1, :] = jnp.where(even, first, last)


def edge_rows(density):
    shape = jax.ShapeDtypeStruct((LAYERS, N), f32)
    return pl.pallas_call(
        rows_kernel,
        out_shape=(shape, shape) + (jax.ShapeDtypeStruct((1, ROWS, N), bf16),) * 2,
        in_specs=[VM],
        out_specs=(VM,) * 4,
        compiler_params=limit(8),
        name="edge_rows",
    )(density)


def longer(field):
    return jnp.concatenate([field, jnp.zeros((8, N), f32)], axis=0)


def smooth_y(field):
    return 0.75 * field + 0.125 * (pltpu.roll(field, 1, 1) + pltpu.roll(field, N - 1, 1))


CHUNK = 1024


def inner_kernel(
    low_ref,
    high_ref,
    d_ref,
    refine_ref,
    kappa_ref,
    mask_ref,
    near_ref,
    calm_ref,
    lifted_ref,
    tx_ref,
    ty_ref,
):
    block = lax.broadcasted_iota(jnp.int32, (256, N), 0)
    lane = lax.broadcasted_iota(jnp.int32, (256, N), 1)
    grow = jnp.where(lane // 8 == block, 1.0, 0.0).astype(bf16)
    coarse = refine_ref[0].astype(f32).astype(bf16)
    mask_ref[...] = jnp.dot(coarse, grow, preferred_element_type=f32)
    for z in range(LAYERS):
        first = d_ref[z, 0:16, :].astype(f32)
        last = d_ref[z, 48:64, :].astype(f32)
        near_ref[0, z : z + 1, :] = first[0:1]
        near_ref[1, z : z + 1, :] = first[1:2]
        near_ref[2, z : z + 1, :] = last[14:15]
        near_ref[3, z : z + 1, :] = last[15:16]

    wide = CHUNK + 256
    row = lax.broadcasted_iota(jnp.int32, (ROWS, CHUNK), 0)
    inside = jnp.logical_and(row > 0, row < ROWS - 1)

    def chunk(i, carry):
        start = pl.multiple_of(i * CHUNK, CHUNK)
        left = pl.multiple_of((start + N - 128) % N, 128)
        right = pl.multiple_of((start + CHUNK) % N, 128)
        base = jnp.zeros((ROWS, CHUNK), f32)
        tz, tx, ty = base, base, base
        centre, step = None, None
        for z in range(LAYERS):
            average = 0.5 * (low_ref[z] + high_ref[z])
            former = centre
            around = jnp.concatenate(
                [
                    d_ref[z, :, pl.ds(left, 128)],
                    d_ref[z, :, pl.ds(start, CHUNK)],
                    d_ref[z, :, pl.ds(right, 128)],
                ],
                axis=1,
            ).astype(f32)
            centre = around[:, 128 : 128 + CHUNK]
            base = base + average * centre
            dy = pltpu.roll(around, wide - 1, 1) - around
            gy = minmod(dy, pltpu.roll(dy, 1, 1))[:, 128 : 128 + CHUNK]
            ty = ty + average * gy
            dx = pltpu.roll(centre, ROWS - 1, 0) - centre
            tx = tx + average * minmod(dx, pltpu.roll(dx, 1, 0))
            if z > 0:
                latter = centre - former
                if step is not None:
                    slope = 0.125 * (high_ref[z - 1] - low_ref[z - 1])
                    tz = tz + slope * minmod(latter, step)
                step = latter
        marked = mask_ref[:, pl.ds(start, CHUNK)]
        marked = jnp.broadcast_to(marked[:, None, :], (8, 8, CHUNK)).reshape(ROWS, CHUNK)
        at = pl.ds(start, CHUNK)
        calm_ref[:, at] = base - marked * base
        lifted_ref[:, at] = marked * (base + tz)
        tx_ref[:, at] = jnp.where(inside, marked * tx, 0.0)
        ty_ref[:, at] = marked * ty
        return carry

    lax.fori_loop(0, N // CHUNK, chunk, 0)
    lifted, tx = lifted_ref[...], tx_ref[...]
    eighth, tilt = 0.125 * lifted, ty_ref[...] * (1.0 / 32.0)
    smooth = 0.75 * lifted + pltpu.roll(eighth + tilt, 1, 1) + pltpu.roll(eighth - tilt, N - 1, 1)
    eighth, tilt = 0.125 * smooth, smooth_y(tx) * (1.0 / 32.0)
    kappa_ref[...] = (
        longer(calm_ref[...] + 0.75 * smooth)
        + pltpu.roll(longer(eighth + tilt), 1, 0)
        + pltpu.roll(longer(eighth - tilt), ROWS + 7, 0)
    )


def inner_sums(low, high, density, refine):
    return pl.pallas_call(
        inner_kernel,
        out_shape=(
            jax.ShapeDtypeStruct((ROWS + 8, N), f32),
            jax.ShapeDtypeStruct((8, N), f32),
            jax.ShapeDtypeStruct((4, LAYERS, N), f32),
        ),
        in_specs=[SM, SM, VM, VM],
        out_specs=(VM,) * 3,
        scratch_shapes=[pltpu.VMEM((ROWS, N), f32)] * 4,
        compiler_params=limit(40),
        cost_estimate=pl.CostEstimate(flops=40_000_000, bytes_accessed=24 * MB, transcendentals=0),
        name="inner_sums",
    )(low, high, density, refine)


def outer_kernel(
    low_ref,
    high_ref,
    d_ref,
    cross_ref,
    layer_ref,
    other_layer_ref,
    row_ref,
    other_row_ref,
    kappa_ref,
    mask_ref,
    near_ref,
    high_table,
    low_table,
    far_ref,
    next_ref,
    last_ref,
    part_ref,
):
    los = lax.axis_index("zhi") * 4 + lax.axis_index("x")
    v0, v1 = d_ref[0].astype(f32), d_ref[1].astype(f32)
    v6, v7 = d_ref[6].astype(f32), d_ref[7].astype(f32)
    odd = los % 2 == 1
    crossing = jnp.logical_or(los == 3, los == 4)
    one = jnp.where(crossing, cross_ref[0], layer_ref[0]).astype(f32)
    other = other_layer_ref[0].astype(f32)
    below = jnp.where(los == 0, v0, jnp.where(odd, other, one))
    above = jnp.where(los == 7, v7, jnp.where(odd, one, other))
    slope0 = 0.125 * (high_ref[0] - low_ref[0])
    slope7 = 0.125 * (high_ref[7] - low_ref[7])
    tz = slope0 * minmod(v1 - v0, v0 - below) + slope7 * minmod(above - v7, v7 - v6)
    mask = mask_ref[...]
    marked = jnp.broadcast_to(mask[:, None, :], (8, 8, N)).reshape(ROWS, N)
    smooth = smooth_y(marked * tz)
    layer = lax.broadcasted_iota(jnp.int32, (LAYERS, 1), 0)
    average = jnp.zeros((LAYERS, 1), f32)
    for z in range(LAYERS):
        average = jnp.where(layer == z, 0.5 * (low_ref[z] + high_ref[z]), average)
    r0, r1, r62, r63 = near_ref[0], near_ref[1], near_ref[2], near_ref[3]
    even = lax.axis_index("sky") % 2 == 0
    before = jnp.where(even, other_row_ref[...], row_ref[...])
    after = jnp.where(even, row_ref[...], other_row_ref[...])
    e0 = jnp.sum(average * minmod(r1 - r0, r0 - before), axis=0, keepdims=True)
    e63 = jnp.sum(average * minmod(after - r63, r63 - r62), axis=0, keepdims=True)
    row = lax.broadcasted_iota(jnp.int32, (8, N), 0)
    e0 = smooth_y(jnp.where(row == 0, mask[0:1] * e0, 0.0)) * (1.0 / 32.0)
    e63 = smooth_y(jnp.where(row == 7, mask[7:8] * e63, 0.0)) * (1.0 / 32.0)
    first = pltpu.roll(e0, 1, 0)
    last = pltpu.roll(e63, 7, 0)
    spill = jnp.where(row == 0, pltpu.roll(e63, 1, 0), -pltpu.roll(e0, 7, 0))
    sides = jnp.concatenate([first, jnp.zeros((ROWS - 16, N), f32), -last, spill], axis=0)
    eighth = longer(0.125 * smooth)
    kappa = (
        (kappa_ref[...] + sides)
        + longer(0.75 * smooth)
        + (pltpu.roll(eighth, 1, 0) + pltpu.roll(eighth, ROWS + 7, 0))
    )
    part = [kappa[:, 128 * a : 128 * a + 128] for a in range(16)]
    even = [part[a] + part[16 - a] for a in range(1, 8)]
    odd = [part[a] - part[16 - a] for a in range(1, 8)]

    def weigh(pairs):
        total = None
        for factor, value in pairs:
            if abs(factor) < 1e-9:
                continue
            term = value if abs(factor - 1) < 1e-9 else factor * value
            total = term if total is None else total + term
        return total

    ends = (part[0] + part[8], part[0] - part[8])
    cosine, sine = [None] * 9, [None] * 9
    for k in range(5):
        factors = [float(np.cos(np.pi * k * a / 8)) for a in range(1, 8)]
        plain = ends[k % 2] + weigh([(factors[a - 1], even[a - 1]) for a in (2, 4, 6)])
        turned = weigh([(factors[a - 1], even[a - 1]) for a in (1, 3, 5, 7)])
        cosine[k] = plain if turned is None else plain + turned
        if k < 4:
            cosine[8 - k] = plain - turned
    for k in range(1, 5):
        factors = [float(-np.sin(np.pi * k * a / 8)) for a in range(1, 8)]
        plain = weigh([(factors[a - 1], odd[a - 1]) for a in (2, 4, 6)])
        turned = weigh([(factors[a - 1], odd[a - 1]) for a in (1, 3, 5, 7)])
        sine[k] = turned if plain is None else turned + plain
        if k < 4:
            sine[8 - k] = turned - plain
    for tile in range(8):
        second = sine[tile] if tile else cosine[8]
        value = jnp.concatenate([cosine[tile], second], axis=1)
        value = jnp.concatenate([value, jnp.zeros((8, 256), f32)], axis=0)
        part_ref[tile] = stacked(value)
    transform_for(2, part_ref, high_table, low_table, far_ref)
    transform_for(1, part_ref, high_table, low_table, next_ref)
    transform_for(3, part_ref, high_table, low_table, last_ref)


def transform_for(ahead, part_ref, high_table, low_table, out_ref):
    target = (lax.axis_index("x") + ahead) % 4
    for half in range(2):
        tile = 2 * target + half
        value = dot3_stacked(part_ref[tile], high_table[tile], low_table[tile])
        for block in (2 * half, 2 * half + 1):
            part = value[:, 128 * (block % 2) : 128 * (block % 2) + 128]
            out_ref[ROWS * block : ROWS * block + ROWS] = part[:ROWS]
            out_ref[4 * ROWS + block : 4 * ROWS + block + 1] = part[ROWS : ROWS + 1]
            out_ref[4 * ROWS + 4 + block : 4 * ROWS + 5 + block] = part[ROWS + 7 : ROWS + 8]


def rest_kernel(part_ref, high_table, low_table, own_ref):
    transform_for(0, part_ref, high_table, low_table, own_ref)


def outer_sums(low, high, density, layers, rows, inner, tables):
    piece = jax.ShapeDtypeStruct((4 * ROWS + 8, 128), f32)
    two, one, three, parts = pl.pallas_call(
        outer_kernel,
        out_shape=(piece, piece, piece, jax.ShapeDtypeStruct((8, 160, 256), bf16)),
        in_specs=[SM, SM] + [VM] * 11,
        out_specs=(VM,) * 4,
        compiler_params=limit(32),
        name="outer_sums",
    )(low, high, density, *layers, *rows, *inner, *tables)
    own = pl.pallas_call(
        rest_kernel,
        out_shape=piece,
        in_specs=[VM] * 3,
        out_specs=VM,
        compiler_params=limit(24),
        name="other_sums",
    )(parts, *tables)
    return own, one, two, three


def turn_kernel(a_ref, b_ref, c_ref, d_ref, out_ref):
    total = (a_ref[...] + b_ref[...]) + (c_ref[...] + d_ref[...])
    none = jnp.zeros((56, 128), f32)
    turned = [
        jnp.concatenate([total[ROWS * block : ROWS * block + ROWS], total[4 * ROWS :], none], axis=0).T
        for block in range(4)
    ]
    lane = lax.broadcasted_iota(jnp.int32, (SKY, 128), 1)
    for half in range(2):
        at = slice(SKY * half, SKY * half + SKY)
        spill = jnp.zeros((SKY, 128), f32)
        for c in range(4):
            block, first = 2 * half + c // 2, 64 * (c % 2)
            real = turned[block][first : first + SKY]
            imag = turned[block][first + SKY : first + 2 * SKY]
            out_ref[at, 0, 128 * c : 128 * c + 128] = jnp.where(
                lane < 64, real, pltpu.roll(imag, 64, 1)
            )
            for sub, part in ((c, real), (4 + c, imag)):
                up = (128 - 16 * sub) % 128
                down = (up + 63) % 128
                spill = jnp.where(lane == up, pltpu.roll(part, (up - 64 - block) % 128, 1), spill)
                spill = jnp.where(
                    lane == down, pltpu.roll(part, (down - 68 - block) % 128, 1), spill
                )
        out_ref[at, 0, 512:640] = spill


def turn(pieces):
    return pl.pallas_call(
        turn_kernel,
        out_shape=jax.ShapeDtypeStruct((64, 1, 640), f32),
        in_specs=[VM] * 4,
        out_specs=VM,
        compiler_params=limit(24),
        name="turn",
    )(*pieces)


def dft_32(values):
    even = [values[s] + values[32 - s] for s in range(1, 16)]
    odd = [values[s] - values[32 - s] for s in range(1, 16)]
    ends = [values[0] + values[16], values[0] - values[16]]
    cosine, sine = [None] * 17, [None] * 17
    for k in range(9):
        plain = ends[k % 2]
        turned = None
        for s in range(1, 16):
            term = float(np.cos(np.pi * k * s / 16)) * even[s - 1]
            if s % 2 == 0:
                plain = plain + term
            else:
                turned = term if turned is None else turned + term
        cosine[k] = plain + turned
        cosine[16 - k] = plain - turned
    for k in range(1, 9):
        plain, turned = None, None
        for s in range(1, 16):
            term = float(np.sin(np.pi * k * s / 16)) * odd[s - 1]
            if s % 2 == 0:
                plain = term if plain is None else plain + term
            else:
                turned = term if turned is None else turned + term
        sine[k] = turned + plain
        sine[16 - k] = turned - plain
    return cosine, sine


def solve_kernel(in_ref, cos_ref, sin_ref, high_table, low_table, out_ref):
    sky = lax.axis_index("sky")
    tile = 2 * lax.axis_index("x") + lax.axis_index("zhi")
    lane = lax.broadcasted_iota(jnp.int32, (8, 128), 1)
    sub = lax.broadcasted_iota(jnp.int32, (8, 128), 0)
    lower = lane < 64
    sign = jnp.where(sub < 4, 1.0, -1.0)
    first = jnp.logical_and(tile == 0, sky == 0)
    packed = jnp.logical_and(sub % 4 == 0, first)

    def swap(v):
        return pltpu.roll(v, 4, v.ndim - 2)

    def bent(v):
        return swap(v) * sign

    main, spill = [], []
    for s in range(SKY):
        rows = [
            jnp.broadcast_to(in_ref[s, :, lanes] + in_ref[SKY + s, :, lanes], (8, 128))
            for lanes in (slice(128 * c, 128 * c + 128) for c in range(5))
        ]
        v = rows[3]
        for c in range(3):
            v = jnp.where(sub % 4 == c, rows[c], v)
        main.append(jnp.where(sub < 4, v, pltpu.roll(v, 64, 1)))
        spill.append(pltpu.roll(rows[4], 0, 1, stride=16, stride_axis=0))
    values = []
    for s in range(SKY):
        up, down = spill[(s - 1) % SKY], spill[(s + 1) % SKY]
        v = main[s] + jnp.where(lane == 0, up, jnp.where(lane == 63, down, 0.0))
        v = jnp.where(lower, v, pltpu.roll(v, 64, 1))
        apart = jnp.where(sub == 4, 0.0, jnp.where(lower, v, swap(v)))
        values.append(jnp.where(packed, apart, v))
    cosine, sine = dft_32(values)
    spectrum = [None] * 32
    spectrum[0], spectrum[16] = cosine[0], cosine[16]
    for k in range(1, 16):
        turned = bent(sine[k])
        spectrum[k], spectrum[32 - k] = cosine[k] + turned, cosine[k] - turned
    twisted = [spectrum[k] * cos_ref[k] + swap(spectrum[k]) * sin_ref[k] for k in range(32)]
    rows = jnp.concatenate(twisted, axis=0)
    pair = dot3(rows, high_table[...], low_table[...])
    pair_c = pair[:, :128].reshape(32, 8, 128)
    pair_s = pair[:, 128:].reshape(32, 8, 128)

    k1 = lax.broadcasted_iota(jnp.int32, (32, 8, 128), 0)
    k2 = lax.broadcasted_iota(jnp.int32, (32, 8, 128), 2) % 64
    nx = k1 + 32 * k2
    nx = jnp.where(nx < N // 2, nx, nx - N)
    n = 4 * sky + sub % 4
    ny = jnp.where(tile > 0, tile + 16 * n, jnp.where(n < 64, 16 * n, 8 + 16 * (n - 64)))
    ny = jnp.where(ny < N // 2, ny, ny - N)
    ny = jnp.where(jnp.logical_and(packed, jnp.logical_not(lower)), -(N // 2), ny)
    along_x = jnp.logical_or(packed, lower)[None]
    squared = nx * nx + (ny * ny)[None]
    wave = jnp.where(along_x, jnp.where(nx == -(N // 2), 0, nx), ny[None])
    unit = 2.0 * np.pi / N
    scale = float(-2.0 / unit / 64.0 / N / N)
    factor = scale * wave.astype(f32) / jnp.maximum(squared, 1).astype(f32)
    kappa_hat = pair_c + swap(pair_s) * sign[None]
    field = factor * (swap(kappa_hat) * (-sign)[None])
    pair = dot3(field.reshape(256, 128), high_table[...], low_table[...])
    values = []
    for k in range(32):
        v = pair[8 * k : 8 * k + 8, :128] - bent(pair[8 * k : 8 * k + 8, 128:])
        values.append(v * cos_ref[k] - swap(v) * sin_ref[k])
    cosine, sine = dft_32(values)
    for s in range(17):
        turned = bent(sine[s]) if 0 < s < 16 else None
        for at in (s,) if turned is None else (s, 32 - s):
            v = cosine[s]
            if turned is not None:
                v = v - turned if at == s else v + turned
            other = swap(pltpu.roll(v, 64, 1))
            joined = jnp.where(lower, jnp.where(sub == 4, other, v), 0.0)
            v = jnp.where(packed, joined, v)
            out_ref[at] = v
            out_ref[SKY + at] = v


def solve(pieces, tables):
    return pl.pallas_call(
        solve_kernel,
        out_shape=jax.ShapeDtypeStruct((64, 8, 128), f32),
        in_specs=[VM] * 5,
        out_specs=VM,
        compiler_params=limit(24),
        name="solve",
    )(pieces, *tables)


def back_for(ahead, eighth_ref, plain, bent, high_table, low_table, out_ref):
    zhi, column = lax.axis_index("zhi"), lax.axis_index("x")
    target = (column + ahead) % 4
    parts = []
    for half in range(2):
        lanes = slice(256 * half, 256 * half + 256)
        turns = (2 * column + half) * (4 * zhi + target) % 8
        cosine, sine = eighth_ref[turns], eighth_ref[8 + turns]
        parts.append(cosine * plain[:, lanes] + sine * bent[:, lanes])
    value = stacked(jnp.concatenate(parts, axis=1))
    out_ref[...] = dot3_stacked(value, high_table[column], low_table[column])


def back_kernel(
    eighth_ref, in_ref, high_table, low_table, far_ref, next_ref, last_ref, plain_ref, bent_ref
):
    value = in_ref[...]
    sub = lax.broadcasted_iota(jnp.int32, (64, 8, 128), 1)
    bent = pltpu.roll(value, 4, 1) * jnp.where(sub < 4, -1.0, 1.0)
    plain, bent = value.reshape(512, 128).T, bent.reshape(512, 128).T
    plain_ref[...] = plain
    bent_ref[...] = bent
    back_for(2, eighth_ref, plain, bent, high_table, low_table, far_ref)
    back_for(1, eighth_ref, plain, bent, high_table, low_table, next_ref)
    back_for(3, eighth_ref, plain, bent, high_table, low_table, last_ref)


def back_rest_kernel(eighth_ref, plain_ref, bent_ref, high_table, low_table, own_ref):
    back_for(0, eighth_ref, plain_ref[...], bent_ref[...], high_table, low_table, own_ref)


def back(pieces, tables):
    turns = np.arange(8) * (2 * np.pi / 8)
    eighth = np.concatenate([np.cos(turns), np.sin(turns)]).astype(np.float32)
    piece = jax.ShapeDtypeStruct((128, 256), f32)
    held = jax.ShapeDtypeStruct((128, 512), f32)
    two, one, three, plain, bent = pl.pallas_call(
        back_kernel,
        out_shape=(piece, piece, piece, held, held),
        in_specs=[SM, VM, VM, VM],
        out_specs=(VM,) * 5,
        compiler_params=limit(24),
        name="back",
    )(eighth, pieces, *tables)
    own = pl.pallas_call(
        back_rest_kernel,
        out_shape=piece,
        in_specs=[SM] + [VM] * 4,
        out_specs=VM,
        compiler_params=limit(24),
        name="back_rest",
    )(eighth, plain, bent, *tables)
    return own, one, two, three


def final_kernel(a_ref, b_ref, c_ref, d_ref, x_ref, y_ref):
    total = (a_ref[...] + b_ref[...]) + (c_ref[...] + d_ref[...])
    x_ref[...] = total[:ROWS]
    y_ref[...] = total[ROWS:]


def final(pieces):
    shape = jax.ShapeDtypeStruct((ROWS, 256), f32)
    return pl.pallas_call(
        final_kernel,
        out_shape=(shape, shape),
        in_specs=[VM] * 4,
        out_specs=(VM, VM),
        compiler_params=limit(24),
        name="final",
    )(*pieces)


def deliver(pieces):
    return [pieces[0]] + [
        lax.ppermute(pieces[a], "x", [(i, (i + a) % 4) for i in range(4)]) for a in (2, 1, 3)
    ]


def body(density, refine, weight_low, weight_high):
    def swap(array, axes, pairs):
        return lax.ppermute(array, axes, pairs + [(b, a) for a, b in pairs])

    odd = lax.axis_index("x") % 2 == 1
    cross = lax.dynamic_slice_in_dim(density, jnp.where(odd, LAYERS - 1, 0), 1, 0)
    cross = swap(cross, LOS, [(3, 4)])
    row, other_row, layer, other_layer = edge_rows(density)
    layer = swap(layer, LOS, [(1, 2), (5, 6)])
    other_layer = swap(other_layer, LOS, [(0, 1), (2, 3), (4, 5), (6, 7)])
    row = swap(row, "sky", [(i, i + 1) for i in range(0, SKY, 2)])
    other_row = swap(other_row, "sky", [(i, (i + 1) % SKY) for i in range(1, SKY, 2)])
    inner = inner_sums(weight_low, weight_high, density, refine)
    tables = halves(forward_table())
    summed = outer_sums(
        weight_low, weight_high, density, (cross, layer, other_layer), (row, other_row), inner, tables
    )
    summed = deliver(summed)
    pieces = lax.all_to_all(turn(summed), ("zhi", "sky"), 0, 0, tiled=True)
    pieces = solve(pieces, twists() + halves(row_table()))
    pieces = lax.all_to_all(pieces, ("zhi", "sky"), 0, 0, tiled=True)
    fields = back(pieces, halves(inverse_table()))
    return final(deliver(fields))


def solution(mesh):
    devices = mesh.devices.reshape(2, 4, SKY)
    inner = Mesh(devices, ("zhi", "x", "sky"))
    placed = (P(LOS, "sky", None), P(LOS, "sky", None), P(LOS), P(LOS))
    return jax.shard_map(
        body,
        mesh=inner,
        in_specs=placed,
        out_specs=(P("sky", LOS), P("sky", LOS)),
        check_vma=False,
    )
```
